32 devices in a mesh: dp: 8 (over y, x, core), mp: 4 (over z).
Axes of the slice: x: 2, y: 2, z: 4, core: 2. Of those that a mesh axis runs over, the one named last changes fastest.
Arguments:
- tokens: bfloat16 [5120, 2048], P(('dp', 'mp')), may hold values from -6 to 6
- attn_gain: float32 [2048], replicated, may hold values from 0.5 to 1.5
- query_down: bfloat16 [2048, 1024], replicated, may hold values from -0.125 to 0.125
- query_up: bfloat16 [1024, 4096], P(None, 'mp'), may hold values from -0.375 to 0.375
- key_value: bfloat16 [2048, 512], replicated, may hold values from -0.125 to 0.125
- attn_out: bfloat16 [4096, 2048], P('mp'), may hold values from -0.375 to 0.375
- mlp_gain: float32 [2048], replicated, may hold values from 0.5 to 1.5
- gate_weight: bfloat16 [2048, 5632], P(None, 'mp'), may hold values from -0.125 to 0.125
- up_weight: bfloat16 [2048, 5632], P(None, 'mp'), may hold values from -0.125 to 0.125
- down_weight: bfloat16 [5632, 2048], P('mp'), may hold values from -0.078125 to 0.078125
- out_grad: bfloat16 [5120, 2048], P(('dp', 'mp')), may hold values from -6 to 6
Outputs:
- layer_out: bfloat16 [5120, 2048], P(('dp', 'mp'))
- tokens_grad: float32 [5120, 2048], P(('dp', 'mp'))
- attn_gain_grad: float32 [2048], P('mp')
- query_down_grad: float32 [2048, 1024], P('mp')
- query_up_grad: float32 [1024, 4096], P(None, 'mp')
- key_value_grad: float32 [2048, 512], P('mp')
- attn_out_grad: float32 [4096, 2048], P('mp')
- mlp_gain_grad: float32 [2048], P('mp')
- gate_grad: float32 [2048, 5632], P(None, 'mp')
- up_grad: float32 [2048, 5632], P(None, 'mp')
- down_grad: float32 [5632, 2048], P('mp')
The draws below stay inside these ranges and needn't reach their ends.
All inputs are finite; a program needn't handle non-finite values.
Results may differ from the reference program's by a relative error of at most 0.025.
Values may be sent and summed in bfloat16 or wider, within the bound.
No kernel may reach another device: no remote copies, remote signals or barrier semaphores. Data moves between devices by JAX's collectives and lax.ppermute only.
A program may use at most 192 MiB of HBM per device.

```python
import math
import jax
import jax.numpy as jnp
from jax import lax

D = 2048
HEADS = 16
HEAD_DIM = 256
QRANK = 1024
FF = 5632
SHORT_PART = 128
LONG_PART = 512
TOKENS = 5120
N_DP = 8


def block_levels(key, extent, pieces, smallest, high):
    level, own = 1.0, jax.random.fold_in(key, 6)
    for position, shards_of in pieces:
        heights = jnp.exp(jax.random.uniform(jax.random.fold_in(own, position), (shards_of,), jnp.float32, smallest / len(pieces), high / len(pieces)))
        level = level * jnp.repeat(heights, extent[position] // shards_of).reshape([-1 if axis == position else 1 for axis in range(len(extent))])
    return level


def centred(own_key, extent, spread, bound, cuts=(), kind=jnp.bfloat16):
    values = jax.random.normal(own_key, extent, jnp.float32) * spread
    if len(cuts) > 0:
        values = block_levels(own_key, extent, cuts, -0.22, 0.18) * values
    return jnp.clip(values, min=-bound, max=bound).astype(kind)


def setup_inputs(seed: int = 0) -> dict:
    arg_keys = jax.random.split(jax.random.key(seed), 12)
    return {
        "tokens": centred(arg_keys[0], (TOKENS, D), 1.0, 6.0, ((0, 32),)),
        "attn_gain": jnp.clip(1.0 + 0.1 * jax.random.normal(arg_keys[1], (D,), jnp.float32), 0.5, 1.5),
        "query_down": centred(arg_keys[2], (D, QRANK), D ** -0.5, 0.125),
        "query_up": centred(arg_keys[3], (QRANK, HEADS * HEAD_DIM), (QRANK // 4) ** -0.5, 0.375, ((1, 4),)),
        "key_value": centred(arg_keys[4], (D, 2 * HEAD_DIM), D ** -0.5, 0.125),
        "attn_out": centred(arg_keys[5], (HEADS * HEAD_DIM, D), (HEADS * HEAD_DIM // 16) ** -0.5, 0.375, ((0, 4),)),
        "mlp_gain": jnp.clip(1.0 + 0.1 * jax.random.normal(arg_keys[6], (D,), jnp.float32), 0.5, 1.5),
        "gate_weight": centred(arg_keys[7], (D, FF), D ** -0.5, 0.125, ((1, 4),)),
        "up_weight": centred(arg_keys[8], (D, FF), D ** -0.5, 0.125, ((1, 4),)),
        "down_weight": centred(arg_keys[9], (FF, D), FF ** -0.5, 0.078125, ((0, 4),)),
        "out_grad": centred(arg_keys[10], (TOKENS, D), 1.0, 6.0, ((0, 32),)),
    }


EPS = 1e-06

@jax.custom_vjp
def low(v):
    return lax.optimization_barrier(v.astype(jnp.bfloat16)).astype(jnp.float32)

@jax.custom_vjp
def low_back(v):
    return v

def low_keep(v):
    return (low(v), None)

def low_pass(kept, grad):
    return (grad,)

def back_keep(v):
    return (v, None)

def back_low(kept, grad):
    return (low(grad),)
low.defvjp(low_keep, low_pass)
low_back.defvjp(back_keep, back_low)

def matmul(left, right):
    return jnp.dot(left, right, preferred_element_type=jnp.float32, precision=lax.Precision.HIGHEST)

def normalize(rows, gain):
    return rows * lax.rsqrt(lax.optimization_barrier(jnp.mean(rows * rows, axis=-1, keepdims=True)) + EPS) * gain

def split_rows(array):
    rest = array.shape[1:]
    blocks = array.reshape((N_DP, SHORT_PART + LONG_PART) + rest)
    short_rows = blocks[:, :SHORT_PART].reshape((N_DP * SHORT_PART,) + rest)
    long_rows = blocks[:, SHORT_PART:].reshape((N_DP * LONG_PART,) + rest)
    return (short_rows, long_rows)

def join_rows(short_rows, long_rows):
    rest = short_rows.shape[1:]
    joined = jnp.concatenate([short_rows.reshape((N_DP, SHORT_PART) + rest), long_rows.reshape((N_DP, LONG_PART) + rest)], axis=1)
    return joined.reshape((N_DP * (SHORT_PART + LONG_PART),) + rest)

def attend(query, key_rows, value_rows):
    length = query.shape[0]
    width = query.shape[2]
    block_rows = math.gcd(512, length)
    query_blocks = query.reshape((length // block_rows, block_rows) + query.shape[1:])
    starts = jnp.arange(length // block_rows, dtype=jnp.int32) * block_rows
    key_pos = jnp.arange(length, dtype=jnp.int32)

    def one_block(packed):
        query_block, first_row = packed
        raw_scores = jnp.einsum('qhd,kd->qhk', query_block, key_rows, precision=lax.Precision.HIGHEST)
        scores = low_back(raw_scores) * width ** (-0.5)
        query_pos = first_row + jnp.arange(block_rows, dtype=jnp.int32)
        visible = key_pos[None, None, :] <= query_pos[:, None, None]
        scores = jnp.where(visible, scores, -jnp.inf)
        probability = low(jax.nn.softmax(scores, axis=-1))
        return jnp.einsum('qhk,kd->qhd', probability, value_rows, precision=lax.Precision.HIGHEST)
    result = lax.map(jax.checkpoint(one_block), (query_blocks, starts))
    return result.reshape(query.shape)

def layer(tokens, attn_gain, query_down, query_up, key_value, attn_out, mlp_gain, gate_weight, up_weight, down_weight):
    normal_one = low(normalize(tokens, attn_gain))
    latent = low_back(low(matmul(normal_one, query_down)))
    query = low_back(low(matmul(latent, query_up))).reshape(TOKENS, HEADS, HEAD_DIM)
    pair = low_back(low(matmul(normal_one, key_value)))
    short_query, long_query = split_rows(query)
    short_pair, long_pair = split_rows(pair)
    short_out = attend(short_query, short_pair[:, :HEAD_DIM], short_pair[:, HEAD_DIM:])
    long_out = attend(long_query, long_pair[:, :HEAD_DIM], long_pair[:, HEAD_DIM:])
    attended = low_back(low(join_rows(short_out, long_out).reshape(TOKENS, HEADS * HEAD_DIM)))
    hidden_res = tokens + low_back(matmul(attended, attn_out))
    normal_two = low(normalize(hidden_res, mlp_gain))
    gate = low_back(matmul(normal_two, gate_weight))
    upward = low_back(matmul(normal_two, up_weight))
    activated = low(jax.nn.silu(gate) * upward)
    return hidden_res + matmul(activated, down_weight)

def reference(tokens, attn_gain, query_down, query_up, key_value, attn_out, mlp_gain, gate_weight, up_weight, down_weight, out_grad):
    inputs = [item.astype(jnp.float32) for item in (tokens, attn_gain, query_down, query_up, key_value, attn_out, mlp_gain, gate_weight, up_weight, down_weight)]
    result, pullback = jax.vjp(layer, *inputs)
    grads = pullback(out_grad.astype(jnp.float32))
    return (result.astype(jnp.bfloat16), grads[0], grads[1], grads[2], grads[3], grads[4], grads[5], grads[6], grads[7], grads[8], grads[9])
```

```python
import functools

import jax
import jax.numpy as jnp
from jax import lax
from jax.experimental import pallas as pl
from jax.experimental.pallas import tpu as pltpu
from jax.sharding import PartitionSpec as P

HEAD_DIM = 256
EPS = 1e-06
SHORT_PART = 128
LONG_PART = 512
BLOCK = SHORT_PART + LONG_PART
LOG2E = 1.4426950408889634


def dotf(left, right):
    return jnp.dot(left, right, preferred_element_type=jnp.float32)


def chunks_of(heads):
    short = [(0, heads * SHORT_PART)]
    long = [(heads * SHORT_PART + h * LONG_PART, LONG_PART) for h in range(heads)]
    return ((0, SHORT_PART, short), (SHORT_PART, LONG_PART, long))


def spread(heads, head_dim, source, turned):
    for h in range(heads):
        cols = slice(h * head_dim, (h + 1) * head_dim)
        turned[:, h * SHORT_PART : (h + 1) * SHORT_PART] = source[:SHORT_PART, cols].T
        first = heads * SHORT_PART + h * LONG_PART
        turned[:, first : first + LONG_PART] = source[SHORT_PART:, cols].T


def visible_in(extent, width):
    key_pos = lax.broadcasted_iota(jnp.int32, (extent, width), 0)
    query_pos = lax.broadcasted_iota(jnp.int32, (extent, width), 1) & (extent - 1)
    return key_pos <= query_pos


def forward_kernel(heads, head_dim, group, query, pair, out, kept, logs, turned, maxima, totals):
    factor = head_dim ** (-0.5) * LOG2E
    spread(heads, head_dim, query, turned)
    kept[...] = jnp.zeros_like(kept)
    maxima[...] = jnp.full_like(maxima, -jnp.inf)
    totals[...] = jnp.zeros_like(totals)
    own = group[0]

    def one_block(index, masked):
        for offset, extent, chunks in chunks_of(heads):
            first = pl.multiple_of(index * BLOCK + offset, SHORT_PART)
            keys = pair[pl.ds(first, extent), :head_dim]
            values = pair[pl.ds(first, extent), head_dim:].T
            for column, width in chunks:
                at = slice(column, column + width)
                scores = dotf(keys, turned[:, at]) * factor
                if masked:
                    scores = jnp.where(visible_in(extent, width), scores, -jnp.inf)
                old = maxima[:, at]
                new = jnp.maximum(old, jnp.max(scores, axis=0, keepdims=True))
                rescale = jnp.exp2(old - new)
                weights = jnp.exp2(scores - new)
                maxima[:, at] = new
                totals[:, at] = totals[:, at] * rescale + jnp.sum(weights, axis=0, keepdims=True)
                kept[:, at] = kept[:, at] * rescale + dotf(values, weights.astype(jnp.bfloat16))

    def step(index, carry):
        one_block(index, False)
        return carry

    lax.fori_loop(0, own, step, 0)
    one_block(own, True)
    logs[...] = maxima[...] + jnp.log2(totals[...])
    for h in range(heads):
        cols = slice(h * head_dim, (h + 1) * head_dim)
        for rows, first, width in (
            (slice(0, SHORT_PART), h * SHORT_PART, SHORT_PART),
            (slice(SHORT_PART, BLOCK), heads * SHORT_PART + h * LONG_PART, LONG_PART),
        ):
            at = slice(first, first + width)
            exact = kept[:, at] * (1.0 / totals[:, at])
            kept[:, at] = exact
            out[rows, cols] = exact.T.astype(jnp.bfloat16)


def backward_kernel(
    heads, head_dim, group, query, grad, pair, kept, logs,
    query_grad, pair_grad, turned, grad_turned, total, delta, short_query, short_grad,
):
    scale = head_dim ** (-0.5)
    factor = scale * LOG2E
    spread(heads, head_dim, query, turned)
    spread(heads, head_dim, grad, grad_turned)
    for h in range(heads):
        cols = slice(h * head_dim, (h + 1) * head_dim)
        rows = slice(h * SHORT_PART, (h + 1) * SHORT_PART)
        short_query[rows, :] = query[:SHORT_PART, cols]
        short_grad[rows, :] = grad[:SHORT_PART, cols]
    delta[...] = jnp.sum(grad_turned[...].astype(jnp.float32) * kept[...], axis=0, keepdims=True)
    total[...] = jnp.zeros_like(total)
    own = group[0]

    def one_block(index, masked):
        for offset, extent, chunks in chunks_of(heads):
            first = pl.multiple_of(index * BLOCK + offset, SHORT_PART)
            keys = pair[pl.ds(first, extent), :head_dim]
            values = pair[pl.ds(first, extent), head_dim:]
            keys_turned = keys.T
            key_sum = None
            value_sum = None
            for h, (column, width) in enumerate(chunks):
                at = slice(column, column + width)
                if offset == 0:
                    rows_query, rows_grad = short_query[...], short_grad[...]
                else:
                    cols = slice(h * head_dim, (h + 1) * head_dim)
                    rows_query, rows_grad = query[SHORT_PART:, cols], grad[SHORT_PART:, cols]
                scores = dotf(keys, turned[:, at]) * factor
                chance = jnp.exp2(scores - logs[:, at])
                if masked:
                    chance = jnp.where(visible_in(extent, width), chance, 0.0)
                chance_grad = dotf(values, grad_turned[:, at])
                score_low = (chance * (chance_grad - delta[:, at])).astype(jnp.bfloat16)
                key_part = dotf(score_low, rows_query)
                value_part = dotf(chance.astype(jnp.bfloat16), rows_grad)
                key_sum = key_part if key_sum is None else key_sum + key_part
                value_sum = value_part if value_sum is None else value_sum + value_part
                total[:, at] += dotf(keys_turned, score_low)
            pair_grad[pl.ds(first, extent), :head_dim] = (key_sum * scale).astype(jnp.bfloat16)
            pair_grad[pl.ds(first, extent), head_dim:] = value_sum.astype(jnp.bfloat16)

    def step(index, carry):
        one_block(index, False)
        return carry

    def clear(index, carry):
        first = pl.multiple_of(index * BLOCK, SHORT_PART)
        pair_grad[pl.ds(first, BLOCK), :] = jnp.zeros((BLOCK, 2 * head_dim), jnp.bfloat16)
        return carry

    lax.fori_loop(0, own, step, 0)
    one_block(own, True)
    lax.fori_loop(own + 1, pair.shape[0] // BLOCK, clear, 0)
    for h in range(heads):
        cols = slice(h * head_dim, (h + 1) * head_dim)
        for rows, first, width in (
            (slice(0, SHORT_PART), h * SHORT_PART, SHORT_PART),
            (slice(SHORT_PART, BLOCK), heads * SHORT_PART + h * LONG_PART, LONG_PART),
        ):
            query_grad[rows, cols] = (total[:, first : first + width] * scale).T.astype(jnp.bfloat16)


def whole(count):
    return [pl.BlockSpec(memory_space=pltpu.VMEM)] * count


def attention_forward(group, query, pair, heads, head_dim):
    columns = heads * BLOCK
    return pl.pallas_call(
        functools.partial(forward_kernel, heads, head_dim),
        out_shape=(
            jax.ShapeDtypeStruct(query.shape, jnp.bfloat16),
            jax.ShapeDtypeStruct((head_dim, columns), jnp.float32),
            jax.ShapeDtypeStruct((1, columns), jnp.float32),
        ),
        in_specs=[pl.BlockSpec(memory_space=pltpu.SMEM)] + whole(2),
        out_specs=tuple(whole(3)),
        scratch_shapes=[
            pltpu.VMEM((head_dim, columns), jnp.bfloat16),
            pltpu.VMEM((1, columns), jnp.float32),
            pltpu.VMEM((1, columns), jnp.float32),
        ],
        compiler_params=pltpu.CompilerParams(vmem_limit_bytes=50 << 20),
        cost_estimate=pl.CostEstimate(
            flops=2 * columns * pair.shape[0] * head_dim * 2,
            bytes_accessed=2 * (pair.size + 2 * query.size) + 4 * query.size,
            transcendentals=columns * pair.shape[0] // 2,
        ),
        name="attention_forward",
    )(group, query, pair)


def attention_backward(group, query, grad, pair, kept, logs, heads, head_dim):
    columns = heads * BLOCK
    return pl.pallas_call(
        functools.partial(backward_kernel, heads, head_dim),
        out_shape=(
            jax.ShapeDtypeStruct(query.shape, jnp.bfloat16),
            jax.ShapeDtypeStruct(pair.shape, jnp.bfloat16),
        ),
        in_specs=[pl.BlockSpec(memory_space=pltpu.SMEM)] + whole(5),
        out_specs=tuple(whole(2)),
        scratch_shapes=[
            pltpu.VMEM((head_dim, columns), jnp.bfloat16),
            pltpu.VMEM((head_dim, columns), jnp.bfloat16),
            pltpu.VMEM((head_dim, columns), jnp.float32),
            pltpu.VMEM((1, columns), jnp.float32),
            pltpu.VMEM((heads * SHORT_PART, head_dim), jnp.bfloat16),
            pltpu.VMEM((heads * SHORT_PART, head_dim), jnp.bfloat16),
        ],
        compiler_params=pltpu.CompilerParams(vmem_limit_bytes=56 << 20),
        cost_estimate=pl.CostEstimate(
            flops=2 * columns * pair.shape[0] * head_dim * 5,
            bytes_accessed=2 * (2 * pair.size + 3 * query.size) + 4 * query.size,
            transcendentals=columns * pair.shape[0] // 2,
        ),
        name="attention_backward",
    )(group, query, grad, pair, kept, logs)


def normalize(rows, gain):
    return rows * lax.rsqrt(jnp.mean(rows * rows, axis=-1, keepdims=True) + EPS) * gain


def gated(gate_in, up_in):
    return jax.nn.silu(gate_in) * up_in


def bits_of(count):
    return max(count.bit_length() - 1, 0)


def trade(array, bit):
    count = lax.axis_size("dp")
    return lax.ppermute(array, "dp", [(i, i ^ (1 << bit)) for i in range(count)])


def orders():
    rest = list(range(1, bits_of(lax.axis_size("dp"))))
    return [0] + rest, [0] + rest[::-1]


def halve(array, bit, axis):
    half = array.shape[axis] // 2
    mine = (lax.axis_index("dp") >> bit) & 1
    send = lax.dynamic_slice_in_dim(array, (1 - mine) * half, half, axis)
    keep = lax.dynamic_slice_in_dim(array, mine * half, half, axis)
    return keep, trade(send, bit)


def scatter_sum(array, order, axis):
    for bit in order:
        keep, other = halve(array, bit, axis)
        array = (keep.astype(jnp.float32) + other.astype(jnp.float32)).astype(jnp.bfloat16)
    return array


def gather_pieces(piece, order, axis):
    for bit in order[:0:-1]:
        piece = jnp.concatenate([piece, trade(piece, bit)], axis=axis)
    return piece, trade(piece, 0)


def places(order):
    me = lax.axis_index("dp")
    own = jnp.int32(0)
    for bit in order[1:]:
        own = own * 2 + ((me >> bit) & 1)
    count = 1 << (len(order) - 1)
    relative = jnp.arange(count, dtype=jnp.int32) ^ own
    core = me & 1
    return jnp.concatenate([core * count + relative, (1 - core) * count + relative])


def lay_kernel(arrays, pieces, row_of, column_of, *refs):
    out = refs[arrays]
    step = pl.program_id(0)
    for a in range(arrays):

        @pl.when((step >= a * pieces) & (step < (a + 1) * pieces))
        def _(source=refs[a]):
            out[...] = source[...].astype(jnp.float32)


def lay_out(sets, rows_of, columns_of, axis, shape, name):
    pieces = lax.axis_size("dp") // 2
    block = list(sets[0].shape)
    block[axis] //= pieces

    def source_map(a):
        def at(step, rows, columns):
            piece = jnp.clip(step - a * pieces, 0, pieces - 1)
            return (piece, 0) if axis == 0 else (0, piece)

        return at

    return pl.pallas_call(
        functools.partial(lay_kernel, len(sets), pieces),
        grid_spec=pltpu.PrefetchScalarGridSpec(
            num_scalar_prefetch=2,
            grid=(len(sets) * pieces,),
            in_specs=[pl.BlockSpec(tuple(block), source_map(a)) for a in range(len(sets))],
            out_specs=pl.BlockSpec(
                tuple(block), lambda step, rows, columns: (rows[step], columns[step])
            ),
        ),
        out_shape=jax.ShapeDtypeStruct(shape, jnp.float32),
        compiler_params=pltpu.CompilerParams(vmem_limit_bytes=40 << 20),
        cost_estimate=pl.CostEstimate(
            flops=0, bytes_accessed=6 * shape[0] * shape[1], transcendentals=0
        ),
        name=name,
    )(rows_of, columns_of, *sets)


def sum_both(low, high, axis):
    first, second = orders()
    low = gather_pieces(scatter_sum(low, first, axis), first, axis)
    high = gather_pieces(scatter_sum(high, second, axis), second, axis)
    return (low, places(first)), (high, places(second))


def sum_over_blocks(partial, axis, name):
    half = partial.shape[1 - axis] // 2
    low = lax.slice_in_dim(partial, 0, half, axis=1 - axis)
    high = lax.slice_in_dim(partial, half, 2 * half, axis=1 - axis)
    (low, low_places), (high, high_places) = sum_both(low, high, axis)
    along = jnp.concatenate([low_places, high_places])
    across = (jnp.arange(along.shape[0], dtype=jnp.int32) >= low_places.shape[0]).astype(jnp.int32)
    rows_of, columns_of = (along, across) if axis == 0 else (across, along)
    return lay_out(low + high, rows_of, columns_of, axis, partial.shape, name)


def sum_two_over_blocks(one, two, names):
    outs = []
    for (sets, along), name in zip(sum_both(one, two, 0), names):
        outs.append(lay_out(sets, along, jnp.zeros_like(along), 0, one.shape, name))
    return outs


def sum_small(array):
    for axis in ("mp", "dp"):
        count = lax.axis_size(axis)
        for bit in range(bits_of(count)):
            pairs = [(i, i ^ (1 << bit)) for i in range(count)]
            array = array + lax.ppermute(array, axis, pairs)
    return array


def sum_pairs(pair_grads):
    count = lax.axis_size("dp")
    first, second = orders()
    blocks = pair_grads.reshape(count, -1, pair_grads.shape[1])
    half = blocks.shape[1] // 2

    def halved(array, order):
        pending = list(range(bits_of(count)))
        for bit in order:
            rest = array.shape[1:]
            place = len(pending) - 1 - pending.index(bit)
            pending.remove(bit)
            view = array.reshape((1 << place, 2, -1) + rest)
            mine = (lax.axis_index("dp") >> bit) & 1
            keep = lax.dynamic_slice_in_dim(view, mine, 1, 1).reshape((-1,) + rest)
            send = lax.dynamic_slice_in_dim(view, 1 - mine, 1, 1).reshape((-1,) + rest)
            other = trade(send, bit)
            array = (keep.astype(jnp.float32) + other.astype(jnp.float32)).astype(jnp.bfloat16)
        return array[0]

    low = halved(blocks[:, :half], first)
    high = halved(blocks[:, half:], second)
    return jnp.concatenate([low, high], axis=0)


def shards(
    tokens,
    attn_gain,
    query_down,
    query_up,
    key_value,
    attn_out,
    mlp_gain,
    gate_weight,
    up_weight,
    down_weight,
    out_grad,
):
    head_dim = HEAD_DIM
    local_heads = query_up.shape[1] // head_dim
    ranks = lax.axis_size("mp")
    rank = lax.axis_index("mp")
    group = lax.axis_index("dp").reshape(1)
    share = query_down.shape[0] // ranks

    def gather(rows):
        return lax.all_gather(rows, "mp", axis=0, tiled=True)

    def scatter(rows):
        return lax.psum_scatter(rows, "mp", scatter_dimension=0, tiled=True)

    inputs = tokens.astype(jnp.float32)
    normal_one = normalize(inputs, attn_gain).astype(jnp.bfloat16)
    latent = dotf(normal_one, query_down).astype(jnp.bfloat16)
    pair_local = dotf(normal_one, key_value).astype(jnp.bfloat16)
    latent_full = gather(latent)
    pair_all = lax.all_gather(pair_local, ("dp", "mp"), axis=0, tiled=True)
    grad_full = gather(out_grad)
    normal_share = lax.all_to_all(normal_one, "mp", split_axis=1, concat_axis=0, tiled=True)
    query_full = dotf(latent_full, query_up).astype(jnp.bfloat16)
    attended, kept, logs = attention_forward(group, query_full, pair_all, local_heads, head_dim)
    attended, grad_full, normal_share = lax.optimization_barrier(
        (attended, grad_full, normal_share)
    )
    hidden_res = inputs + scatter(dotf(attended, attn_out).astype(jnp.bfloat16)).astype(jnp.float32)
    normal_two = normalize(hidden_res, mlp_gain).astype(jnp.bfloat16)
    normal_full = gather(normal_two)
    gate = dotf(normal_full, gate_weight)
    upward = dotf(normal_full, up_weight)
    activated = gated(gate, upward).astype(jnp.bfloat16)
    act_grad = jnp.einsum("td,fd->tf", grad_full, down_weight, preferred_element_type=jnp.float32)
    _, gated_pull = jax.vjp(gated, gate, upward)
    gate_grad32, up_grad32 = gated_pull(act_grad)
    gate_low = gate_grad32.astype(jnp.bfloat16)
    up_low = up_grad32.astype(jnp.bfloat16)
    normal_two_grad = scatter(
        (
            jnp.einsum("tf,df->td", gate_low, gate_weight, preferred_element_type=jnp.float32)
            + jnp.einsum("tf,df->td", up_low, up_weight, preferred_element_type=jnp.float32)
        ).astype(jnp.bfloat16)
    ).astype(jnp.float32)

    def weight_grad(left, right):
        return jnp.einsum("tk,td->kd", left, right, preferred_element_type=jnp.float32).astype(
            jnp.bfloat16
        )

    down_sum = sum_over_blocks(weight_grad(activated, grad_full), 1, "down_grad")
    gate_sum, up_sum = sum_two_over_blocks(
        weight_grad(normal_full, gate_low),
        weight_grad(normal_full, up_low),
        ("gate_grad", "up_grad"),
    )
    result = hidden_res + scatter(dotf(activated, down_weight).astype(jnp.bfloat16)).astype(
        jnp.float32
    )
    _, norm_pull_two = jax.vjp(normalize, hidden_res, mlp_gain)
    resid_from_norm, mlp_gain_part = norm_pull_two(normal_two_grad)
    hidden_grad = out_grad.astype(jnp.float32) + resid_from_norm
    branch_full = gather(hidden_grad.astype(jnp.bfloat16))
    attended_low = jnp.einsum(
        "td,kd->tk", branch_full, attn_out, preferred_element_type=jnp.float32
    ).astype(jnp.bfloat16)
    out_sum = sum_over_blocks(weight_grad(attended, branch_full), 0, "attn_out_grad")
    query_low, pair_grads = attention_backward(
        group, query_full, attended_low, pair_all, kept, logs, local_heads, head_dim
    )
    latent_low = scatter(
        jnp.einsum("tk,rk->tr", query_low, query_up, preferred_element_type=jnp.float32).astype(
            jnp.bfloat16
        )
    )
    pair_low = scatter(sum_pairs(pair_grads))
    up_query_sum = sum_over_blocks(weight_grad(latent_full, query_low), 0, "query_up_grad")
    low_full = gather(latent_low)
    pair_full = gather(pair_low)
    down_query_sum = sum_over_blocks(weight_grad(normal_share, low_full), 0, "query_down_grad")
    pair_weight_sum = sum_over_blocks(weight_grad(normal_share, pair_full), 0, "key_value_grad")
    normal_one_grad = jnp.einsum(
        "tr,dr->td", latent_low, query_down, preferred_element_type=jnp.float32
    ) + jnp.einsum("tp,dp->td", pair_low, key_value, preferred_element_type=jnp.float32)
    _, norm_pull_one = jax.vjp(normalize, inputs, attn_gain)
    input_from_norm, attn_gain_part = norm_pull_one(normal_one_grad)
    input_grad = hidden_grad + input_from_norm
    attn_gain_sum = lax.dynamic_slice_in_dim(sum_small(attn_gain_part), rank * share, share)
    mlp_gain_sum = lax.dynamic_slice_in_dim(sum_small(mlp_gain_part), rank * share, share)
    return (
        result.astype(jnp.bfloat16),
        input_grad,
        attn_gain_sum,
        down_query_sum,
        up_query_sum,
        pair_weight_sum,
        out_sum,
        mlp_gain_sum,
        gate_sum,
        up_sum,
        down_sum,
    )


def solution(mesh):
    return jax.shard_map(
        shards,
        mesh=mesh,
        in_specs=(
            P(("dp", "mp"), None),
            P(),
            P(),
            P(None, "mp"),
            P(),
            P("mp", None),
            P(),
            P(None, "mp"),
            P(None, "mp"),
            P("mp", None),
            P(("dp", "mp"), None),
        ),
        out_specs=(
            P(("dp", "mp"), None),
            P(("dp", "mp"), None),
            P("mp"),
            P("mp", None),
            P(None, "mp"),
            P("mp", None),
            P("mp", None),
            P("mp"),
            P(None, "mp"),
            P(None, "mp"),
            P("mp", None),
        ),
        check_vma=False,
    )
```

```python
import functools

import jax
import jax.numpy as jnp
from jax import lax
from jax.experimental import pallas as pl
from jax.experimental.pallas import tpu as pltpu
from jax.sharding import PartitionSpec as P

HEAD_DIM = 256
EPS = 1e-06
SHORT_PART = 128
LONG_PART = 512
BLOCK = SHORT_PART + LONG_PART
LOG2E = 1.4426950408889634


def dotf(left, right):
    return jnp.dot(left, right, preferred_element_type=jnp.float32)


def turned_bits(value, count):
    return sum(((value >> b) & 1) << (count - 1 - b) for b in range(count))


def bits_of(count):
    return max(count.bit_length() - 1, 0)


def chunks_of(heads):
    short = [(0, heads * SHORT_PART)]
    long = [(heads * SHORT_PART + h * LONG_PART, LONG_PART) for h in range(heads)]
    return ((0, SHORT_PART, short), (SHORT_PART, LONG_PART, long))


def spread(heads, head_dim, source, turned):
    for h in range(heads):
        cols = slice(h * head_dim, (h + 1) * head_dim)
        turned[:, h * SHORT_PART : (h + 1) * SHORT_PART] = source[:SHORT_PART, cols].T
        first = heads * SHORT_PART + h * LONG_PART
        turned[:, first : first + LONG_PART] = source[SHORT_PART:, cols].T


def visible_in(extent, width):
    key_pos = lax.broadcasted_iota(jnp.int32, (extent, width), 0)
    query_pos = lax.broadcasted_iota(jnp.int32, (extent, width), 1) & (extent - 1)
    return key_pos <= query_pos


def block_copies(own, sources, all_keys, all_values, sems):
    copies = []
    for kind, (parts, target) in enumerate(((sources[:4], all_keys), (sources[4:], all_values))):
        held = parts[0].shape[0] // BLOCK
        bits = bits_of(2 * held)
        for place, part in enumerate(parts):
            for i in range(held):
                relative = place % 2 * held + i
                if kind == 1:
                    relative = turned_bits(relative, bits)
                index = own ^ (2 * relative + place // 2)
                first = pl.multiple_of(index * BLOCK, BLOCK)
                copies.append(
                    pltpu.make_async_copy(
                        part.at[pl.ds(i * BLOCK, BLOCK), :],
                        target.at[pl.ds(first, BLOCK), :],
                        sems.at[len(copies)],
                    )
                )
    return copies


def forward_kernel(
    heads, head_dim, group, query, *refs
):
    sources, (out, kept, logs, turned, maxima, totals, all_keys, all_values, sems) = (
        refs[:8],
        refs[8:],
    )
    factor = head_dim ** (-0.5) * LOG2E
    own = group[0]
    copies = block_copies(own, sources, all_keys, all_values, sems)
    for copy in copies:
        copy.start()
    spread(heads, head_dim, query, turned)
    kept[...] = jnp.zeros_like(kept)
    maxima[...] = jnp.full_like(maxima, -jnp.inf)
    totals[...] = jnp.zeros_like(totals)
    for copy in copies:
        copy.wait()

    def one_block(index, masked):
        for offset, extent, chunks in chunks_of(heads):
            first = pl.multiple_of(index * BLOCK + offset, SHORT_PART)
            keys = all_keys[pl.ds(first, extent), :]
            values = all_values[pl.ds(first, extent), :].T
            for column, width in chunks:
                at = slice(column, column + width)
                scores = dotf(keys, turned[:, at]) * factor
                if masked:
                    scores = jnp.where(visible_in(extent, width), scores, -jnp.inf)
                old = maxima[:, at]
                new = jnp.maximum(old, jnp.max(scores, axis=0, keepdims=True))
                rescale = jnp.exp2(old - new)
                weights = jnp.exp2(scores - new)
                maxima[:, at] = new
                totals[:, at] = totals[:, at] * rescale + jnp.sum(weights, axis=0, keepdims=True)
                kept[:, at] = kept[:, at] * rescale + dotf(values, weights.astype(jnp.bfloat16))

    def step(index, carry):
        one_block(index, False)
        return carry

    lax.fori_loop(0, own, step, 0)
    one_block(own, True)
    logs[...] = maxima[...] + jnp.log2(totals[...])
    for h in range(heads):
        cols = slice(h * head_dim, (h + 1) * head_dim)
        for rows, first, width in (
            (slice(0, SHORT_PART), h * SHORT_PART, SHORT_PART),
            (slice(SHORT_PART, BLOCK), heads * SHORT_PART + h * LONG_PART, LONG_PART),
        ):
            at = slice(first, first + width)
            exact = kept[:, at] * (1.0 / totals[:, at])
            kept[:, at] = exact
            out[rows, cols] = exact.T.astype(jnp.bfloat16)


def backward_kernel(heads, head_dim, group, query, grad, kept, logs, *refs):
    sources = refs[:8]
    query_grad, key_grad, value_grad = refs[8:11]
    turned, grad_turned, total, delta, short_query, short_grad = refs[11:17]
    all_keys, all_values, sems = refs[17:]
    scale = head_dim ** (-0.5)
    factor = scale * LOG2E
    own = group[0]
    count = all_keys.shape[0] // BLOCK
    bits = bits_of(count) - 1
    copies = block_copies(own, sources, all_keys, all_values, sems)
    for copy in copies:
        copy.start()
    spread(heads, head_dim, query, turned)
    spread(heads, head_dim, grad, grad_turned)
    for h in range(heads):
        cols = slice(h * head_dim, (h + 1) * head_dim)
        rows = slice(h * SHORT_PART, (h + 1) * SHORT_PART)
        short_query[rows, :] = query[:SHORT_PART, cols]
        short_grad[rows, :] = grad[:SHORT_PART, cols]
    delta[...] = jnp.sum(grad_turned[...].astype(jnp.float32) * kept[...], axis=0, keepdims=True)
    total[...] = jnp.zeros_like(total)
    for copy in copies:
        copy.wait()

    def places(index):
        relative = index ^ own
        core, rest = relative & 1, relative >> 1
        key_place = core * (count // 2) + turned_bits(rest, bits)
        return key_place * BLOCK, (core * (count // 2) + rest) * BLOCK

    def one_block(index, masked):
        key_first, value_first = places(index)
        for offset, extent, chunks in chunks_of(heads):
            first = pl.multiple_of(index * BLOCK + offset, SHORT_PART)
            keys = all_keys[pl.ds(first, extent), :]
            values = all_values[pl.ds(first, extent), :]
            keys_turned = keys.T
            key_sum = None
            value_sum = None
            for h, (column, width) in enumerate(chunks):
                at = slice(column, column + width)
                if offset == 0:
                    rows_query, rows_grad = short_query[...], short_grad[...]
                else:
                    cols = slice(h * head_dim, (h + 1) * head_dim)
                    rows_query, rows_grad = query[SHORT_PART:, cols], grad[SHORT_PART:, cols]
                scores = dotf(keys, turned[:, at]) * factor
                chance = jnp.exp2(scores - logs[:, at])
                if masked:
                    chance = jnp.where(visible_in(extent, width), chance, 0.0)
                chance_grad = dotf(values, grad_turned[:, at])
                score_low = (chance * (chance_grad - delta[:, at])).astype(jnp.bfloat16)
                key_part = dotf(score_low, rows_query)
                value_part = dotf(chance.astype(jnp.bfloat16), rows_grad)
                key_sum = key_part if key_sum is None else key_sum + key_part
                value_sum = value_part if value_sum is None else value_sum + value_part
                total[:, at] += dotf(keys_turned, score_low)
            key_rows = pl.ds(pl.multiple_of(key_first + offset, SHORT_PART), extent)
            value_rows = pl.ds(pl.multiple_of(value_first + offset, SHORT_PART), extent)
            key_grad[key_rows, :] = (key_sum * scale).astype(jnp.bfloat16)
            value_grad[value_rows, :] = value_sum.astype(jnp.bfloat16)

    def step(index, carry):
        one_block(index, False)
        return carry

    def clear(index, carry):
        nothing = jnp.zeros((BLOCK, head_dim), jnp.bfloat16)
        key_first, value_first = places(index)
        key_grad[pl.ds(pl.multiple_of(key_first, SHORT_PART), BLOCK), :] = nothing
        value_grad[pl.ds(pl.multiple_of(value_first, SHORT_PART), BLOCK), :] = nothing
        return carry

    lax.fori_loop(0, own, step, 0)
    one_block(own, True)
    lax.fori_loop(own + 1, count, clear, 0)
    for h in range(heads):
        cols = slice(h * head_dim, (h + 1) * head_dim)
        for rows, first, width in (
            (slice(0, SHORT_PART), h * SHORT_PART, SHORT_PART),
            (slice(SHORT_PART, BLOCK), heads * SHORT_PART + h * LONG_PART, LONG_PART),
        ):
            query_grad[rows, cols] = (total[:, first : first + width] * scale).T.astype(jnp.bfloat16)


def in_vmem(count):
    return [pl.BlockSpec(memory_space=pltpu.VMEM)] * count


def gathered_scratch(sources, head_dim):
    rows = sum(part.shape[0] for part in sources[:4])
    return [
        pltpu.VMEM((rows, head_dim), jnp.bfloat16),
        pltpu.VMEM((rows, head_dim), jnp.bfloat16),
        pltpu.SemaphoreType.DMA((2 * rows // BLOCK,)),
    ], rows


def attention_forward(group, query, sources, heads, head_dim):
    columns = heads * BLOCK
    scratch, rows = gathered_scratch(sources, head_dim)
    return pl.pallas_call(
        functools.partial(forward_kernel, heads, head_dim),
        out_shape=(
            jax.ShapeDtypeStruct(query.shape, jnp.bfloat16),
            jax.ShapeDtypeStruct((head_dim, columns), jnp.float32),
            jax.ShapeDtypeStruct((1, columns), jnp.float32),
        ),
        in_specs=[pl.BlockSpec(memory_space=pltpu.SMEM)]
        + in_vmem(1)
        + [pl.BlockSpec(memory_space=pl.ANY)] * 8,
        out_specs=tuple(in_vmem(3)),
        scratch_shapes=[
            pltpu.VMEM((head_dim, columns), jnp.bfloat16),
            pltpu.VMEM((1, columns), jnp.float32),
            pltpu.VMEM((1, columns), jnp.float32),
        ]
        + scratch,
        compiler_params=pltpu.CompilerParams(vmem_limit_bytes=50 << 20),
        cost_estimate=pl.CostEstimate(
            flops=2 * columns * rows * head_dim * 2,
            bytes_accessed=4 * rows * head_dim + 8 * query.size,
            transcendentals=columns * rows // 2,
        ),
        name="attention_forward",
    )(group, query, *sources)


def attention_backward(group, query, grad, sources, kept, logs, heads, head_dim):
    columns = heads * BLOCK
    scratch, rows = gathered_scratch(sources, head_dim)
    return pl.pallas_call(
        functools.partial(backward_kernel, heads, head_dim),
        out_shape=(
            jax.ShapeDtypeStruct(query.shape, jnp.bfloat16),
            jax.ShapeDtypeStruct((rows, head_dim), jnp.bfloat16),
            jax.ShapeDtypeStruct((rows, head_dim), jnp.bfloat16),
        ),
        in_specs=[pl.BlockSpec(memory_space=pltpu.SMEM)]
        + in_vmem(4)
        + [pl.BlockSpec(memory_space=pl.ANY)] * 8,
        out_specs=tuple(in_vmem(3)),
        scratch_shapes=[
            pltpu.VMEM((head_dim, columns), jnp.bfloat16),
            pltpu.VMEM((head_dim, columns), jnp.bfloat16),
            pltpu.VMEM((head_dim, columns), jnp.float32),
            pltpu.VMEM((1, columns), jnp.float32),
            pltpu.VMEM((heads * SHORT_PART, head_dim), jnp.bfloat16),
            pltpu.VMEM((heads * SHORT_PART, head_dim), jnp.bfloat16),
        ]
        + scratch,
        compiler_params=pltpu.CompilerParams(vmem_limit_bytes=56 << 20),
        cost_estimate=pl.CostEstimate(
            flops=2 * columns * rows * head_dim * 5,
            bytes_accessed=8 * rows * head_dim + 10 * query.size,
            transcendentals=columns * rows // 2,
        ),
        name="attention_backward",
    )(group, query, grad, kept, logs, *sources)


def normalize(rows, gain):
    return rows * lax.rsqrt(jnp.mean(rows * rows, axis=-1, keepdims=True) + EPS) * gain


def gated(gate_in, up_in):
    return jax.nn.silu(gate_in) * up_in


class Order:
    def __init__(self):
        self.last = ()

    def take(self, *values):
        out = lax.optimization_barrier(values + self.last)[: len(values)]
        return out if len(values) > 1 else out[0]

    def mark(self, *values):
        self.last = tuple(jax.tree.leaves(values))


def add_low(left, right):
    return (left.astype(jnp.float32) + right.astype(jnp.float32)).astype(jnp.bfloat16)


def ring_of(count):
    return [0] + list(range(1, count, 2)) + list(range(2, count, 2))[::-1]


def ring_place(back):
    ring = ring_of(lax.axis_size("mp"))
    count = len(ring)
    table = [ring[(ring.index(i) - back) % count] for i in range(count)]
    return jnp.asarray(table, jnp.int32)[lax.axis_index("mp")]


def ring_pass(array):
    ring = ring_of(lax.axis_size("mp"))
    pairs = [(ring[i], ring[(i + 1) % len(ring)]) for i in range(len(ring))]
    return lax.ppermute(array, "mp", pairs)


def put_rows(whole_rows, rows, place):
    return lax.dynamic_update_slice_in_dim(whole_rows, rows, place * rows.shape[0], 0)


def take_rows(whole_rows, place):
    count = whole_rows.shape[0] // lax.axis_size("mp")
    return lax.dynamic_slice_in_dim(whole_rows, place * count, count, 0)


def ring_rows(parts):
    out = jnp.zeros((parts[0].shape[0] * len(parts),) + parts[0].shape[1:], parts[0].dtype)
    for step, rows in enumerate(parts):
        out = put_rows(out, rows, ring_place(step))
    return out


class RingGather:
    def __init__(self, rows):
        self.parts = [rows]
        self.start()

    def start(self):
        if len(self.parts) < lax.axis_size("mp"):
            self.flying = ring_pass(self.parts[-1])

    def step(self, order):
        if len(self.parts) < lax.axis_size("mp"):
            rows = order.take(self.flying)
            order.mark(rows)
            self.parts.append(rows)
            self.start()

    def steps_left(self):
        return lax.axis_size("mp") - len(self.parts)

    def rows(self):
        return ring_rows(self.parts)


class RingScatter:
    def __init__(self, partial):
        self.partial, self.steps = partial, 1
        self.held = take_rows(partial, ring_place(1))
        self.flying = ring_pass(self.held)

    def step(self, order):
        if self.steps_left():
            got, partial = order.take(self.flying, self.partial)
            self.steps += 1
            self.held = add_low(take_rows(partial, ring_place(self.steps)), got)
            order.mark(self.held)
            if self.steps_left():
                self.flying = ring_pass(self.held)

    def steps_left(self):
        return lax.axis_size("mp") - self.steps


def trade(array, bit):
    count = lax.axis_size("dp")
    return lax.ppermute(array, "dp", [(i, i ^ (1 << bit)) for i in range(count)])


def bit_here(bit):
    return (lax.axis_index("dp") >> bit) & 1


def orders():
    rest = list(range(1, bits_of(lax.axis_size("dp"))))
    return [0] + rest, [0] + rest[::-1]


class Lane:
    def __init__(self, partial, order, axis):
        self.bits, self.axis = order, axis
        self.steps = [("halve", bit) for bit in order]
        self.steps += [("double", bit) for bit in order[:0:-1]] + [("core", 0)]
        self.cut_and_start(lambda which, half: self.cut(partial, which, half), partial.shape[axis])

    def cut(self, array, which, half):
        return lax.dynamic_slice_in_dim(array, which * half, half, self.axis)

    def cut_and_start(self, part, extent):
        bit = self.steps[0][1]
        mine = bit_here(bit)
        self.sent, self.held = part(1 - mine, extent // 2), part(mine, extent // 2)
        self.flying = trade(self.sent, bit)

    def step(self, order):
        kind, _ = self.steps.pop(0)
        got, held = order.take(self.flying, self.held)
        if not self.steps:
            self.pieces = [held, got]
            order.mark(self.pieces)
            return
        following, bit = self.steps[0]
        if kind == "halve" and following == "halve":
            self.cut_and_start(
                lambda which, half: add_low(self.cut(held, which, half), self.cut(got, which, half)),
                held.shape[self.axis],
            )
        else:
            if kind == "halve":
                self.held = add_low(held, got)
            else:
                self.held = jnp.concatenate([held, got], axis=self.axis)
            self.sent = self.held
            self.flying = trade(self.sent, bit)
        order.mark(self.sent, self.held)

    def places(self):
        own = jnp.int32(0)
        for bit in self.bits[1:]:
            own = own * 2 + bit_here(bit)
        count = 1 << (len(self.bits) - 1)
        relative = jnp.arange(count, dtype=jnp.int32) ^ own
        core = bit_here(0)
        return jnp.concatenate([core * count + relative, (1 - core) * count + relative])


def lay_kernel(sets, pieces, axis, split, places, *refs):
    sources, out = refs[:sets], refs[sets]
    landed, raised, in_sems, out_sems = refs[sets + 1 :]
    total, slots = sets * pieces, raised.shape[0]
    rows, columns = landed.shape[1:]

    def fetch(i):
        first = i % pieces * (rows, columns)[axis]
        source = sources[i // pieces]
        window = (
            source.at[pl.ds(first, rows), :] if axis == 0 else source.at[:, pl.ds(first, columns)]
        )
        return pltpu.make_async_copy(window, landed.at[i], in_sems.at[i])

    def store(i):
        along = places[i]
        across = i * split // total
        if axis == 0:
            window = out.at[
                pl.ds(pl.multiple_of(along * rows, rows), rows), pl.ds(across * columns, columns)
            ]
        else:
            window = out.at[
                pl.ds(across * rows, rows), pl.ds(pl.multiple_of(along * columns, 128), columns)
            ]
        return pltpu.make_async_copy(raised.at[i % slots], window, out_sems.at[i])

    for i in range(total):
        fetch(i).start()
    for i in range(total):
        fetch(i).wait()
        if i >= slots:
            store(i - slots).wait()
        raised[i % slots] = landed[i].astype(jnp.float32)
        store(i).start()
    for i in range(max(total - slots, 0), total):
        store(i).wait()


def lay_out(lanes, shape, name):
    sets = [piece for lane in lanes for piece in lane.pieces]
    axis = lanes[0].axis
    places = jnp.concatenate([lane.places() for lane in lanes])
    pieces = places.shape[0] // len(sets)
    block = list(sets[0].shape)
    block[axis] //= pieces
    total = len(sets) * pieces
    anywhere = pl.BlockSpec(memory_space=pl.ANY)
    return pl.pallas_call(
        functools.partial(lay_kernel, len(sets), pieces, axis, len(lanes)),
        in_specs=[pl.BlockSpec(memory_space=pltpu.SMEM)] + [anywhere] * len(sets),
        out_specs=anywhere,
        out_shape=jax.ShapeDtypeStruct(shape, jnp.float32),
        scratch_shapes=[
            pltpu.VMEM((total, *block), jnp.bfloat16),
            pltpu.VMEM((min(total, 6), *block), jnp.float32),
            pltpu.SemaphoreType.DMA((total,)),
            pltpu.SemaphoreType.DMA((total,)),
        ],
        compiler_params=pltpu.CompilerParams(vmem_limit_bytes=40 << 20),
        cost_estimate=pl.CostEstimate(
            flops=0, bytes_accessed=6 * shape[0] * shape[1], transcendentals=0
        ),
        name=name,
    )(places, *sets)


def sum_halves(partial, axis):
    first, second = orders()
    half = partial.shape[1 - axis] // 2
    low = lax.slice_in_dim(partial, 0, half, axis=1 - axis)
    high = lax.slice_in_dim(partial, half, 2 * half, axis=1 - axis)
    return [Lane(low, first, axis), Lane(high, second, axis)]


def sum_ranks(array):
    count = lax.axis_size("mp")
    for bit in range(bits_of(count)):
        array = array + lax.ppermute(array, "mp", [(i, i ^ (1 << bit)) for i in range(count)])
    return array


def own_share(array):
    share = array.shape[0] // lax.axis_size("mp")
    return lax.dynamic_slice_in_dim(array, lax.axis_index("mp") * share, share)


class BlockSum:
    def __init__(self, blocks, order):
        self.bits = list(order)
        half = blocks.shape[0] // 2
        self.held, self.sent = blocks[:half], blocks[half:]
        self.flying = trade(self.sent, self.bits[0])

    def step(self, order):
        self.bits.pop(0)
        got, held = order.take(self.flying, self.held)
        if self.bits:
            half = held.shape[0] // 2
            self.sent = add_low(held[half:], got[half:])
            self.held = add_low(held[:half], got[:half])
            self.flying = trade(self.sent, self.bits[0])
        else:
            self.held = self.sent = add_low(held, got)
        order.mark(self.sent, self.held)


class BlockGather:
    def __init__(self, rows, order):
        self.bits, self.held = list(order), rows
        self.flying = trade(rows, self.bits[0])

    def step(self, order):
        if not self.bits:
            got = order.take(*self.flying)
            order.mark(got)
            self.parts = self.held + list(got)
            return
        self.bits.pop(0)
        got, held = order.take(self.flying, self.held)
        if self.bits:
            self.held = jnp.concatenate([held, got], axis=0)
            self.flying = trade(self.held, self.bits[0])
        else:
            self.held = [held, got]
            self.flying = [trade(part, 0) for part in self.held]
        order.mark(self.held)


class SmallSum:
    def __init__(self, array, axis):
        self.axis, self.held = axis, array
        self.bits = list(range(bits_of(lax.axis_size(axis))))
        self.start()

    def start(self):
        if self.bits:
            count = lax.axis_size(self.axis)
            pairs = [(i, i ^ (1 << self.bits[0])) for i in range(count)]
            self.flying = lax.ppermute(self.held, self.axis, pairs)

    def step(self, order):
        if self.bits:
            self.bits.pop(0)
            got, held = order.take(self.flying, self.held)
            self.held = held + got
            order.mark(self.held)
            self.start()


def column_share(rows):
    ring = ring_of(lax.axis_size("mp"))
    count = len(ring)
    width = rows.shape[1] // count
    parts = []
    for step in range(count):
        part = lax.dynamic_slice_in_dim(rows, ring_place(-step) * width, width, 1)
        pairs = [(ring[i], ring[(i + step) % count]) for i in range(count)]
        parts.append(lax.ppermute(part, "mp", pairs) if step else part)
    return parts


def shards(
    tokens,
    attn_gain,
    query_down,
    query_up,
    key_value,
    attn_out,
    mlp_gain,
    gate_weight,
    up_weight,
    down_weight,
    out_grad,
):
    head_dim = HEAD_DIM
    local_heads = query_up.shape[1] // head_dim
    ranks = lax.axis_size("mp")
    group = lax.axis_index("dp").reshape(1)
    first, second = orders()

    def gather(rows):
        return lax.all_gather(rows, "mp", axis=0, tiled=True)

    def scatter(rows):
        return lax.psum_scatter(rows, "mp", scatter_dimension=0, tiled=True)

    def weight_grad(left, right):
        return jnp.einsum("tk,td->kd", left, right, preferred_element_type=jnp.float32).astype(
            jnp.bfloat16
        )

    def steps(*moving):
        for one in moving:
            one.step(order)

    def finish(*lanes):
        while lanes[0].steps:
            steps(*lanes)

    order = Order()
    inputs = tokens.astype(jnp.float32)
    normal_one = normalize(inputs, attn_gain).astype(jnp.bfloat16)
    pair_local = dotf(normal_one, key_value).astype(jnp.bfloat16)
    order.mark(pair_local)
    pair_ring = RingGather(pair_local)
    latent = dotf(order.take(normal_one), query_down).astype(jnp.bfloat16)
    order.mark(latent)
    latent_ring = RingGather(latent)
    while pair_ring.steps_left() > 1:
        steps(pair_ring, latent_ring)
    steps(pair_ring)
    pair_own = pair_ring.rows()
    order.mark(pair_own)
    keys = BlockGather(pair_own[:, :head_dim], first[1:])
    values = BlockGather(pair_own[:, head_dim:], second[1:])
    while latent_ring.steps_left():
        steps(latent_ring)
    grad_ring = RingGather(order.take(out_grad))
    latent_full = order.take(latent_ring.rows())
    query_full = dotf(latent_full, query_up).astype(jnp.bfloat16)
    order.mark(query_full)
    steps(keys, values, grad_ring)
    while keys.bits:
        steps(keys, values)
    steps(grad_ring, keys, values)
    sources = order.take(*keys.parts, *values.parts)
    attended, kept, logs = attention_forward(group, query_full, sources, local_heads, head_dim)
    order.mark(attended)
    steps(grad_ring)
    share_parts = column_share(order.take(normal_one))
    attn_partial = dotf(order.take(attended), attn_out).astype(jnp.bfloat16)
    order.mark(attn_partial)
    attn_sum = scatter(attn_partial)
    while grad_ring.steps_left():
        steps(grad_ring)
    share_parts = order.take(*share_parts)
    order.mark(*share_parts)
    grad_full = order.take(grad_ring.rows())
    act_grad = jnp.einsum("td,fd->tf", grad_full, down_weight, preferred_element_type=jnp.float32)
    normal_share = ring_rows(share_parts)
    order.mark(act_grad, normal_share)
    hidden_res = inputs + order.take(attn_sum).astype(jnp.float32)
    normal_two = normalize(hidden_res, mlp_gain).astype(jnp.bfloat16)
    order.mark(normal_two)
    normal_full = order.take(gather(normal_two))
    gate = dotf(normal_full, gate_weight)
    upward = dotf(normal_full, up_weight)
    activated = gated(gate, upward).astype(jnp.bfloat16)
    _, gated_pull = jax.vjp(gated, gate, upward)
    gate_grad32, up_grad32 = gated_pull(act_grad)
    gate_low = gate_grad32.astype(jnp.bfloat16)
    up_low = up_grad32.astype(jnp.bfloat16)
    two_partial = (
        jnp.einsum("tf,df->td", gate_low, gate_weight, preferred_element_type=jnp.float32)
        + jnp.einsum("tf,df->td", up_low, up_weight, preferred_element_type=jnp.float32)
    ).astype(jnp.bfloat16)
    order.mark(two_partial)
    two_sum = scatter(two_partial)
    down_part = weight_grad(order.take(activated), grad_full)
    order.mark(down_part)
    down = sum_halves(order.take(down_part), 1)
    order.mark([lane.sent for lane in down])
    gate_part = weight_grad(order.take(normal_full), gate_low)
    order.mark(gate_part)
    gate_lane = Lane(order.take(gate_part), first, 0)
    order.mark(gate_lane.sent)
    steps(*down)
    up_part = weight_grad(order.take(normal_full), up_low)
    order.mark(up_part)
    up_lane = Lane(order.take(up_part), second, 0)
    order.mark(up_lane.sent)
    steps(gate_lane, up_lane)
    steps(*down)
    result_partial = dotf(order.take(activated), down_weight).astype(jnp.bfloat16)
    order.mark(result_partial)
    normal_two_grad = order.take(two_sum).astype(jnp.float32)
    _, norm_pull_two = jax.vjp(normalize, hidden_res, mlp_gain)
    resid_from_norm, mlp_gain_part = norm_pull_two(normal_two_grad)
    hidden_grad = out_grad.astype(jnp.float32) + resid_from_norm
    branch = hidden_grad.astype(jnp.bfloat16)
    order.mark(branch)
    branch_full = gather(branch)
    steps(gate_lane, up_lane)
    steps(*down)
    mlp_gain_sum = SmallSum(order.take(mlp_gain_part), "mp")
    steps(gate_lane, up_lane)
    steps(mlp_gain_sum)
    steps(*down)
    while mlp_gain_sum.bits:
        steps(mlp_gain_sum)
    branch_full = order.take(branch_full)
    attended_low = jnp.einsum(
        "td,kd->tk", branch_full, attn_out, preferred_element_type=jnp.float32
    ).astype(jnp.bfloat16)
    order.mark(attended_low)
    result_sum = scatter(order.take(result_partial))
    steps(gate_lane, up_lane)
    query_low, key_grads, value_grads = attention_backward(
        group, query_full, order.take(attended_low), sources, kept, logs, local_heads, head_dim
    )
    beside = [lane.flying for lane in down + [gate_lane, up_lane]]
    query_low, key_grads, value_grads = lax.optimization_barrier(
        (query_low, key_grads, value_grads, *beside)
    )[:3]
    order.mark(query_low)
    key_sum = BlockSum(order.take(key_grads), first)
    value_sum = BlockSum(order.take(value_grads), second)
    order.mark(key_sum.sent, value_sum.sent)
    latent_partial = jnp.einsum(
        "tk,rk->tr", order.take(query_low), query_up, preferred_element_type=jnp.float32
    ).astype(jnp.bfloat16)
    order.mark(latent_partial)
    latent_sum = RingScatter(latent_partial)
    up_query_part = weight_grad(latent_full, order.take(query_low))
    order.mark(up_query_part)
    steps(key_sum, value_sum)
    out_part = weight_grad(order.take(attended), branch_full)
    order.mark(out_part)
    steps(*down)
    steps(latent_sum)
    out_part, up_query_part, result_sum = order.take(out_part, up_query_part, result_sum)
    order.mark(out_part, up_query_part)
    out_sum, up_query_sum = lax.psum((out_part, up_query_part), "dp")
    finish(*down)
    down_sum = lay_out(down, (activated.shape[1], grad_full.shape[1]), "down_grad")
    order.mark(down_sum)
    steps(key_sum, value_sum)
    steps(latent_sum)
    steps(gate_lane, up_lane)
    while len(key_sum.bits) > 1:
        steps(key_sum, value_sum)
    while latent_sum.steps_left():
        steps(latent_sum)
    latent_low = latent_sum.held
    low_ring = RingGather(latent_low)
    finish(gate_lane, up_lane)
    while key_sum.bits:
        steps(key_sum, value_sum)
    pair_partial = jnp.concatenate([key_sum.held, value_sum.held], axis=1)
    order.mark(pair_partial)
    pair_low_sum = RingScatter(pair_partial)
    gate_sum = lay_out([gate_lane], gate_weight.shape, "gate_grad")
    order.mark(gate_sum)
    steps(pair_low_sum, low_ring)
    up_sum = lay_out([up_lane], up_weight.shape, "up_grad")
    order.mark(up_sum)
    while pair_low_sum.steps_left():
        steps(pair_low_sum, low_ring)
    pair_low = pair_low_sum.held
    low_pair_ring = RingGather(pair_low)
    normal_one_grad = jnp.einsum(
        "tr,dr->td", latent_low, query_down, preferred_element_type=jnp.float32
    ) + jnp.einsum("tp,dp->td", order.take(pair_low), key_value, preferred_element_type=jnp.float32)
    _, norm_pull_one = jax.vjp(normalize, inputs, attn_gain)
    input_from_norm, attn_gain_part = norm_pull_one(normal_one_grad)
    input_grad = hidden_grad + input_from_norm
    order.mark(input_grad, attn_gain_part)
    attn_gain_sum = SmallSum(order.take(attn_gain_part), "mp")
    while low_ring.steps_left():
        steps(low_ring)
    steps(low_pair_ring)
    down_query_part = weight_grad(normal_share, order.take(low_ring.rows()))
    order.mark(down_query_part)
    down_query = Lane(order.take(down_query_part), first, 0)
    order.mark(down_query.sent)
    steps(attn_gain_sum)
    steps(low_pair_ring)
    while low_pair_ring.steps_left() > 1:
        steps(low_pair_ring, attn_gain_sum)
    while attn_gain_sum.bits:
        steps(attn_gain_sum)
    gains = jnp.stack([own_share(attn_gain_sum.held), own_share(mlp_gain_sum.held)])
    order.mark(gains)
    gains = SmallSum(gains, "dp")
    steps(low_pair_ring)
    pair_weight_part = weight_grad(normal_share, order.take(low_pair_ring.rows()))
    order.mark(pair_weight_part)
    pair_weight = Lane(order.take(pair_weight_part), second, 0)
    order.mark(pair_weight.sent)
    result = (hidden_res + order.take(result_sum).astype(jnp.float32)).astype(jnp.bfloat16)
    order.mark(result)
    while down_query.steps or gains.bits:
        if down_query.steps:
            steps(down_query, pair_weight)
        steps(gains)
    down_query_sum = lay_out(
        [down_query], (normal_share.shape[1], query_down.shape[1]), "query_down_grad"
    )
    pair_weight_sum = lay_out(
        [pair_weight], (normal_share.shape[1], key_value.shape[1]), "key_value_grad"
    )
    out_sum, up_query_sum = out_sum.astype(jnp.float32), up_query_sum.astype(jnp.float32)
    attn_gain_sum, mlp_gain_sum = gains.held[0], gains.held[1]
    return (
        result,
        input_grad,
        attn_gain_sum,
        down_query_sum,
        up_query_sum,
        pair_weight_sum,
        out_sum,
        mlp_gain_sum,
        gate_sum,
        up_sum,
        down_sum,
    )


def solution(mesh):
    return jax.shard_map(
        shards,
        mesh=mesh,
        in_specs=(
            P(("dp", "mp"), None),
            P(),
            P(),
            P(None, "mp"),
            P(),
            P("mp", None),
            P(),
            P(None, "mp"),
            P(None, "mp"),
            P("mp", None),
            P(("dp", "mp"), None),
        ),
        out_specs=(
            P(("dp", "mp"), None),
            P(("dp", "mp"), None),
            P("mp"),
            P("mp", None),
            P(None, "mp"),
            P("mp", None),
            P("mp", None),
            P("mp"),
            P(None, "mp"),
            P(None, "mp"),
            P("mp", None),
        ),
        check_vma=False,
    )
```

```python
import functools

import jax
import jax.numpy as jnp
from jax import lax
from jax.experimental import pallas as pl
from jax.experimental.pallas import tpu as pltpu
from jax.sharding import PartitionSpec as P

HEAD_DIM = 256
EPS = 1e-06
SHORT_PART = 128
LONG_PART = 512
BLOCK = SHORT_PART + LONG_PART
LOG2E = 1.4426950408889634
FREE = pl.CostEstimate(flops=0, bytes_accessed=0, transcendentals=0)


def dotf(left, right):
    return jnp.dot(left, right, preferred_element_type=jnp.float32)


def turned_bits(value, count):
    return sum(((value >> b) & 1) << (count - 1 - b) for b in range(count))


def bits_of(count):
    return max(count.bit_length() - 1, 0)


def chunks_of(heads):
    short = [(0, heads * SHORT_PART)]
    long = [(heads * SHORT_PART + h * LONG_PART, LONG_PART) for h in range(heads)]
    return ((0, SHORT_PART, short), (SHORT_PART, LONG_PART, long))


def spread(heads, head_dim, source, turned):
    for h in range(heads):
        cols = slice(h * head_dim, (h + 1) * head_dim)
        turned[:, h * SHORT_PART : (h + 1) * SHORT_PART] = source[:SHORT_PART, cols].T
        first = heads * SHORT_PART + h * LONG_PART
        turned[:, first : first + LONG_PART] = source[SHORT_PART:, cols].T


def visible_in(extent, width):
    key_pos = lax.broadcasted_iota(jnp.int32, (extent, width), 0)
    query_pos = lax.broadcasted_iota(jnp.int32, (extent, width), 1) & (extent - 1)
    return key_pos <= query_pos


def block_copies(own, sources, all_keys, all_values, sems):
    copies = []
    for kind, (parts, target) in enumerate(((sources[:4], all_keys), (sources[4:], all_values))):
        held = parts[0].shape[0] // BLOCK
        bits = bits_of(2 * held)
        for place, part in enumerate(parts):
            for i in range(held):
                relative = place % 2 * held + i
                if kind == 1:
                    relative = turned_bits(relative, bits)
                index = own ^ (2 * relative + place // 2)
                first = pl.multiple_of(index * BLOCK, BLOCK)
                copies.append(
                    pltpu.make_async_copy(
                        part.at[pl.ds(i * BLOCK, BLOCK), :],
                        target.at[pl.ds(first, BLOCK), :],
                        sems.at[len(copies)],
                    )
                )
    return copies


def forward_kernel(
    heads, head_dim, group, query, *refs
):
    sources, (out, kept, logs, turned, maxima, totals, all_keys, all_values, sems) = (
        refs[:8],
        refs[8:],
    )
    factor = head_dim ** (-0.5) * LOG2E
    own = group[0]
    copies = block_copies(own, sources, all_keys, all_values, sems)
    for copy in copies:
        copy.start()
    spread(heads, head_dim, query, turned)
    kept[...] = jnp.zeros_like(kept)
    maxima[...] = jnp.full_like(maxima, -jnp.inf)
    totals[...] = jnp.zeros_like(totals)
    for copy in copies:
        copy.wait()

    def one_block(index, masked):
        for offset, extent, chunks in chunks_of(heads):
            first = pl.multiple_of(index * BLOCK + offset, SHORT_PART)
            keys = all_keys[pl.ds(first, extent), :]
            values = all_values[pl.ds(first, extent), :].T
            for column, width in chunks:
                at = slice(column, column + width)
                scores = dotf(keys, turned[:, at]) * factor
                if masked:
                    scores = jnp.where(visible_in(extent, width), scores, -jnp.inf)
                old = maxima[:, at]
                new = jnp.maximum(old, jnp.max(scores, axis=0, keepdims=True))
                rescale = jnp.exp2(old - new)
                weights = jnp.exp2(scores - new)
                maxima[:, at] = new
                totals[:, at] = totals[:, at] * rescale + jnp.sum(weights, axis=0, keepdims=True)
                kept[:, at] = kept[:, at] * rescale + dotf(values, weights.astype(jnp.bfloat16))

    def step(index, carry):
        one_block(index, False)
        return carry

    lax.fori_loop(0, own, step, 0)
    one_block(own, True)
    logs[...] = maxima[...] + jnp.log2(totals[...])
    for h in range(heads):
        cols = slice(h * head_dim, (h + 1) * head_dim)
        for rows, first, width in (
            (slice(0, SHORT_PART), h * SHORT_PART, SHORT_PART),
            (slice(SHORT_PART, BLOCK), heads * SHORT_PART + h * LONG_PART, LONG_PART),
        ):
            at = slice(first, first + width)
            exact = kept[:, at] * (1.0 / totals[:, at])
            kept[:, at] = exact
            out[rows, cols] = exact.T.astype(jnp.bfloat16)


def backward_kernel(heads, head_dim, group, query, grad, kept, logs, *refs):
    sources = refs[:8]
    query_grad, key_grad, value_grad = refs[8:11]
    turned, grad_turned, total, delta, short_query, short_grad = refs[11:17]
    all_keys, all_values, sems = refs[17:]
    scale = head_dim ** (-0.5)
    factor = scale * LOG2E
    own = group[0]
    count = all_keys.shape[0] // BLOCK
    bits = bits_of(count) - 1
    copies = block_copies(own, sources, all_keys, all_values, sems)
    for copy in copies:
        copy.start()
    spread(heads, head_dim, query, turned)
    spread(heads, head_dim, grad, grad_turned)
    for h in range(heads):
        cols = slice(h * head_dim, (h + 1) * head_dim)
        rows = slice(h * SHORT_PART, (h + 1) * SHORT_PART)
        short_query[rows, :] = query[:SHORT_PART, cols]
        short_grad[rows, :] = grad[:SHORT_PART, cols]
    delta[...] = jnp.sum(grad_turned[...].astype(jnp.float32) * kept[...], axis=0, keepdims=True)
    total[...] = jnp.zeros_like(total)
    for copy in copies:
        copy.wait()

    def places(index):
        relative = index ^ own
        core, rest = relative & 1, relative >> 1
        key_place = core * (count // 2) + turned_bits(rest, bits)
        return key_place * BLOCK, (core * (count // 2) + rest) * BLOCK

    def one_block(index, masked):
        key_first, value_first = places(index)
        for offset, extent, chunks in chunks_of(heads):
            first = pl.multiple_of(index * BLOCK + offset, SHORT_PART)
            keys = all_keys[pl.ds(first, extent), :]
            values = all_values[pl.ds(first, extent), :]
            keys_turned = keys.T
            key_sum = None
            value_sum = None
            for h, (column, width) in enumerate(chunks):
                at = slice(column, column + width)
                if offset == 0:
                    rows_query, rows_grad = short_query[...], short_grad[...]
                else:
                    cols = slice(h * head_dim, (h + 1) * head_dim)
                    rows_query, rows_grad = query[SHORT_PART:, cols], grad[SHORT_PART:, cols]
                scores = dotf(keys, turned[:, at]) * factor
                chance = jnp.exp2(scores - logs[:, at])
                if masked:
                    chance = jnp.where(visible_in(extent, width), chance, 0.0)
                chance_grad = dotf(values, grad_turned[:, at])
                score_low = (chance * (chance_grad - delta[:, at])).astype(jnp.bfloat16)
                key_part = dotf(score_low, rows_query)
                value_part = dotf(chance.astype(jnp.bfloat16), rows_grad)
                key_sum = key_part if key_sum is None else key_sum + key_part
                value_sum = value_part if value_sum is None else value_sum + value_part
                total[:, at] += dotf(keys_turned, score_low)
            key_rows = pl.ds(pl.multiple_of(key_first + offset, SHORT_PART), extent)
            value_rows = pl.ds(pl.multiple_of(value_first + offset, SHORT_PART), extent)
            key_grad[key_rows, :] = (key_sum * scale).astype(jnp.bfloat16)
            value_grad[value_rows, :] = value_sum.astype(jnp.bfloat16)

    def step(index, carry):
        one_block(index, False)
        return carry

    def clear(index, carry):
        nothing = jnp.zeros((BLOCK, head_dim), jnp.bfloat16)
        key_first, value_first = places(index)
        key_grad[pl.ds(pl.multiple_of(key_first, SHORT_PART), BLOCK), :] = nothing
        value_grad[pl.ds(pl.multiple_of(value_first, SHORT_PART), BLOCK), :] = nothing
        return carry

    lax.fori_loop(0, own, step, 0)
    one_block(own, True)
    lax.fori_loop(own + 1, count, clear, 0)
    for h in range(heads):
        cols = slice(h * head_dim, (h + 1) * head_dim)
        for rows, first, width in (
            (slice(0, SHORT_PART), h * SHORT_PART, SHORT_PART),
            (slice(SHORT_PART, BLOCK), heads * SHORT_PART + h * LONG_PART, LONG_PART),
        ):
            query_grad[rows, cols] = (total[:, first : first + width] * scale).T.astype(jnp.bfloat16)


def in_vmem(count):
    return [pl.BlockSpec(memory_space=pltpu.VMEM)] * count


def gathered_scratch(sources, head_dim):
    rows = sum(part.shape[0] for part in sources[:4])
    return [
        pltpu.VMEM((rows, head_dim), jnp.bfloat16),
        pltpu.VMEM((rows, head_dim), jnp.bfloat16),
        pltpu.SemaphoreType.DMA((2 * rows // BLOCK,)),
    ], rows


def attention_forward(group, query, sources, heads, head_dim):
    columns = heads * BLOCK
    scratch, rows = gathered_scratch(sources, head_dim)
    return pl.pallas_call(
        functools.partial(forward_kernel, heads, head_dim),
        out_shape=(
            jax.ShapeDtypeStruct(query.shape, jnp.bfloat16),
            jax.ShapeDtypeStruct((head_dim, columns), jnp.float32),
            jax.ShapeDtypeStruct((1, columns), jnp.float32),
        ),
        in_specs=[pl.BlockSpec(memory_space=pltpu.SMEM)]
        + in_vmem(1)
        + [pl.BlockSpec(memory_space=pl.ANY)] * 8,
        out_specs=tuple(in_vmem(3)),
        scratch_shapes=[
            pltpu.VMEM((head_dim, columns), jnp.bfloat16),
            pltpu.VMEM((1, columns), jnp.float32),
            pltpu.VMEM((1, columns), jnp.float32),
        ]
        + scratch,
        compiler_params=pltpu.CompilerParams(vmem_limit_bytes=50 << 20),
        cost_estimate=pl.CostEstimate(flops=2 * columns * rows * head_dim * 2, bytes_accessed=4 * rows * head_dim, transcendentals=0),
        name="attention_forward",
    )(group, query, *sources)


def attention_backward(group, query, grad, sources, kept, logs, heads, head_dim):
    columns = heads * BLOCK
    scratch, rows = gathered_scratch(sources, head_dim)
    return pl.pallas_call(
        functools.partial(backward_kernel, heads, head_dim),
        out_shape=(
            jax.ShapeDtypeStruct(query.shape, jnp.bfloat16),
            jax.ShapeDtypeStruct((rows, head_dim), jnp.bfloat16),
            jax.ShapeDtypeStruct((rows, head_dim), jnp.bfloat16),
        ),
        in_specs=[pl.BlockSpec(memory_space=pltpu.SMEM)]
        + in_vmem(4)
        + [pl.BlockSpec(memory_space=pl.ANY)] * 8,
        out_specs=tuple(in_vmem(3)),
        scratch_shapes=[
            pltpu.VMEM((head_dim, columns), jnp.bfloat16),
            pltpu.VMEM((head_dim, columns), jnp.bfloat16),
            pltpu.VMEM((head_dim, columns), jnp.float32),
            pltpu.VMEM((1, columns), jnp.float32),
            pltpu.VMEM((heads * SHORT_PART, head_dim), jnp.bfloat16),
            pltpu.VMEM((heads * SHORT_PART, head_dim), jnp.bfloat16),
        ]
        + scratch,
        compiler_params=pltpu.CompilerParams(vmem_limit_bytes=56 << 20),
        cost_estimate=pl.CostEstimate(flops=2 * columns * rows * head_dim * 2, bytes_accessed=4 * rows * head_dim, transcendentals=0),
        name="attention_backward",
    )(group, query, grad, kept, logs, *sources)


def normalize(rows, gain):
    return rows * lax.rsqrt(jnp.mean(rows * rows, axis=-1, keepdims=True) + EPS) * gain


def gated(gate_in, up_in):
    return jax.nn.silu(gate_in) * up_in


def after(value, *others):
    return lax.optimization_barrier((value,) + others)[0]


class Order:
    def __init__(self):
        self.last = ()

    def take(self, *values):
        out = lax.optimization_barrier(values + self.last)[: len(values)]
        return out if len(values) > 1 else out[0]

    def mark(self, *values):
        self.last = tuple(jax.tree.leaves(values))


def add_low(left, right):
    return (left.astype(jnp.float32) + right.astype(jnp.float32)).astype(jnp.bfloat16)


def plus_kernel(held, got, *outs):
    value = held[...].astype(jnp.float32) + got[...].astype(jnp.float32)
    if len(outs) == 1:
        outs[0][...] = value.astype(jnp.bfloat16)
        return
    half = pl.num_programs(0) // 2

    @pl.when(pl.program_id(0) < half)
    def _():
        outs[0][...] = value.astype(jnp.bfloat16)

    @pl.when(pl.program_id(0) >= half)
    def _():
        outs[1][...] = value.astype(jnp.bfloat16)


def plus(held, got, halves):
    rows, width = held.shape
    steps = 4 if rows % 64 == 0 else 2
    block = (rows // steps, width)
    if halves:
        half = steps // 2
        source = lambda i: (lax.rem(i + half, steps), 0)
        out_specs = [
            pl.BlockSpec(block, lambda i: (jnp.minimum(i, half - 1), 0)),
            pl.BlockSpec(block, lambda i: (jnp.maximum(i - half, 0), 0)),
        ]
        out_shape = [jax.ShapeDtypeStruct((rows // 2, width), jnp.bfloat16)] * 2
    else:
        source = lambda i: (i, 0)
        out_specs = [pl.BlockSpec(block, source)]
        out_shape = [jax.ShapeDtypeStruct((rows, width), jnp.bfloat16)]
    out = pl.pallas_call(
        plus_kernel,
        grid=(steps,),
        in_specs=[pl.BlockSpec(block, source)] * 2,
        out_specs=out_specs,
        out_shape=out_shape,
        compiler_params=pltpu.CompilerParams(vmem_limit_bytes=24 << 20),
        cost_estimate=FREE,
        name="plus",
    )(held, got)
    return out if halves else out[0]


def join_kernel(axis, *refs):
    *parts, out, inside, in_sems, out_sems = refs
    arriving, leaving, first = [], [], 0
    for i, part in enumerate(parts):
        extent = part.shape[axis]
        cut = (pl.ds(first, extent), slice(None)) if axis == 0 else (slice(None), pl.ds(first, extent))
        arriving.append(pltpu.make_async_copy(part, inside.at[cut], in_sems.at[i]))
        leaving.append(pltpu.make_async_copy(inside.at[cut], out.at[cut], out_sems.at[i]))
        first += extent
    for copy in arriving:
        copy.start()
    for arrived, left in zip(arriving, leaving):
        arrived.wait()
        left.start()
    for copy in leaving:
        copy.wait()


def join(parts, axis):
    shape = list(parts[0].shape)
    shape[axis] = sum(part.shape[axis] for part in parts)
    anywhere = pl.BlockSpec(memory_space=pl.ANY)
    return pl.pallas_call(
        functools.partial(join_kernel, axis),
        in_specs=[anywhere] * len(parts),
        out_specs=anywhere,
        out_shape=jax.ShapeDtypeStruct(tuple(shape), parts[0].dtype),
        scratch_shapes=[
            pltpu.VMEM(tuple(shape), parts[0].dtype),
            pltpu.SemaphoreType.DMA((len(parts),)),
            pltpu.SemaphoreType.DMA((len(parts),)),
        ],
        compiler_params=pltpu.CompilerParams(vmem_limit_bytes=24 << 20),
        cost_estimate=FREE,
        name="join",
    )(*parts)


def rows_kernel(contract, count, places, *refs):
    parts, (weight, out) = refs[:count], refs[count:]
    for i, part in enumerate(parts):
        rows = part.shape[contract[0] ^ 1]
        out[pl.ds(pl.multiple_of(places[i] * rows, 16), rows), :] = lax.dot_general(
            part[...],
            weight[...],
            (((contract[0],), (contract[1],)), ((), ())),
            preferred_element_type=jnp.float32,
        ).astype(jnp.bfloat16)


def rows_product(parts, weight, contract, name, places=None):
    count = len(parts)
    if places is None:
        places = jnp.arange(count, dtype=jnp.int32)
    rows, width = parts[0].shape[contract[0] ^ 1], weight.shape[contract[1] ^ 1]
    return pl.pallas_call(
        functools.partial(rows_kernel, contract, count),
        in_specs=[pl.BlockSpec(memory_space=pltpu.SMEM)] + in_vmem(count + 1),
        out_specs=pl.BlockSpec(memory_space=pltpu.VMEM),
        out_shape=jax.ShapeDtypeStruct((rows * count, width), jnp.bfloat16),
        compiler_params=pltpu.CompilerParams(vmem_limit_bytes=40 << 20),
        cost_estimate=FREE,
        name=name,
    )(places, *parts, weight)


def ring_of(count):
    return [0] + list(range(1, count, 2)) + list(range(2, count, 2))[::-1]


def ring_place(back):
    ring = ring_of(lax.axis_size("mp"))
    count = len(ring)
    table = [ring[(ring.index(i) - back) % count] for i in range(count)]
    return jnp.asarray(table, jnp.int32)[lax.axis_index("mp")]


def ring_pass(array):
    ring = ring_of(lax.axis_size("mp"))
    pairs = [(ring[i], ring[(i + 1) % len(ring)]) for i in range(len(ring))]
    return lax.ppermute(array, "mp", pairs)


def put_rows(whole_rows, rows, place):
    return lax.dynamic_update_slice_in_dim(whole_rows, rows, place * rows.shape[0], 0)


def take_rows(whole_rows, place):
    count = whole_rows.shape[0] // lax.axis_size("mp")
    return lax.dynamic_slice_in_dim(whole_rows, place * count, count, 0)


def ring_rows(parts):
    out = jnp.zeros((parts[0].shape[0] * len(parts),) + parts[0].shape[1:], parts[0].dtype)
    for step, rows in enumerate(parts):
        out = put_rows(out, rows, ring_place(step))
    return out


class RingGather:
    def __init__(self, rows):
        self.parts = [rows]
        self.start()

    def start(self):
        if len(self.parts) < lax.axis_size("mp"):
            self.flying = ring_pass(self.parts[-1])

    def step(self, order):
        if len(self.parts) < lax.axis_size("mp"):
            rows = order.take(self.flying)
            order.mark(rows)
            self.parts.append(rows)
            self.start()

    def steps_left(self):
        return lax.axis_size("mp") - len(self.parts)

    def rows(self):
        return ring_rows(self.parts)


class RingScatter:
    def __init__(self, part):
        self.part, self.steps = part, 1
        self.held = part(1)
        self.flying = ring_pass(self.held)

    def step(self, order):
        if self.steps_left():
            self.steps += 1
            got, own = order.take(self.flying, self.part(self.steps % lax.axis_size("mp")))
            self.held = add_low(own, got)
            order.mark(self.held)
            if self.steps_left():
                self.flying = ring_pass(self.held)

    def steps_left(self):
        return lax.axis_size("mp") - self.steps


def trade(array, bit):
    count = lax.axis_size("dp")
    return lax.ppermute(array, "dp", [(i, i ^ (1 << bit)) for i in range(count)])


def bit_here(bit):
    return (lax.axis_index("dp") >> bit) & 1


def orders():
    rest = list(range(1, bits_of(lax.axis_size("dp"))))
    return [0] + rest, [0] + rest[::-1]


class Lane:
    def __init__(self, partial, order, axis):
        self.bits, self.axis = order, axis
        self.steps = [("halve", bit) for bit in order]
        self.steps += [("double", bit) for bit in order[:0:-1]] + [("core", 0)]
        self.cut_and_start(lambda which, half: self.cut(partial, which, half), partial.shape[axis])

    def cut(self, array, which, half):
        return lax.dynamic_slice_in_dim(array, which * half, half, self.axis)

    def cut_and_start(self, part, extent):
        bit = self.steps[0][1]
        mine = bit_here(bit)
        self.sent, self.held = part(1 - mine, extent // 2), part(mine, extent // 2)
        self.flying = trade(self.sent, bit)

    def step(self, order):
        kind, _ = self.steps.pop(0)
        got, held = order.take(self.flying, self.held)
        if not self.steps:
            self.pieces = [held, got]
            order.mark(self.pieces)
            return
        following, bit = self.steps[0]
        if kind == "halve" and following == "halve":
            self.cut_and_start(
                lambda which, half: add_low(self.cut(held, which, half), self.cut(got, which, half)),
                held.shape[self.axis],
            )
        else:
            if kind == "halve":
                self.held = add_low(held, got)
            else:
                self.held = jnp.concatenate([held, got], axis=self.axis)
            self.sent = self.held
            self.flying = trade(self.sent, bit)
        order.mark(self.sent, self.held)

    def places(self):
        own = jnp.int32(0)
        for bit in self.bits[1:]:
            own = own * 2 + bit_here(bit)
        count = 1 << (len(self.bits) - 1)
        relative = jnp.arange(count, dtype=jnp.int32) ^ own
        core = bit_here(0)
        return jnp.concatenate([core * count + relative, (1 - core) * count + relative])


def kept_first(first_bit_first):
    count = lax.axis_size("dp")
    bits = bits_of(count) - 1
    order = [turned_bits(i, bits) if first_bit_first else i for i in range(count // 2)]
    own = lax.axis_index("dp").astype(jnp.int32)
    relative = jnp.asarray([2 * i for i in order] + [2 * i + 1 for i in order], jnp.int32)
    return relative ^ own


def product_kernel(groups, split, places, *refs):
    inputs, at = [], 0
    for parts, beside in groups:
        inputs.append((refs[at : at + parts], refs[at + parts : at + parts * (1 + beside)]))
        at += parts * (1 + beside)
    scratch = refs[len(refs) - 2 * len(groups) :]
    values = []
    for g, ((lefts, rights), (parts, _)) in enumerate(zip(inputs, groups)):
        left, right = scratch[2 * g : 2 * g + 2]
        count, width = rights[0].shape

        @pl.when(pl.program_id(0) == 0)
        def _(rights=rights, right=right, count=count, width=width, parts=parts):
            for i, part in enumerate(rights):
                row, column = i % parts * count, i // parts * width
                right[row : row + count, column : column + width] = part[...]

        for i, part in enumerate(lefts):
            left[i * count : (i + 1) * count, :] = part[...]
        values.append(
            lax.dot_general(
                left[...], right[...], (((0,), (0,)), ((), ())), preferred_element_type=jnp.float32
            ).astype(jnp.bfloat16)
        )
    first = 0
    for value in values:
        cut = (slice(None), slice(first, first + value.shape[1]))
        first += value.shape[1]
        if split is None:
            refs[at][cut] = value
            continue
        other, sent, held = refs[at : at + 3]
        total = (value.astype(jnp.float32) + other[cut].astype(jnp.float32)).astype(jnp.bfloat16)

        @pl.when(pl.program_id(0) < split)
        def _(total=total, cut=cut):
            sent[cut] = total

        @pl.when(pl.program_id(0) >= split)
        def _(total=total, cut=cut):
            held[cut] = total


def product_blocks(products, places, rows, name, other=None):
    blocks = places.shape[0]
    if other is None:
        split, order, inputs = None, lambda i: i, ()
    else:
        split, order, inputs = blocks // 2, lambda i: lax.rem(i + blocks // 2, blocks), (other,)
    arrays, in_specs, scratch, groups, total = [], [], [], [], 0
    for lefts, rights in products:
        tokens = lefts[0].shape[0]
        moving = pl.BlockSpec((tokens, rows), lambda i, places: (0, places[order(i)]))
        arrays += list(lefts)
        in_specs += [moving] * len(lefts)
        width = sum(right[0].shape[1] for right in rights)
        for right in rights:
            arrays += list(right)
            in_specs += [pl.BlockSpec(right[0].shape, lambda i, places: (0, 0))] * len(right)
        scratch += [
            pltpu.VMEM((tokens * len(lefts), rows), jnp.bfloat16),
            pltpu.VMEM((tokens * len(lefts), width), jnp.bfloat16),
        ]
        groups.append((len(lefts), len(rights)))
        total += width
    block = (rows, total)
    if other is None:
        out_specs = pl.BlockSpec(block, lambda i, places: (i, 0))
        out_shape = jax.ShapeDtypeStruct((blocks * rows, total), jnp.bfloat16)
    else:
        in_specs.append(pl.BlockSpec(block, lambda i, places: (order(i), 0)))
        out_specs = [
            pl.BlockSpec(block, lambda i, places: (jnp.minimum(i, split - 1), 0)),
            pl.BlockSpec(block, lambda i, places: (jnp.maximum(i - split, 0), 0)),
        ]
        out_shape = [jax.ShapeDtypeStruct((split * rows, total), jnp.bfloat16)] * 2
    return pl.pallas_call(
        functools.partial(product_kernel, tuple(groups), split),
        grid_spec=pltpu.PrefetchScalarGridSpec(
            num_scalar_prefetch=1,
            grid=(blocks,),
            in_specs=in_specs,
            out_specs=out_specs,
            scratch_shapes=scratch,
        ),
        out_shape=out_shape,
        compiler_params=pltpu.CompilerParams(vmem_limit_bytes=48 << 20),
        cost_estimate=FREE,
        name=name,
    )(places, *arrays, *inputs)


class BlockLane:
    def __init__(self, order, products, bits, name, first_row=0, rows=None):
        self.bits, self.name, self.products = list(bits), name, products
        self.rows = rows or products[0][0][0].shape[1] // lax.axis_size("dp")
        self.first_row = first_row
        self.places = kept_first(bits[1] == 1)
        self.table = self.places + first_row // self.rows
        half = self.places.shape[0] // 2
        self.sent = product_blocks(self.taken(order), self.table[half:], self.rows, name + "_sent")
        order.mark(self.sent)
        self.flying = trade(self.sent, 0)
        self.steps = ["product"] + ["halve"] * (len(bits) - 1) + ["double"] * (len(bits) - 1)
        self.steps += ["core"]

    def taken(self, order):
        leaves, shape = jax.tree.flatten(self.products)
        return jax.tree.unflatten(shape, order.take(*leaves))

    def step(self, order):
        kind = self.steps.pop(0)
        if kind == "product":
            self.bits.pop(0)
            got = order.take(self.flying)
            half = self.places.shape[0] // 2
            self.sent, self.held = product_blocks(
                self.taken(order), self.table[:half], self.rows, self.name + "_kept", got
            )
            self.done_bits = []
            self.flying = trade(self.sent, self.bits[0])
            order.mark(self.sent, self.held)
            return
        if kind == "both":
            near, far, own = order.take(*self.flying, self.held)
            self.held = self.sent = (own, near, far)
            self.flying = trade(near, self.done_bits[0])
            order.mark(self.held)
            return
        if kind == "rest":
            self.held = self.sent = join(order.take(*self.held, self.flying), 0)
            self.flying = trade(self.held, 0)
            order.mark(self.held)
            return
        got, held = order.take(self.flying, self.held)
        if kind == "core":
            self.pieces = [held, got]
            order.mark(self.pieces)
            return
        if kind == "halve":
            self.done_bits.append(self.bits.pop(0))
            if self.bits:
                self.sent, self.held = plus(held, got, True)
                self.flying = trade(self.sent, self.bits[0])
                order.mark(self.sent, self.held)
                return
            held = plus(held, got, False)
            if len(self.done_bits) == 2:
                self.steps = ["both", "rest", "core"]
                self.held = self.sent = held
                self.flying = (trade(held, self.done_bits[1]), trade(held, self.done_bits[0]))
                order.mark(held)
                return
        else:
            self.done_bits.pop()
            held = join([held, got], 0)
        self.held = self.sent = held
        self.flying = trade(held, self.done_bits[-1] if self.done_bits else 0)
        order.mark(self.held)


def block_lanes(order, products, name):
    first, second = orders()
    total = products[0][0][0].shape[1]
    rows = total // lax.axis_size("dp")
    if rows % 256:
        return [BlockLane(order, products, first, name)]
    return [
        BlockLane(order, products, first, name + "_low", 0, rows // 2),
        BlockLane(order, products, second, name + "_high", total // 2, rows // 2),
    ]


def unfold_kernel(firsts, pieces, targets, places, *refs):
    sets = 2 * len(firsts)
    sources, outs = refs[:sets], refs[sets : sets + len(targets)]
    landed = refs[sets + len(targets)]
    raised = refs[sets + len(targets) + 1 : -2]
    in_sems, out_sems = refs[-2:]
    rows = landed.shape[1]
    slots = raised[0].shape[0]
    total = sets * pieces

    def fetch(i):
        source = sources[i // pieces]
        return pltpu.make_async_copy(
            source.at[pl.ds(i % pieces * rows, rows), :], landed.at[i], in_sems.at[i]
        )

    def store(i):
        along = pl.multiple_of(firsts[i // (2 * pieces)] + places[i] * rows, rows)
        copies = []
        for k, ((_, turned), out) in enumerate(zip(targets, outs)):
            window = out.at[:, pl.ds(along, rows)] if turned else out.at[pl.ds(along, rows), :]
            copies.append(
                pltpu.make_async_copy(
                    raised[k].at[i % slots], window, out_sems.at[i * len(targets) + k]
                )
            )
        return copies

    for i in range(total):
        fetch(i).start()
    for i in range(total):
        fetch(i).wait()
        if i >= slots:
            for copy in store(i - slots):
                copy.wait()
        first = 0
        for k, (width, turned) in enumerate(targets):
            value = landed[i, :, first : first + width].astype(jnp.float32)
            raised[k][i % slots] = value.T if turned else value
            first += width
        for copy in store(i):
            copy.start()
    for i in range(max(total - slots, 0), total):
        for copy in store(i):
            copy.wait()


def unfold(lanes, targets, name):
    sets = [piece for lane in lanes for piece in lane.pieces]
    rows, width = lanes[0].rows, sets[0].shape[1]
    pieces = sets[0].shape[0] // rows
    total, slots = len(sets) * pieces, 4
    height = total * rows
    anywhere = pl.BlockSpec(memory_space=pl.ANY)
    return pl.pallas_call(
        functools.partial(
            unfold_kernel, tuple(lane.first_row for lane in lanes), pieces, tuple(targets)
        ),
        in_specs=[pl.BlockSpec(memory_space=pltpu.SMEM)] + [anywhere] * len(sets),
        out_specs=[anywhere] * len(targets),
        out_shape=[
            jax.ShapeDtypeStruct((w, height) if turned else (height, w), jnp.float32)
            for w, turned in targets
        ],
        scratch_shapes=[pltpu.VMEM((total, rows, width), jnp.bfloat16)]
        + [
            pltpu.VMEM((slots, w, rows) if turned else (slots, rows, w), jnp.float32)
            for w, turned in targets
        ]
        + [
            pltpu.SemaphoreType.DMA((total,)),
            pltpu.SemaphoreType.DMA((total * len(targets),)),
        ],
        compiler_params=pltpu.CompilerParams(vmem_limit_bytes=48 << 20),
        cost_estimate=FREE,
        name=name,
    )(jnp.concatenate([lane.places for lane in lanes]), *sets)


def lay_kernel(lanes, sets, pieces, axis, cuts, places, *refs):
    outs = refs[lanes * sets : -4]
    landed, raised, in_sems, out_sems = refs[-4:]
    rows, columns = landed.shape[1:]
    slots = raised.shape[0]
    total = lanes * sets * pieces

    def window(ref, along, across, extent):
        if axis == 0:
            return ref.at[pl.ds(along, rows), pl.ds(across, extent)]
        return ref.at[pl.ds(across, extent), pl.ds(along, columns)]

    def fetch(i):
        first = i % pieces * (rows, columns)[axis]
        source = refs[i // pieces]
        across = source.shape[1 - axis]
        return pltpu.make_async_copy(
            window(source, first, 0, across), window(landed.at[i], 0, 0, across), in_sems.at[i]
        )

    def store(i):
        along = pl.multiple_of(places[i] * (rows, columns)[axis], (rows, columns)[axis])
        return [
            pltpu.make_async_copy(
                window(raised.at[i % slots], 0, first, extent),
                window(outs[out], along, target, extent),
                out_sems.at[2 * i + k],
            )
            for k, (out, first, extent, target) in enumerate(cuts[i // (sets * pieces)])
        ]

    for i in range(total):
        fetch(i).start()
    for i in range(total):
        fetch(i).wait()
        if i >= slots:
            for copy in store(i - slots):
                copy.wait()
        extent = refs[i // pieces].shape[1 - axis]
        filled = (slice(None), slice(extent)) if axis == 0 else (slice(extent), slice(None))
        raised[(i % slots, *filled)] = landed[(i, *filled)].astype(jnp.float32)
        for copy in store(i):
            copy.start()
    for i in range(max(total - slots, 0), total):
        for copy in store(i):
            copy.wait()


def lay_out(lanes, cuts, shapes, name):
    sets = [piece for lane in lanes for piece in lane.pieces]
    axis = lanes[0].axis
    places = jnp.concatenate([lane.places() for lane in lanes])
    pieces = places.shape[0] // len(sets)
    block = [max(piece.shape[d] for piece in sets) for d in (0, 1)]
    block[axis] //= pieces
    total = len(sets) * pieces
    anywhere = pl.BlockSpec(memory_space=pl.ANY)
    return pl.pallas_call(
        functools.partial(lay_kernel, len(lanes), len(lanes[0].pieces), pieces, axis, cuts),
        in_specs=[pl.BlockSpec(memory_space=pltpu.SMEM)] + [anywhere] * len(sets),
        out_specs=[anywhere] * len(shapes),
        out_shape=[jax.ShapeDtypeStruct(shape, jnp.float32) for shape in shapes],
        scratch_shapes=[
            pltpu.VMEM((total, *block), jnp.bfloat16),
            pltpu.VMEM((min(total, 6), *block), jnp.float32),
            pltpu.SemaphoreType.DMA((total,)),
            pltpu.SemaphoreType.DMA((2 * total,)),
        ],
        compiler_params=pltpu.CompilerParams(vmem_limit_bytes=44 << 20),
        cost_estimate=FREE,
        name=name,
    )(places, *sets)


def own_share(array):
    share = array.shape[0] // lax.axis_size("mp")
    return lax.dynamic_slice_in_dim(array, lax.axis_index("mp") * share, share)


class BlockSum:
    def __init__(self, blocks, order):
        self.bits = list(order)
        half = blocks.shape[0] // 2
        self.held, self.sent = blocks[:half], blocks[half:]
        self.flying = trade(self.sent, self.bits[0])

    def step(self, order):
        self.bits.pop(0)
        got, held = order.take(self.flying, self.held)
        if self.bits:
            self.sent, self.held = plus(held, got, True)
            self.flying = trade(self.sent, self.bits[0])
        else:
            self.held = self.sent = plus(held, got, False)
        order.mark(self.sent, self.held)


class BlockGather:
    def __init__(self, rows, order):
        self.bits, self.held = list(order), rows
        self.flying = trade(rows, self.bits[0])

    def step(self, order):
        if not self.bits:
            got = order.take(*self.flying)
            order.mark(got)
            self.parts = self.held + list(got)
            return
        self.bits.pop(0)
        got, held = order.take(self.flying, self.held)
        if self.bits:
            self.held = jnp.concatenate([held, got], axis=0)
            self.flying = trade(self.held, self.bits[0])
        else:
            self.held = [held, got]
            self.flying = [trade(part, 0) for part in self.held]
        order.mark(self.held)


class SmallSum:
    def __init__(self, array, axis):
        self.axis, self.held = axis, array
        self.bits = list(range(bits_of(lax.axis_size(axis))))
        self.start()

    def start(self):
        if self.bits:
            count = lax.axis_size(self.axis)
            pairs = [(i, i ^ (1 << self.bits[0])) for i in range(count)]
            self.flying = lax.ppermute(self.held, self.axis, pairs)

    def step(self, order):
        if self.bits:
            self.bits.pop(0)
            got, held = order.take(self.flying, self.held)
            self.held = held + got
            order.mark(self.held)
            self.start()


def column_share(rows):
    ring = ring_of(lax.axis_size("mp"))
    count = len(ring)
    width = rows.shape[1] // count
    parts = []
    for step in range(count):
        part = lax.dynamic_slice_in_dim(rows, ring_place(-step) * width, width, 1)
        pairs = [(ring[i], ring[(i + step) % count]) for i in range(count)]
        parts.append(lax.ppermute(part, "mp", pairs) if step else part)
    return parts


def shards(
    tokens,
    attn_gain,
    query_down,
    query_up,
    key_value,
    attn_out,
    mlp_gain,
    gate_weight,
    up_weight,
    down_weight,
    out_grad,
):
    head_dim = HEAD_DIM
    local_heads = query_up.shape[1] // head_dim
    ranks = lax.axis_size("mp")
    group = lax.axis_index("dp").reshape(1).astype(jnp.int32)
    ring_places = jnp.stack([ring_place(i) for i in range(lax.axis_size("mp"))])
    first, second = orders()

    def rows_of(array):
        return lambda back: take_rows(array, ring_place(back))

    def parts_of(array):
        count = array.shape[0] // ranks
        return lambda back: array[back * count : (back + 1) * count]

    def weight_grad(left, right):
        return jnp.einsum("tk,td->kd", left, right, preferred_element_type=jnp.float32).astype(
            jnp.bfloat16
        )

    def steps(*moving):
        for one in moving:
            one.step(order)

    def finish(*lanes):
        while lanes[0].steps:
            steps(*lanes)

    order = Order()
    inputs = tokens.astype(jnp.float32)
    normal_one = normalize(inputs, attn_gain).astype(jnp.bfloat16)
    pair_local = dotf(normal_one, key_value).astype(jnp.bfloat16)
    order.mark(pair_local)
    pair_ring = RingGather(pair_local)
    latent = dotf(order.take(normal_one), query_down).astype(jnp.bfloat16)
    order.mark(latent)
    latent_ring = RingGather(latent)
    while pair_ring.steps_left() > 1:
        steps(pair_ring, latent_ring)
    steps(pair_ring)
    pair_own = pair_ring.rows()
    order.mark(pair_own)
    keys = BlockGather(pair_own[:, :head_dim], first[1:])
    values = BlockGather(pair_own[:, head_dim:], second[1:])
    while latent_ring.steps_left():
        steps(latent_ring)
    grad_ring = RingGather(order.take(out_grad))
    latent_full = order.take(latent_ring.rows())
    query_full = dotf(latent_full, query_up).astype(jnp.bfloat16)
    order.mark(query_full)
    steps(keys, values, grad_ring)
    while keys.bits:
        steps(keys, values)
    steps(grad_ring, keys, values)
    share_parts = column_share(order.take(normal_one))
    sources = order.take(*keys.parts, *values.parts)
    attended, kept, logs = attention_forward(group, query_full, sources, local_heads, head_dim)
    order.mark(attended)
    share_parts = order.take(*share_parts)
    order.mark(*share_parts)
    steps(grad_ring)
    attn_partial = dotf(order.take(attended), attn_out).astype(jnp.bfloat16)
    order.mark(attn_partial)
    attn_ring = RingScatter(rows_of(attn_partial))
    while grad_ring.steps_left():
        steps(grad_ring)
    grad_ringed = jnp.concatenate(order.take(*grad_ring.parts), axis=0)
    act_grad = jnp.einsum("td,fd->tf", grad_ringed, down_weight, preferred_element_type=jnp.float32)
    normal_share = ring_rows(share_parts)
    order.mark(act_grad, normal_share)
    while attn_ring.steps_left():
        steps(attn_ring)
    hidden_res = inputs + attn_ring.held.astype(jnp.float32)
    normal_two = normalize(hidden_res, mlp_gain).astype(jnp.bfloat16)
    order.mark(normal_two)
    two_ring = RingGather(normal_two)
    act_parts = parts_of(act_grad)
    activated, gate_low, up_low, two_terms = [], [], [], []
    two_sum = None
    for block in range(ranks):
        steps(*([two_ring] if block else []))
        rows = order.take(two_ring.parts[block])
        gate = dotf(rows, gate_weight)
        upward = dotf(rows, up_weight)
        _, gated_pull = jax.vjp(gated, gate, upward)
        gate_grad32, up_grad32 = gated_pull(act_parts(block))
        activated.append(gated(gate, upward).astype(jnp.bfloat16))
        gate_low.append(gate_grad32.astype(jnp.bfloat16))
        up_low.append(up_grad32.astype(jnp.bfloat16))
        two_terms.append(
            (
                jnp.einsum("tf,df->td", gate_low[-1], gate_weight, preferred_element_type=jnp.float32)
                + jnp.einsum("tf,df->td", up_low[-1], up_weight, preferred_element_type=jnp.float32)
            ).astype(jnp.bfloat16)
        )
        order.mark(two_terms[-1], activated[-1])
        if block == 1:
            two_sum = RingScatter(lambda back: two_terms[back])
        elif block > 1:
            steps(two_sum)
    while two_sum.steps_left():
        steps(two_sum)
    normal_two_grad = two_sum.held.astype(jnp.float32)
    _, norm_pull_two = jax.vjp(normalize, hidden_res, mlp_gain)
    resid_from_norm, mlp_gain_part = norm_pull_two(normal_two_grad)
    hidden_grad = out_grad.astype(jnp.float32) + resid_from_norm
    branch = hidden_grad.astype(jnp.bfloat16)
    order.mark(branch)
    branch_ring = RingGather(branch)
    def part_sent(*lanes):
        order.mark([lane.sent for lane in lanes])

    low_parts = []

    def low_part():
        rows = order.take(branch_ring.parts[len(low_parts)])
        low_parts.append(rows_product([rows], attn_out, (1, 1), "attended_low"))
        order.mark(low_parts[-1])

    mlp = block_lanes(
        order,
        [(grad_ring.parts, [activated]), (two_ring.parts, [gate_low, up_low])],
        "mlp_grads",
    )
    steps(branch_ring)
    low_part()
    low_part()
    steps(mlp[0])
    steps(branch_ring)
    low_part()
    steps(*mlp[1:])
    while branch_ring.steps_left():
        steps(branch_ring)
        low_part()
    while len(low_parts) < ranks:
        low_part()
    attended_low = ring_rows(low_parts)
    order.mark(attended_low)
    query_low, key_grads, value_grads = attention_backward(
        group, query_full, order.take(attended_low), sources, kept, logs, local_heads, head_dim
    )
    query_low, key_grads, value_grads = lax.optimization_barrier(
        (query_low, key_grads, value_grads, mlp[0].flying)
    )[:3]
    order.mark(query_low)
    key_sum = BlockSum(order.take(key_grads), first)
    value_sum = BlockSum(order.take(value_grads), second)
    part_sent(key_sum, value_sum)
    steps(*mlp)
    latent_partial = rows_product([order.take(query_low)], query_up, (1, 1), "latent_low")
    order.mark(latent_partial)
    latent_low = lax.psum_scatter(latent_partial, "mp", scatter_dimension=0, tiled=True)
    steps(key_sum, value_sum)
    up_query_part = rows_product([latent_full], order.take(query_low), (0, 0), "query_up_grad")
    out_part = weight_grad(attended, ring_rows(order.take(*branch_ring.parts)))
    order.mark(up_query_part, out_part)
    out_sum, up_query_sum = lax.psum((out_part, up_query_part), "dp")
    steps(key_sum, value_sum)
    steps(*mlp)
    while key_sum.bits:
        steps(key_sum, value_sum)
    pair_partial = join(order.take(key_sum.held, value_sum.held), 1)
    order.mark(pair_partial)
    pair_low_sum = RingScatter(rows_of(pair_partial))
    steps(pair_low_sum)
    latent_low = order.take(latent_low)
    order.mark(latent_low)
    low_full = lax.all_gather(latent_low, "mp", axis=0, tiled=True)
    while pair_low_sum.steps_left():
        steps(pair_low_sum)
    pair_low = pair_low_sum.held
    low_pair_ring = RingGather(pair_low)
    result_partial = rows_product(
        order.take(*activated), down_weight, (1, 0), "result", ring_places
    )
    order.mark(result_partial)
    steps(low_pair_ring)
    steps(*mlp)
    while low_pair_ring.steps_left():
        steps(low_pair_ring)
    pair_weight_part = rows_product(
        [normal_share], order.take(low_pair_ring.rows()), (0, 0), "key_value_grad"
    )
    order.mark(pair_weight_part)
    pair_weight = Lane(order.take(pair_weight_part), first, 0)
    part_sent(pair_weight)
    down_query_part = rows_product(
        [normal_share], order.take(low_full), (0, 0), "query_down_grad"
    )
    order.mark(down_query_part)
    down_query = Lane(order.take(down_query_part), second, 0)
    part_sent(down_query)
    result_sum = lax.psum_scatter(
        after(result_partial, low_full), "mp", scatter_dimension=0, tiled=True
    )
    steps(pair_weight, down_query)
    latent_term = jnp.einsum(
        "tr,dr->td", order.take(latent_low), query_down, preferred_element_type=jnp.float32
    )
    order.mark(latent_term)
    normal_one_grad = latent_term + jnp.einsum(
        "tp,dp->td", order.take(pair_low), key_value, preferred_element_type=jnp.float32
    )
    _, norm_pull_one = jax.vjp(normalize, inputs, attn_gain)
    input_from_norm, attn_gain_part = norm_pull_one(normal_one_grad)
    input_grad = hidden_grad + input_from_norm
    order.mark(input_grad, attn_gain_part)
    attn_gain_sum = SmallSum(order.take(attn_gain_part), "mp")
    mlp_gain_sum = SmallSum(order.take(mlp_gain_part), "mp")
    steps(pair_weight, down_query)
    while attn_gain_sum.bits or mlp_gain_sum.bits:
        steps(attn_gain_sum, mlp_gain_sum)
    gains = jnp.stack([own_share(attn_gain_sum.held), own_share(mlp_gain_sum.held)])
    order.mark(gains)
    steps(pair_weight, down_query)
    gains = SmallSum(order.take(gains), "dp")
    while len(down_query.steps) > 2:
        steps(pair_weight, down_query)
        steps(gains)
    out_sum, up_query_sum = order.take(out_sum, up_query_sum)
    order.mark(out_sum, up_query_sum)
    while len(mlp[0].steps) > 1:
        steps(*mlp)
    steps(pair_weight, down_query)
    out_sum = order.take(out_sum).astype(jnp.float32)
    up_query_sum = up_query_sum.astype(jnp.float32)
    order.mark(out_sum, up_query_sum)
    finish(pair_weight, down_query)
    while gains.bits:
        steps(gains)
    cuts = tuple(((i, 0, part.shape[1], 0),) for i, part in enumerate((query_down, key_value)))
    down_query_sum, pair_weight_sum = lay_out(
        [down_query, pair_weight],
        cuts,
        [(normal_share.shape[1], part.shape[1]) for part in (query_down, key_value)],
        "query_down_key_value_laid",
    )
    order.mark(down_query_sum)
    finish(*mlp)
    down_sum, gate_sum, up_sum = unfold(
        mlp, [(down_weight.shape[0], True)] + [(gate_weight.shape[1], False)] * 2, "mlp_grads_laid"
    )
    order.mark(down_sum)
    result = (hidden_res + order.take(result_sum).astype(jnp.float32)).astype(jnp.bfloat16)
    attn_gain_sum, mlp_gain_sum = gains.held[0], gains.held[1]
    return (
        result,
        input_grad,
        attn_gain_sum,
        down_query_sum,
        up_query_sum,
        pair_weight_sum,
        out_sum,
        mlp_gain_sum,
        gate_sum,
        up_sum,
        down_sum,
    )


def solution(mesh):
    return jax.shard_map(
        shards,
        mesh=mesh,
        in_specs=(
            P(("dp", "mp"), None),
            P(),
            P(),
            P(None, "mp"),
            P(),
            P("mp", None),
            P(),
            P(None, "mp"),
            P(None, "mp"),
            P("mp", None),
            P(("dp", "mp"), None),
        ),
        out_specs=(
            P(("dp", "mp"), None),
            P(("dp", "mp"), None),
            P("mp"),
            P("mp", None),
            P(None, "mp"),
            P("mp", None),
            P("mp", None),
            P("mp"),
            P(None, "mp"),
            P(None, "mp"),
            P("mp", None),
        ),
        check_vma=False,
    )
```

```python
import functools

import jax
import jax.numpy as jnp
from jax import lax
from jax.experimental import pallas as pl
from jax.experimental.pallas import tpu as pltpu
from jax.sharding import PartitionSpec as P

HEAD_DIM = 256
EPS = 1e-06
SHORT_PART = 128
LONG_PART = 512
BLOCK = SHORT_PART + LONG_PART
LOG2E = 1.4426950408889634
FREE = pl.CostEstimate(flops=0, bytes_accessed=0, transcendentals=0)


def dotf(left, right):
    return jnp.dot(left, right, preferred_element_type=jnp.float32)


def turned_bits(value, count):
    return sum(((value >> b) & 1) << (count - 1 - b) for b in range(count))


def bits_of(count):
    return max(count.bit_length() - 1, 0)


def chunks_of(heads):
    short = [(0, heads * SHORT_PART)]
    long = [(heads * SHORT_PART + h * LONG_PART, LONG_PART) for h in range(heads)]
    return ((0, SHORT_PART, short), (SHORT_PART, LONG_PART, long))


def spread(heads, head_dim, source, turned):
    for h in range(heads):
        cols = slice(h * head_dim, (h + 1) * head_dim)
        turned[:, h * SHORT_PART : (h + 1) * SHORT_PART] = source[:SHORT_PART, cols].T
        first = heads * SHORT_PART + h * LONG_PART
        turned[:, first : first + LONG_PART] = source[SHORT_PART:, cols].T


def visible_in(extent, width):
    key_pos = lax.broadcasted_iota(jnp.int32, (extent, width), 0)
    query_pos = lax.broadcasted_iota(jnp.int32, (extent, width), 1) & (extent - 1)
    return key_pos <= query_pos


def block_copies(own, sources, all_keys, all_values, sems):
    copies = []
    for kind, (parts, target) in enumerate(((sources[:4], all_keys), (sources[4:], all_values))):
        held = parts[0].shape[0] // BLOCK
        bits = bits_of(2 * held)
        for place, part in enumerate(parts):
            for i in range(held):
                relative = place % 2 * held + i
                if kind == 1:
                    relative = turned_bits(relative, bits)
                index = own ^ (2 * relative + place // 2)
                first = pl.multiple_of(index * BLOCK, BLOCK)
                copies.append(
                    pltpu.make_async_copy(
                        part.at[pl.ds(i * BLOCK, BLOCK), :],
                        target.at[pl.ds(first, BLOCK), :],
                        sems.at[len(copies)],
                    )
                )
    return copies


def forward_kernel(
    heads, head_dim, group, query, *refs
):
    sources, (out, kept, logs, turned, maxima, totals, all_keys, all_values, sems) = (
        refs[:8],
        refs[8:],
    )
    factor = head_dim ** (-0.5) * LOG2E
    own = group[0]
    copies = block_copies(own, sources, all_keys, all_values, sems)
    for copy in copies:
        copy.start()
    spread(heads, head_dim, query, turned)
    kept[...] = jnp.zeros_like(kept)
    maxima[...] = jnp.full_like(maxima, -jnp.inf)
    totals[...] = jnp.zeros_like(totals)
    for copy in copies:
        copy.wait()

    def one_block(index, masked):
        for offset, extent, chunks in chunks_of(heads):
            first = pl.multiple_of(index * BLOCK + offset, SHORT_PART)
            keys = all_keys[pl.ds(first, extent), :]
            values = all_values[pl.ds(first, extent), :].T
            for column, width in chunks:
                at = slice(column, column + width)
                scores = dotf(keys, turned[:, at]) * factor
                if masked:
                    scores = jnp.where(visible_in(extent, width), scores, -jnp.inf)
                old = maxima[:, at]
                new = jnp.maximum(old, jnp.max(scores, axis=0, keepdims=True))
                rescale = jnp.exp2(old - new)
                weights = jnp.exp2(scores - new)
                maxima[:, at] = new
                totals[:, at] = totals[:, at] * rescale + jnp.sum(weights, axis=0, keepdims=True)
                kept[:, at] = kept[:, at] * rescale + dotf(values, weights.astype(jnp.bfloat16))

    def step(index, carry):
        one_block(index, False)
        return carry

    lax.fori_loop(0, own, step, 0)
    one_block(own, True)
    logs[...] = maxima[...] + jnp.log2(totals[...])
    for h in range(heads):
        cols = slice(h * head_dim, (h + 1) * head_dim)
        for rows, first, width in (
            (slice(0, SHORT_PART), h * SHORT_PART, SHORT_PART),
            (slice(SHORT_PART, BLOCK), heads * SHORT_PART + h * LONG_PART, LONG_PART),
        ):
            at = slice(first, first + width)
            exact = kept[:, at] * (1.0 / totals[:, at])
            kept[:, at] = exact
            out[rows, cols] = exact.T.astype(jnp.bfloat16)


def backward_kernel(heads, head_dim, group, query, grad, kept, logs, *refs):
    sources = refs[:8]
    query_grad, key_grad, value_grad = refs[8:11]
    turned, grad_turned, total, delta, short_query, short_grad = refs[11:17]
    all_keys, all_values, sems = refs[17:]
    scale = head_dim ** (-0.5)
    factor = scale * LOG2E
    own = group[0]
    count = all_keys.shape[0] // BLOCK
    bits = bits_of(count) - 1
    copies = block_copies(own, sources, all_keys, all_values, sems)
    for copy in copies:
        copy.start()
    spread(heads, head_dim, query, turned)
    spread(heads, head_dim, grad, grad_turned)
    for h in range(heads):
        cols = slice(h * head_dim, (h + 1) * head_dim)
        rows = slice(h * SHORT_PART, (h + 1) * SHORT_PART)
        short_query[rows, :] = query[:SHORT_PART, cols]
        short_grad[rows, :] = grad[:SHORT_PART, cols]
    delta[...] = jnp.sum(grad_turned[...].astype(jnp.float32) * kept[...], axis=0, keepdims=True)
    total[...] = jnp.zeros_like(total)
    for copy in copies:
        copy.wait()

    def places(index):
        relative = index ^ own
        core, rest = relative & 1, relative >> 1
        key_place = core * (count // 2) + turned_bits(rest, bits)
        return key_place * BLOCK, (core * (count // 2) + rest) * BLOCK

    def one_block(index, masked):
        key_first, value_first = places(index)
        for offset, extent, chunks in chunks_of(heads):
            first = pl.multiple_of(index * BLOCK + offset, SHORT_PART)
            keys = all_keys[pl.ds(first, extent), :]
            values = all_values[pl.ds(first, extent), :]
            keys_turned = keys.T
            key_sum = None
            value_sum = None
            for h, (column, width) in enumerate(chunks):
                at = slice(column, column + width)
                if offset == 0:
                    rows_query, rows_grad = short_query[...], short_grad[...]
                else:
                    cols = slice(h * head_dim, (h + 1) * head_dim)
                    rows_query, rows_grad = query[SHORT_PART:, cols], grad[SHORT_PART:, cols]
                scores = dotf(keys, turned[:, at]) * factor
                chance = jnp.exp2(scores - logs[:, at])
                if masked:
                    chance = jnp.where(visible_in(extent, width), chance, 0.0)
                chance_grad = dotf(values, grad_turned[:, at])
                score_low = (chance * (chance_grad - delta[:, at])).astype(jnp.bfloat16)
                key_part = dotf(score_low, rows_query)
                value_part = dotf(chance.astype(jnp.bfloat16), rows_grad)
                key_sum = key_part if key_sum is None else key_sum + key_part
                value_sum = value_part if value_sum is None else value_sum + value_part
                total[:, at] += dotf(keys_turned, score_low)
            key_rows = pl.ds(pl.multiple_of(key_first + offset, SHORT_PART), extent)
            value_rows = pl.ds(pl.multiple_of(value_first + offset, SHORT_PART), extent)
            key_grad[key_rows, :] = (key_sum * scale).astype(jnp.bfloat16)
            value_grad[value_rows, :] = value_sum.astype(jnp.bfloat16)

    def step(index, carry):
        one_block(index, False)
        return carry

    def clear(index, carry):
        nothing = jnp.zeros((BLOCK, head_dim), jnp.bfloat16)
        key_first, value_first = places(index)
        key_grad[pl.ds(pl.multiple_of(key_first, SHORT_PART), BLOCK), :] = nothing
        value_grad[pl.ds(pl.multiple_of(value_first, SHORT_PART), BLOCK), :] = nothing
        return carry

    lax.fori_loop(0, own, step, 0)
    one_block(own, True)
    lax.fori_loop(own + 1, count, clear, 0)
    for h in range(heads):
        cols = slice(h * head_dim, (h + 1) * head_dim)
        for rows, first, width in (
            (slice(0, SHORT_PART), h * SHORT_PART, SHORT_PART),
            (slice(SHORT_PART, BLOCK), heads * SHORT_PART + h * LONG_PART, LONG_PART),
        ):
            query_grad[rows, cols] = (total[:, first : first + width] * scale).T.astype(jnp.bfloat16)


def in_vmem(count):
    return [pl.BlockSpec(memory_space=pltpu.VMEM)] * count


def gathered_scratch(sources, head_dim):
    rows = sum(part.shape[0] for part in sources[:4])
    return [
        pltpu.VMEM((rows, head_dim), jnp.bfloat16),
        pltpu.VMEM((rows, head_dim), jnp.bfloat16),
        pltpu.SemaphoreType.DMA((2 * rows // BLOCK,)),
    ], rows


def attention_forward(group, query, sources, heads, head_dim):
    columns = heads * BLOCK
    scratch, rows = gathered_scratch(sources, head_dim)
    return pl.pallas_call(
        functools.partial(forward_kernel, heads, head_dim),
        out_shape=(
            jax.ShapeDtypeStruct(query.shape, jnp.bfloat16),
            jax.ShapeDtypeStruct((head_dim, columns), jnp.float32),
            jax.ShapeDtypeStruct((1, columns), jnp.float32),
        ),
        in_specs=[pl.BlockSpec(memory_space=pltpu.SMEM)]
        + in_vmem(1)
        + [pl.BlockSpec(memory_space=pl.ANY)] * 8,
        out_specs=tuple(in_vmem(3)),
        scratch_shapes=[
            pltpu.VMEM((head_dim, columns), jnp.bfloat16),
            pltpu.VMEM((1, columns), jnp.float32),
            pltpu.VMEM((1, columns), jnp.float32),
        ]
        + scratch,
        compiler_params=pltpu.CompilerParams(vmem_limit_bytes=50 << 20),
        cost_estimate=pl.CostEstimate(flops=2 * columns * rows * head_dim * 2, bytes_accessed=4 * rows * head_dim, transcendentals=0),
        name="attention_forward",
    )(group, query, *sources)


def attention_backward(group, query, grad, sources, kept, logs, heads, head_dim):
    columns = heads * BLOCK
    scratch, rows = gathered_scratch(sources, head_dim)
    return pl.pallas_call(
        functools.partial(backward_kernel, heads, head_dim),
        out_shape=(
            jax.ShapeDtypeStruct(query.shape, jnp.bfloat16),
            jax.ShapeDtypeStruct((rows, head_dim), jnp.bfloat16),
            jax.ShapeDtypeStruct((rows, head_dim), jnp.bfloat16),
        ),
        in_specs=[pl.BlockSpec(memory_space=pltpu.SMEM)]
        + in_vmem(4)
        + [pl.BlockSpec(memory_space=pl.ANY)] * 8,
        out_specs=tuple(in_vmem(3)),
        scratch_shapes=[
            pltpu.VMEM((head_dim, columns), jnp.bfloat16),
            pltpu.VMEM((head_dim, columns), jnp.bfloat16),
            pltpu.VMEM((head_dim, columns), jnp.float32),
            pltpu.VMEM((1, columns), jnp.float32),
            pltpu.VMEM((heads * SHORT_PART, head_dim), jnp.bfloat16),
            pltpu.VMEM((heads * SHORT_PART, head_dim), jnp.bfloat16),
        ]
        + scratch,
        compiler_params=pltpu.CompilerParams(vmem_limit_bytes=56 << 20),
        cost_estimate=pl.CostEstimate(flops=2 * columns * rows * head_dim * 2, bytes_accessed=4 * rows * head_dim, transcendentals=0),
        name="attention_backward",
    )(group, query, grad, kept, logs, *sources)


def normalize(rows, gain):
    return rows * lax.rsqrt(jnp.mean(rows * rows, axis=-1, keepdims=True) + EPS) * gain


def gated(gate_in, up_in):
    return jax.nn.silu(gate_in) * up_in


def after(value, *others):
    return lax.optimization_barrier((value,) + others)[0]


class Order:
    def __init__(self):
        self.last = ()

    def take(self, *values):
        out = lax.optimization_barrier(values + self.last)[: len(values)]
        return out if len(values) > 1 else out[0]

    def mark(self, *values):
        self.last = tuple(jax.tree.leaves(values))


def add_low(left, right):
    return (left.astype(jnp.float32) + right.astype(jnp.float32)).astype(jnp.bfloat16)


def plus_kernel(held, got, *outs):
    value = held[...].astype(jnp.float32) + got[...].astype(jnp.float32)
    if len(outs) == 1:
        outs[0][...] = value.astype(jnp.bfloat16)
        return
    half = pl.num_programs(0) // 2

    @pl.when(pl.program_id(0) < half)
    def _():
        outs[0][...] = value.astype(jnp.bfloat16)

    @pl.when(pl.program_id(0) >= half)
    def _():
        outs[1][...] = value.astype(jnp.bfloat16)


def plus(held, got, halves):
    rows, width = held.shape
    steps = 4 if rows % 64 == 0 else 2
    block = (rows // steps, width)
    if halves:
        half = steps // 2
        source = lambda i: (lax.rem(i + half, steps), 0)
        out_specs = [
            pl.BlockSpec(block, lambda i: (jnp.minimum(i, half - 1), 0)),
            pl.BlockSpec(block, lambda i: (jnp.maximum(i - half, 0), 0)),
        ]
        out_shape = [jax.ShapeDtypeStruct((rows // 2, width), jnp.bfloat16)] * 2
    else:
        source = lambda i: (i, 0)
        out_specs = [pl.BlockSpec(block, source)]
        out_shape = [jax.ShapeDtypeStruct((rows, width), jnp.bfloat16)]
    out = pl.pallas_call(
        plus_kernel,
        grid=(steps,),
        in_specs=[pl.BlockSpec(block, source)] * 2,
        out_specs=out_specs,
        out_shape=out_shape,
        compiler_params=pltpu.CompilerParams(vmem_limit_bytes=24 << 20),
        cost_estimate=FREE,
        name="plus",
    )(held, got)
    return out if halves else out[0]


def join_kernel(axis, *refs):
    *parts, out, inside, in_sems, out_sems = refs
    arriving, leaving, first = [], [], 0
    for i, part in enumerate(parts):
        extent = part.shape[axis]
        cut = (pl.ds(first, extent), slice(None)) if axis == 0 else (slice(None), pl.ds(first, extent))
        arriving.append(pltpu.make_async_copy(part, inside.at[cut], in_sems.at[i]))
        leaving.append(pltpu.make_async_copy(inside.at[cut], out.at[cut], out_sems.at[i]))
        first += extent
    for copy in arriving:
        copy.start()
    for arrived, left in zip(arriving, leaving):
        arrived.wait()
        left.start()
    for copy in leaving:
        copy.wait()


def join(parts, axis):
    shape = list(parts[0].shape)
    shape[axis] = sum(part.shape[axis] for part in parts)
    anywhere = pl.BlockSpec(memory_space=pl.ANY)
    return pl.pallas_call(
        functools.partial(join_kernel, axis),
        in_specs=[anywhere] * len(parts),
        out_specs=anywhere,
        out_shape=jax.ShapeDtypeStruct(tuple(shape), parts[0].dtype),
        scratch_shapes=[
            pltpu.VMEM(tuple(shape), parts[0].dtype),
            pltpu.SemaphoreType.DMA((len(parts),)),
            pltpu.SemaphoreType.DMA((len(parts),)),
        ],
        compiler_params=pltpu.CompilerParams(vmem_limit_bytes=24 << 20),
        cost_estimate=FREE,
        name="join",
    )(*parts)


def rows_kernel(contract, count, places, *refs):
    parts, (weight, out) = refs[:count], refs[count:]
    for i, part in enumerate(parts):
        rows = part.shape[contract[0] ^ 1]
        out[pl.ds(pl.multiple_of(places[i] * rows, 16), rows), :] = lax.dot_general(
            part[...],
            weight[...],
            (((contract[0],), (contract[1],)), ((), ())),
            preferred_element_type=jnp.float32,
        ).astype(jnp.bfloat16)


def rows_product(parts, weight, contract, name, places=None):
    count = len(parts)
    if places is None:
        places = jnp.arange(count, dtype=jnp.int32)
    rows, width = parts[0].shape[contract[0] ^ 1], weight.shape[contract[1] ^ 1]
    return pl.pallas_call(
        functools.partial(rows_kernel, contract, count),
        in_specs=[pl.BlockSpec(memory_space=pltpu.SMEM)] + in_vmem(count + 1),
        out_specs=pl.BlockSpec(memory_space=pltpu.VMEM),
        out_shape=jax.ShapeDtypeStruct((rows * count, width), jnp.bfloat16),
        compiler_params=pltpu.CompilerParams(vmem_limit_bytes=40 << 20),
        cost_estimate=FREE,
        name=name,
    )(places, *parts, weight)


def ring_of(count):
    return [0] + list(range(1, count, 2)) + list(range(2, count, 2))[::-1]


def ring_place(back):
    ring = ring_of(lax.axis_size("mp"))
    count = len(ring)
    table = [ring[(ring.index(i) - back) % count] for i in range(count)]
    return jnp.asarray(table, jnp.int32)[lax.axis_index("mp")]


def ring_pass(array):
    ring = ring_of(lax.axis_size("mp"))
    pairs = [(ring[i], ring[(i + 1) % len(ring)]) for i in range(len(ring))]
    return lax.ppermute(array, "mp", pairs)


def put_rows(whole_rows, rows, place):
    return lax.dynamic_update_slice_in_dim(whole_rows, rows, place * rows.shape[0], 0)


def take_rows(whole_rows, place):
    count = whole_rows.shape[0] // lax.axis_size("mp")
    return lax.dynamic_slice_in_dim(whole_rows, place * count, count, 0)


def ring_rows(parts):
    out = jnp.zeros((parts[0].shape[0] * len(parts),) + parts[0].shape[1:], parts[0].dtype)
    for step, rows in enumerate(parts):
        out = put_rows(out, rows, ring_place(step))
    return out


class RingGather:
    def __init__(self, rows):
        self.parts = [rows]
        self.start()

    def start(self):
        if len(self.parts) < lax.axis_size("mp"):
            self.flying = ring_pass(self.parts[-1])

    def step(self, order):
        if len(self.parts) < lax.axis_size("mp"):
            rows = order.take(self.flying)
            order.mark(rows)
            self.parts.append(rows)
            self.start()

    def steps_left(self):
        return lax.axis_size("mp") - len(self.parts)

    def rows(self):
        return ring_rows(self.parts)


class RingScatter:
    def __init__(self, part):
        self.part, self.steps = part, 1
        self.held = part(1)
        self.flying = ring_pass(self.held)

    def step(self, order):
        if self.steps_left():
            self.steps += 1
            got, own = order.take(self.flying, self.part(self.steps % lax.axis_size("mp")))
            self.held = add_low(own, got)
            order.mark(self.held)
            if self.steps_left():
                self.flying = ring_pass(self.held)

    def steps_left(self):
        return lax.axis_size("mp") - self.steps


def trade(array, bit):
    count = lax.axis_size("dp")
    return lax.ppermute(array, "dp", [(i, i ^ (1 << bit)) for i in range(count)])


def bit_here(bit):
    return (lax.axis_index("dp") >> bit) & 1


def orders():
    rest = list(range(1, bits_of(lax.axis_size("dp"))))
    return [0] + rest, [0] + rest[::-1]


class Lane:
    def __init__(self, partial, order, axis):
        self.bits, self.axis = order, axis
        self.steps = [("halve", bit) for bit in order]
        self.steps += [("double", bit) for bit in order[:0:-1]] + [("core", 0)]
        self.cut_and_start(lambda which, half: self.cut(partial, which, half), partial.shape[axis])

    def cut(self, array, which, half):
        return lax.dynamic_slice_in_dim(array, which * half, half, self.axis)

    def cut_and_start(self, part, extent):
        bit = self.steps[0][1]
        mine = bit_here(bit)
        self.sent, self.held = part(1 - mine, extent // 2), part(mine, extent // 2)
        self.flying = trade(self.sent, bit)

    def step(self, order):
        kind, _ = self.steps.pop(0)
        got, held = order.take(self.flying, self.held)
        if not self.steps:
            self.pieces = [held, got]
            order.mark(self.pieces)
            return
        following, bit = self.steps[0]
        if kind == "halve" and following == "halve":
            self.cut_and_start(
                lambda which, half: add_low(self.cut(held, which, half), self.cut(got, which, half)),
                held.shape[self.axis],
            )
        else:
            if kind == "halve":
                self.held = add_low(held, got)
            else:
                self.held = jnp.concatenate([held, got], axis=self.axis)
            self.sent = self.held
            self.flying = trade(self.sent, bit)
        order.mark(self.sent, self.held)

    def places(self):
        own = jnp.int32(0)
        for bit in self.bits[1:]:
            own = own * 2 + bit_here(bit)
        count = 1 << (len(self.bits) - 1)
        relative = jnp.arange(count, dtype=jnp.int32) ^ own
        core = bit_here(0)
        return jnp.concatenate([core * count + relative, (1 - core) * count + relative])


def kept_first(first_bit_first):
    count = lax.axis_size("dp")
    bits = bits_of(count) - 1
    order = [turned_bits(i, bits) if first_bit_first else i for i in range(count // 2)]
    own = lax.axis_index("dp").astype(jnp.int32)
    relative = jnp.asarray([2 * i for i in order] + [2 * i + 1 for i in order], jnp.int32)
    return relative ^ own


def product_kernel(groups, split, places, *refs):
    inputs, at = [], 0
    for parts, beside in groups:
        inputs.append((refs[at : at + parts], refs[at + parts : at + parts * (1 + beside)]))
        at += parts * (1 + beside)
    scratch = refs[len(refs) - 2 * len(groups) :]
    values = []
    for g, ((lefts, rights), (parts, _)) in enumerate(zip(inputs, groups)):
        left, right = scratch[2 * g : 2 * g + 2]
        count, width = rights[0].shape

        @pl.when(pl.program_id(0) == 0)
        def _(rights=rights, right=right, count=count, width=width, parts=parts):
            for i, part in enumerate(rights):
                row, column = i % parts * count, i // parts * width
                right[row : row + count, column : column + width] = part[...]

        for i, part in enumerate(lefts):
            left[i * count : (i + 1) * count, :] = part[...]
        values.append(
            lax.dot_general(
                left[...], right[...], (((0,), (0,)), ((), ())), preferred_element_type=jnp.float32
            ).astype(jnp.bfloat16)
        )
    first = 0
    for value in values:
        cut = (slice(None), slice(first, first + value.shape[1]))
        first += value.shape[1]
        if split is None:
            refs[at][cut] = value
            continue
        other, sent, held = refs[at : at + 3]
        total = (value.astype(jnp.float32) + other[cut].astype(jnp.float32)).astype(jnp.bfloat16)

        @pl.when(pl.program_id(0) < split)
        def _(total=total, cut=cut):
            sent[cut] = total

        @pl.when(pl.program_id(0) >= split)
        def _(total=total, cut=cut):
            held[cut] = total


def product_blocks(products, places, rows, name, other=None):
    blocks = places.shape[0]
    if other is None:
        split, order, inputs = None, lambda i: i, ()
    else:
        split, order, inputs = blocks // 2, lambda i: lax.rem(i + blocks // 2, blocks), (other,)
    arrays, in_specs, scratch, groups, total = [], [], [], [], 0
    for lefts, rights in products:
        tokens = lefts[0].shape[0]
        moving = pl.BlockSpec((tokens, rows), lambda i, places: (0, places[order(i)]))
        arrays += list(lefts)
        in_specs += [moving] * len(lefts)
        width = sum(right[0].shape[1] for right in rights)
        for right in rights:
            arrays += list(right)
            in_specs += [pl.BlockSpec(right[0].shape, lambda i, places: (0, 0))] * len(right)
        scratch += [
            pltpu.VMEM((tokens * len(lefts), rows), jnp.bfloat16),
            pltpu.VMEM((tokens * len(lefts), width), jnp.bfloat16),
        ]
        groups.append((len(lefts), len(rights)))
        total += width
    block = (rows, total)
    if other is None:
        out_specs = pl.BlockSpec(block, lambda i, places: (i, 0))
        out_shape = jax.ShapeDtypeStruct((blocks * rows, total), jnp.bfloat16)
    else:
        in_specs.append(pl.BlockSpec(block, lambda i, places: (order(i), 0)))
        out_specs = [
            pl.BlockSpec(block, lambda i, places: (jnp.minimum(i, split - 1), 0)),
            pl.BlockSpec(block, lambda i, places: (jnp.maximum(i - split, 0), 0)),
        ]
        out_shape = [jax.ShapeDtypeStruct((split * rows, total), jnp.bfloat16)] * 2
    return pl.pallas_call(
        functools.partial(product_kernel, tuple(groups), split),
        grid_spec=pltpu.PrefetchScalarGridSpec(
            num_scalar_prefetch=1,
            grid=(blocks,),
            in_specs=in_specs,
            out_specs=out_specs,
            scratch_shapes=scratch,
        ),
        out_shape=out_shape,
        compiler_params=pltpu.CompilerParams(vmem_limit_bytes=48 << 20),
        cost_estimate=FREE,
        name=name,
    )(places, *arrays, *inputs)


class BlockLane:
    def __init__(self, order, products, bits, name, first_row=0, rows=None):
        self.bits, self.name, self.products = list(bits), name, products
        self.rows = rows or products[0][0][0].shape[1] // lax.axis_size("dp")
        self.first_row = first_row
        self.places = kept_first(bits[1] == 1)
        self.table = self.places + first_row // self.rows
        half = self.places.shape[0] // 2
        self.sent = product_blocks(self.taken(order), self.table[half:], self.rows, name + "_sent")
        order.mark(self.sent)
        self.flying = trade(self.sent, 0)
        self.steps = ["product"] + ["halve"] * (len(bits) - 1) + ["double"] * (len(bits) - 1)
        self.steps += ["core"]

    def taken(self, order):
        leaves, shape = jax.tree.flatten(self.products)
        return jax.tree.unflatten(shape, order.take(*leaves))

    def step(self, order):
        kind = self.steps.pop(0)
        if kind == "product":
            self.bits.pop(0)
            got = order.take(self.flying)
            half = self.places.shape[0] // 2
            self.sent, self.held = product_blocks(
                self.taken(order), self.table[:half], self.rows, self.name + "_kept", got
            )
            self.done_bits = []
            self.flying = trade(self.sent, self.bits[0])
            order.mark(self.sent, self.held)
            return
        if kind == "both":
            near, far, own = order.take(*self.flying, self.held)
            self.held = self.sent = (own, near, far)
            self.flying = trade(near, self.done_bits[0])
            order.mark(self.held)
            return
        if kind == "rest":
            self.held = self.sent = join(order.take(*self.held, self.flying), 0)
            self.flying = trade(self.held, 0)
            order.mark(self.held)
            return
        got, held = order.take(self.flying, self.held)
        if kind == "core":
            self.pieces = [held, got]
            order.mark(self.pieces)
            return
        if kind == "halve":
            self.done_bits.append(self.bits.pop(0))
            if self.bits:
                self.sent, self.held = plus(held, got, True)
                self.flying = trade(self.sent, self.bits[0])
                order.mark(self.sent, self.held)
                return
            held = plus(held, got, False)
            if len(self.done_bits) == 2:
                self.steps = ["both", "rest", "core"]
                self.held = self.sent = held
                self.flying = (trade(held, self.done_bits[1]), trade(held, self.done_bits[0]))
                order.mark(held)
                return
        else:
            self.done_bits.pop()
            held = join([held, got], 0)
        self.held = self.sent = held
        self.flying = trade(held, self.done_bits[-1] if self.done_bits else 0)
        order.mark(self.held)


def block_lanes(order, products, name):
    first, second = orders()
    total = products[0][0][0].shape[1]
    rows = total // lax.axis_size("dp")
    if rows % 256:
        return [BlockLane(order, products, first, name)]
    return [
        BlockLane(order, products, first, name + "_low", 0, rows // 2),
        BlockLane(order, products, second, name + "_high", total // 2, rows // 2),
    ]


def unfold_kernel(firsts, pieces, targets, places, *refs):
    sets = 2 * len(firsts)
    sources, outs = refs[:sets], refs[sets : sets + len(targets)]
    landed = refs[sets + len(targets)]
    raised = refs[sets + len(targets) + 1 : -2]
    in_sems, out_sems = refs[-2:]
    rows = landed.shape[1]
    slots = raised[0].shape[0]
    total = sets * pieces

    def fetch(i):
        source = sources[i // pieces]
        return pltpu.make_async_copy(
            source.at[pl.ds(i % pieces * rows, rows), :], landed.at[i], in_sems.at[i]
        )

    def store(i):
        along = pl.multiple_of(firsts[i // (2 * pieces)] + places[i] * rows, rows)
        copies = []
        for k, ((_, turned), out) in enumerate(zip(targets, outs)):
            window = out.at[:, pl.ds(along, rows)] if turned else out.at[pl.ds(along, rows), :]
            copies.append(
                pltpu.make_async_copy(
                    raised[k].at[i % slots], window, out_sems.at[i * len(targets) + k]
                )
            )
        return copies

    for i in range(total):
        fetch(i).start()
    for i in range(total):
        fetch(i).wait()
        if i >= slots:
            for copy in store(i - slots):
                copy.wait()
        first = 0
        for k, (width, turned) in enumerate(targets):
            value = landed[i, :, first : first + width].astype(jnp.float32)
            raised[k][i % slots] = value.T if turned else value
            first += width
        for copy in store(i):
            copy.start()
    for i in range(max(total - slots, 0), total):
        for copy in store(i):
            copy.wait()


def unfold(lanes, targets, name):
    sets = [piece for lane in lanes for piece in lane.pieces]
    rows, width = lanes[0].rows, sets[0].shape[1]
    pieces = sets[0].shape[0] // rows
    total, slots = len(sets) * pieces, 4
    height = total * rows
    anywhere = pl.BlockSpec(memory_space=pl.ANY)
    return pl.pallas_call(
        functools.partial(
            unfold_kernel, tuple(lane.first_row for lane in lanes), pieces, tuple(targets)
        ),
        in_specs=[pl.BlockSpec(memory_space=pltpu.SMEM)] + [anywhere] * len(sets),
        out_specs=[anywhere] * len(targets),
        out_shape=[
            jax.ShapeDtypeStruct((w, height) if turned else (height, w), jnp.float32)
            for w, turned in targets
        ],
        scratch_shapes=[pltpu.VMEM((total, rows, width), jnp.bfloat16)]
        + [
            pltpu.VMEM((slots, w, rows) if turned else (slots, rows, w), jnp.float32)
            for w, turned in targets
        ]
        + [
            pltpu.SemaphoreType.DMA((total,)),
            pltpu.SemaphoreType.DMA((total * len(targets),)),
        ],
        compiler_params=pltpu.CompilerParams(vmem_limit_bytes=48 << 20),
        cost_estimate=FREE,
        name=name,
    )(jnp.concatenate([lane.places for lane in lanes]), *sets)


def lay_kernel(lanes, sets, pieces, axis, cuts, places, *refs):
    outs = refs[lanes * sets : -4]
    landed, raised, in_sems, out_sems = refs[-4:]
    rows, columns = landed.shape[1:]
    slots = raised.shape[0]
    total = lanes * sets * pieces

    def window(ref, along, across, extent):
        if axis == 0:
            return ref.at[pl.ds(along, rows), pl.ds(across, extent)]
        return ref.at[pl.ds(across, extent), pl.ds(along, columns)]

    def fetch(i):
        first = i % pieces * (rows, columns)[axis]
        source = refs[i // pieces]
        across = source.shape[1 - axis]
        return pltpu.make_async_copy(
            window(source, first, 0, across), window(landed.at[i], 0, 0, across), in_sems.at[i]
        )

    def store(i):
        along = pl.multiple_of(places[i] * (rows, columns)[axis], (rows, columns)[axis])
        return [
            pltpu.make_async_copy(
                window(raised.at[i % slots], 0, first, extent),
                window(outs[out], along, target, extent),
                out_sems.at[2 * i + k],
            )
            for k, (out, first, extent, target) in enumerate(cuts[i // (sets * pieces)])
        ]

    for i in range(total):
        fetch(i).start()
    for i in range(total):
        fetch(i).wait()
        if i >= slots:
            for copy in store(i - slots):
                copy.wait()
        extent = refs[i // pieces].shape[1 - axis]
        filled = (slice(None), slice(extent)) if axis == 0 else (slice(extent), slice(None))
        raised[(i % slots, *filled)] = landed[(i, *filled)].astype(jnp.float32)
        for copy in store(i):
            copy.start()
    for i in range(max(total - slots, 0), total):
        for copy in store(i):
            copy.wait()


def lay_out(lanes, cuts, shapes, name):
    sets = [piece for lane in lanes for piece in lane.pieces]
    axis = lanes[0].axis
    places = jnp.concatenate([lane.places() for lane in lanes])
    pieces = places.shape[0] // len(sets)
    block = [max(piece.shape[d] for piece in sets) for d in (0, 1)]
    block[axis] //= pieces
    total = len(sets) * pieces
    anywhere = pl.BlockSpec(memory_space=pl.ANY)
    return pl.pallas_call(
        functools.partial(lay_kernel, len(lanes), len(lanes[0].pieces), pieces, axis, cuts),
        in_specs=[pl.BlockSpec(memory_space=pltpu.SMEM)] + [anywhere] * len(sets),
        out_specs=[anywhere] * len(shapes),
        out_shape=[jax.ShapeDtypeStruct(shape, jnp.float32) for shape in shapes],
        scratch_shapes=[
            pltpu.VMEM((total, *block), jnp.bfloat16),
            pltpu.VMEM((min(total, 6), *block), jnp.float32),
            pltpu.SemaphoreType.DMA((total,)),
            pltpu.SemaphoreType.DMA((2 * total,)),
        ],
        compiler_params=pltpu.CompilerParams(vmem_limit_bytes=44 << 20),
        cost_estimate=FREE,
        name=name,
    )(places, *sets)


def own_share(array):
    share = array.shape[0] // lax.axis_size("mp")
    return lax.dynamic_slice_in_dim(array, lax.axis_index("mp") * share, share)


class BlockSum:
    def __init__(self, blocks, order):
        self.bits = list(order)
        half = blocks.shape[0] // 2
        self.held, self.sent = blocks[:half], blocks[half:]
        self.flying = trade(self.sent, self.bits[0])

    def step(self, order):
        self.bits.pop(0)
        got, held = order.take(self.flying, self.held)
        if self.bits:
            self.sent, self.held = plus(held, got, True)
            self.flying = trade(self.sent, self.bits[0])
        else:
            self.held = self.sent = plus(held, got, False)
        order.mark(self.sent, self.held)


class BlockGather:
    def __init__(self, rows, order):
        self.bits, self.held = list(order), rows
        self.flying = trade(rows, self.bits[0])

    def step(self, order):
        if not self.bits:
            got = order.take(*self.flying)
            order.mark(got)
            self.parts = self.held + list(got)
            return
        self.bits.pop(0)
        got, held = order.take(self.flying, self.held)
        if self.bits:
            self.held = jnp.concatenate([held, got], axis=0)
            self.flying = trade(self.held, self.bits[0])
        else:
            self.held = [held, got]
            self.flying = [trade(part, 0) for part in self.held]
        order.mark(self.held)


class SmallSum:
    def __init__(self, array, axis):
        self.axis, self.held = axis, array
        self.bits = list(range(bits_of(lax.axis_size(axis))))
        self.start()

    def start(self):
        if self.bits:
            count = lax.axis_size(self.axis)
            pairs = [(i, i ^ (1 << self.bits[0])) for i in range(count)]
            self.flying = lax.ppermute(self.held, self.axis, pairs)

    def step(self, order):
        if self.bits:
            self.bits.pop(0)
            got, held = order.take(self.flying, self.held)
            self.held = held + got
            order.mark(self.held)
            self.start()


def column_share(rows):
    ring = ring_of(lax.axis_size("mp"))
    count = len(ring)
    width = rows.shape[1] // count
    parts = []
    for step in range(count):
        part = lax.dynamic_slice_in_dim(rows, ring_place(-step) * width, width, 1)
        pairs = [(ring[i], ring[(i + step) % count]) for i in range(count)]
        parts.append(lax.ppermute(part, "mp", pairs) if step else part)
    return parts


def shards(
    tokens,
    attn_gain,
    query_down,
    query_up,
    key_value,
    attn_out,
    mlp_gain,
    gate_weight,
    up_weight,
    down_weight,
    out_grad,
):
    head_dim = HEAD_DIM
    local_heads = query_up.shape[1] // head_dim
    ranks = lax.axis_size("mp")
    group = lax.axis_index("dp").reshape(1).astype(jnp.int32)
    ring_places = jnp.stack([ring_place(i) for i in range(lax.axis_size("mp"))])
    first, second = orders()

    def rows_of(array):
        return lambda back: take_rows(array, ring_place(back))

    def parts_of(array):
        count = array.shape[0] // ranks
        return lambda back: array[back * count : (back + 1) * count]

    def weight_grad(left, right):
        return jnp.einsum("tk,td->kd", left, right, preferred_element_type=jnp.float32).astype(
            jnp.bfloat16
        )

    def steps(*moving):
        for one in moving:
            one.step(order)

    def finish(*lanes):
        while lanes[0].steps:
            steps(*lanes)

    order = Order()
    inputs = tokens.astype(jnp.float32)
    normal_one = normalize(inputs, attn_gain).astype(jnp.bfloat16)
    pair_local = dotf(normal_one, key_value).astype(jnp.bfloat16)
    order.mark(pair_local)
    pair_ring = RingGather(pair_local)
    latent = dotf(order.take(normal_one), query_down).astype(jnp.bfloat16)
    order.mark(latent)
    latent_ring = RingGather(latent)
    while pair_ring.steps_left() > 1:
        steps(pair_ring, latent_ring)
    steps(pair_ring)
    pair_own = pair_ring.rows()
    order.mark(pair_own)
    keys = BlockGather(pair_own[:, :head_dim], first[1:])
    values = BlockGather(pair_own[:, head_dim:], second[1:])
    while latent_ring.steps_left():
        steps(latent_ring)
    grad_ring = RingGather(order.take(out_grad))
    latent_full = order.take(latent_ring.rows())
    query_full = dotf(latent_full, query_up).astype(jnp.bfloat16)
    order.mark(query_full)
    steps(keys, values, grad_ring)
    while keys.bits:
        steps(keys, values)
    steps(grad_ring, keys, values)
    share_parts = column_share(order.take(normal_one))
    sources = order.take(*keys.parts, *values.parts)
    attended, kept, logs = attention_forward(group, query_full, sources, local_heads, head_dim)
    order.mark(attended)
    share_parts = order.take(*share_parts)
    order.mark(*share_parts)
    steps(grad_ring)
    attn_partial = dotf(order.take(attended), attn_out).astype(jnp.bfloat16)
    order.mark(attn_partial)
    attn_ring = RingScatter(rows_of(attn_partial))
    while grad_ring.steps_left():
        steps(grad_ring)
    grad_ringed = jnp.concatenate(order.take(*grad_ring.parts), axis=0)
    act_grad = jnp.einsum("td,fd->tf", grad_ringed, down_weight, preferred_element_type=jnp.float32)
    normal_share = ring_rows(share_parts)
    order.mark(act_grad, normal_share)
    while attn_ring.steps_left():
        steps(attn_ring)
    hidden_res = inputs + attn_ring.held.astype(jnp.float32)
    normal_two = normalize(hidden_res, mlp_gain).astype(jnp.bfloat16)
    order.mark(normal_two)
    two_ring = RingGather(normal_two)
    act_parts = parts_of(act_grad)
    activated, gate_low, up_low, two_terms = [], [], [], []
    two_sum = None
    for block in range(ranks):
        steps(*([two_ring] if block else []))
        rows = order.take(two_ring.parts[block])
        gate = dotf(rows, gate_weight)
        upward = dotf(rows, up_weight)
        _, gated_pull = jax.vjp(gated, gate, upward)
        gate_grad32, up_grad32 = gated_pull(act_parts(block))
        activated.append(gated(gate, upward).astype(jnp.bfloat16))
        gate_low.append(gate_grad32.astype(jnp.bfloat16))
        up_low.append(up_grad32.astype(jnp.bfloat16))
        two_terms.append(
            (
                jnp.einsum("tf,df->td", gate_low[-1], gate_weight, preferred_element_type=jnp.float32)
                + jnp.einsum("tf,df->td", up_low[-1], up_weight, preferred_element_type=jnp.float32)
            ).astype(jnp.bfloat16)
        )
        order.mark(two_terms[-1], activated[-1])
        if block == 1:
            two_sum = RingScatter(lambda back: two_terms[back])
        elif block > 1:
            steps(two_sum)
    while two_sum.steps_left():
        steps(two_sum)
    normal_two_grad = two_sum.held.astype(jnp.float32)
    _, norm_pull_two = jax.vjp(normalize, hidden_res, mlp_gain)
    resid_from_norm, mlp_gain_part = norm_pull_two(normal_two_grad)
    hidden_grad = out_grad.astype(jnp.float32) + resid_from_norm
    branch = hidden_grad.astype(jnp.bfloat16)
    order.mark(branch)
    branch_ring = RingGather(branch)
    def part_sent(*lanes):
        order.mark([lane.sent for lane in lanes])

    low_parts = []

    def low_part():
        rows = order.take(branch_ring.parts[len(low_parts)])
        low_parts.append(rows_product([rows], attn_out, (1, 1), "attended_low"))
        order.mark(low_parts[-1])

    mlp = block_lanes(
        order,
        [(grad_ring.parts, [activated]), (two_ring.parts, [gate_low, up_low])],
        "mlp_grads",
    )
    steps(branch_ring)
    low_part()
    low_part()
    steps(mlp[0])
    steps(branch_ring)
    low_part()
    steps(*mlp[1:])
    while branch_ring.steps_left():
        steps(branch_ring)
        low_part()
    while len(low_parts) < ranks:
        low_part()
    attended_low = ring_rows(low_parts)
    order.mark(attended_low)
    query_low, key_grads, value_grads = attention_backward(
        group, query_full, order.take(attended_low), sources, kept, logs, local_heads, head_dim
    )
    query_low, key_grads, value_grads = lax.optimization_barrier(
        (query_low, key_grads, value_grads, mlp[0].flying)
    )[:3]
    order.mark(query_low)
    key_sum = BlockSum(order.take(key_grads), first)
    value_sum = BlockSum(order.take(value_grads), second)
    part_sent(key_sum, value_sum)
    steps(*mlp)
    latent_partial = rows_product([order.take(query_low)], query_up, (1, 1), "latent_low")
    order.mark(latent_partial)
    latent_low = lax.psum_scatter(latent_partial, "mp", scatter_dimension=0, tiled=True)
    steps(key_sum, value_sum)
    up_query_part = rows_product([latent_full], order.take(query_low), (0, 0), "query_up_grad")
    out_part = weight_grad(attended, ring_rows(order.take(*branch_ring.parts)))
    order.mark(up_query_part, out_part)
    out_sum, up_query_sum = lax.psum((out_part, up_query_part), "dp")
    steps(key_sum, value_sum)
    steps(*mlp)
    while key_sum.bits:
        steps(key_sum, value_sum)
    pair_partial = join(order.take(key_sum.held, value_sum.held), 1)
    order.mark(pair_partial)
    pair_low_sum = RingScatter(rows_of(pair_partial))
    steps(pair_low_sum)
    latent_low = order.take(latent_low)
    order.mark(latent_low)
    low_full = lax.all_gather(latent_low, "mp", axis=0, tiled=True)
    while pair_low_sum.steps_left():
        steps(pair_low_sum)
    pair_low = pair_low_sum.held
    low_pair_ring = RingGather(pair_low)
    result_partial = rows_product(
        order.take(*activated), down_weight, (1, 0), "result", ring_places
    )
    order.mark(result_partial)
    steps(low_pair_ring)
    steps(*mlp)
    while low_pair_ring.steps_left():
        steps(low_pair_ring)
    pair_weight_part = rows_product(
        [normal_share], order.take(low_pair_ring.rows()), (0, 0), "key_value_grad"
    )
    order.mark(pair_weight_part)
    pair_weight = Lane(order.take(pair_weight_part), first, 0)
    part_sent(pair_weight)
    down_query_part = rows_product(
        [normal_share], order.take(low_full), (0, 0), "query_down_grad"
    )
    order.mark(down_query_part)
    down_query = Lane(order.take(down_query_part), second, 0)
    part_sent(down_query)
    result_sum = lax.psum_scatter(
        after(result_partial, low_full), "mp", scatter_dimension=0, tiled=True
    )
    steps(pair_weight, down_query)
    latent_term = jnp.einsum(
        "tr,dr->td", order.take(latent_low), query_down, preferred_element_type=jnp.float32
    )
    order.mark(latent_term)
    normal_one_grad = latent_term + jnp.einsum(
        "tp,dp->td", order.take(pair_low), key_value, preferred_element_type=jnp.float32
    )
    _, norm_pull_one = jax.vjp(normalize, inputs, attn_gain)
    input_from_norm, attn_gain_part = norm_pull_one(normal_one_grad)
    input_grad = hidden_grad + input_from_norm
    order.mark(input_grad, attn_gain_part)
    attn_gain_sum = SmallSum(order.take(attn_gain_part), "mp")
    mlp_gain_sum = SmallSum(order.take(mlp_gain_part), "mp")
    steps(pair_weight, down_query)
    while attn_gain_sum.bits or mlp_gain_sum.bits:
        steps(attn_gain_sum, mlp_gain_sum)
    gains = jnp.stack([own_share(attn_gain_sum.held), own_share(mlp_gain_sum.held)])
    order.mark(gains)
    steps(pair_weight, down_query)
    gains = SmallSum(order.take(gains), "dp")
    while len(down_query.steps) > 2:
        steps(pair_weight, down_query)
        steps(gains)
    finish(pair_weight, down_query)
    while gains.bits:
        steps(gains)
    cuts = tuple(((i, 0, part.shape[1], 0),) for i, part in enumerate((query_down, key_value)))
    down_query_sum, pair_weight_sum = lay_out(
        [down_query, pair_weight],
        cuts,
        [(normal_share.shape[1], part.shape[1]) for part in (query_down, key_value)],
        "query_down_key_value_laid",
    )
    order.mark(down_query_sum)
    out_sum, up_query_sum = order.take(out_sum, up_query_sum)
    order.mark(out_sum, up_query_sum)
    while len(mlp[0].steps) > 1:
        steps(*mlp)
    out_sum = order.take(out_sum).astype(jnp.float32)
    up_query_sum = up_query_sum.astype(jnp.float32)
    order.mark(out_sum, up_query_sum)
    finish(*mlp)
    down_sum, gate_sum, up_sum = unfold(
        mlp, [(down_weight.shape[0], True)] + [(gate_weight.shape[1], False)] * 2, "mlp_grads_laid"
    )
    order.mark(down_sum)
    result = (hidden_res + order.take(result_sum).astype(jnp.float32)).astype(jnp.bfloat16)
    attn_gain_sum, mlp_gain_sum = gains.held[0], gains.held[1]
    return (
        result,
        input_grad,
        attn_gain_sum,
        down_query_sum,
        up_query_sum,
        pair_weight_sum,
        out_sum,
        mlp_gain_sum,
        gate_sum,
        up_sum,
        down_sum,
    )


def solution(mesh):
    return jax.shard_map(
        shards,
        mesh=mesh,
        in_specs=(
            P(("dp", "mp"), None),
            P(),
            P(),
            P(None, "mp"),
            P(),
            P("mp", None),
            P(),
            P(None, "mp"),
            P(None, "mp"),
            P("mp", None),
            P(("dp", "mp"), None),
        ),
        out_specs=(
            P(("dp", "mp"), None),
            P(("dp", "mp"), None),
            P("mp"),
            P("mp", None),
            P(None, "mp"),
            P("mp", None),
            P("mp", None),
            P("mp"),
            P(None, "mp"),
            P(None, "mp"),
            P("mp", None),
        ),
        check_vma=False,
    )
```

```python
import functools

import jax
import jax.numpy as jnp
from jax import lax
from jax.experimental import pallas as pl
from jax.experimental.pallas import tpu as pltpu
from jax.sharding import PartitionSpec as P

HEAD_DIM = 256
EPS = 1e-06
SHORT_PART = 128
LONG_PART = 512
BLOCK = SHORT_PART + LONG_PART
LOG2E = 1.4426950408889634
FREE = pl.CostEstimate(flops=0, bytes_accessed=0, transcendentals=0)


def dotf(left, right):
    return jnp.dot(left, right, preferred_element_type=jnp.float32)


def turned_bits(value, count):
    return sum(((value >> b) & 1) << (count - 1 - b) for b in range(count))


def bits_of(count):
    return max(count.bit_length() - 1, 0)


def chunks_of(heads):
    short = [(0, heads * SHORT_PART)]
    long = [(heads * SHORT_PART + h * LONG_PART, LONG_PART) for h in range(heads)]
    return ((0, SHORT_PART, short), (SHORT_PART, LONG_PART, long))


def spread(heads, head_dim, source, turned):
    for h in range(heads):
        cols = slice(h * head_dim, (h + 1) * head_dim)
        turned[:, h * SHORT_PART : (h + 1) * SHORT_PART] = source[:SHORT_PART, cols].T
        first = heads * SHORT_PART + h * LONG_PART
        turned[:, first : first + LONG_PART] = source[SHORT_PART:, cols].T


def visible_in(extent, width):
    key_pos = lax.broadcasted_iota(jnp.int32, (extent, width), 0)
    query_pos = lax.broadcasted_iota(jnp.int32, (extent, width), 1) & (extent - 1)
    return key_pos <= query_pos


def block_copies(own, sources, all_keys, all_values, sems):
    copies = []
    for kind, (parts, target) in enumerate(((sources[:4], all_keys), (sources[4:], all_values))):
        held = parts[0].shape[0] // BLOCK
        bits = bits_of(2 * held)
        for place, part in enumerate(parts):
            for i in range(held):
                relative = place % 2 * held + i
                if kind == 1:
                    relative = turned_bits(relative, bits)
                index = own ^ (2 * relative + place // 2)
                first = pl.multiple_of(index * BLOCK, BLOCK)
                copies.append(
                    pltpu.make_async_copy(
                        part.at[pl.ds(i * BLOCK, BLOCK), :],
                        target.at[pl.ds(first, BLOCK), :],
                        sems.at[len(copies)],
                    )
                )
    return copies


def forward_kernel(
    heads, head_dim, group, query, *refs
):
    sources, (out, kept, logs, turned, maxima, totals, all_keys, all_values, sems) = (
        refs[:8],
        refs[8:],
    )
    factor = head_dim ** (-0.5) * LOG2E
    own = group[0]
    copies = block_copies(own, sources, all_keys, all_values, sems)
    for copy in copies:
        copy.start()
    spread(heads, head_dim, query, turned)
    kept[...] = jnp.zeros_like(kept)
    maxima[...] = jnp.full_like(maxima, -jnp.inf)
    totals[...] = jnp.zeros_like(totals)
    for copy in copies:
        copy.wait()

    def one_block(index, masked):
        for offset, extent, chunks in chunks_of(heads):
            first = pl.multiple_of(index * BLOCK + offset, SHORT_PART)
            keys = all_keys[pl.ds(first, extent), :]
            values = all_values[pl.ds(first, extent), :].T
            for column, width in chunks:
                at = slice(column, column + width)
                scores = dotf(keys, turned[:, at]) * factor
                if masked:
                    scores = jnp.where(visible_in(extent, width), scores, -jnp.inf)
                old = maxima[:, at]
                new = jnp.maximum(old, jnp.max(scores, axis=0, keepdims=True))
                rescale = jnp.exp2(old - new)
                weights = jnp.exp2(scores - new)
                maxima[:, at] = new
                totals[:, at] = totals[:, at] * rescale + jnp.sum(weights, axis=0, keepdims=True)
                kept[:, at] = kept[:, at] * rescale + dotf(values, weights.astype(jnp.bfloat16))

    def step(index, carry):
        one_block(index, False)
        return carry

    lax.fori_loop(0, own, step, 0)
    one_block(own, True)
    logs[...] = maxima[...] + jnp.log2(totals[...])
    for h in range(heads):
        cols = slice(h * head_dim, (h + 1) * head_dim)
        for rows, first, width in (
            (slice(0, SHORT_PART), h * SHORT_PART, SHORT_PART),
            (slice(SHORT_PART, BLOCK), heads * SHORT_PART + h * LONG_PART, LONG_PART),
        ):
            at = slice(first, first + width)
            exact = kept[:, at] * (1.0 / totals[:, at])
            kept[:, at] = exact
            out[rows, cols] = exact.T.astype(jnp.bfloat16)


def backward_kernel(heads, head_dim, group, query, grad, kept, logs, *refs):
    sources = refs[:8]
    query_grad, key_grad, value_grad = refs[8:11]
    turned, grad_turned, total, delta, short_query, short_grad = refs[11:17]
    all_keys, all_values, sems = refs[17:]
    scale = head_dim ** (-0.5)
    factor = scale * LOG2E
    own = group[0]
    count = all_keys.shape[0] // BLOCK
    bits = bits_of(count) - 1
    copies = block_copies(own, sources, all_keys, all_values, sems)
    for copy in copies:
        copy.start()
    spread(heads, head_dim, query, turned)
    spread(heads, head_dim, grad, grad_turned)
    for h in range(heads):
        cols = slice(h * head_dim, (h + 1) * head_dim)
        rows = slice(h * SHORT_PART, (h + 1) * SHORT_PART)
        short_query[rows, :] = query[:SHORT_PART, cols]
        short_grad[rows, :] = grad[:SHORT_PART, cols]
    delta[...] = jnp.sum(grad_turned[...].astype(jnp.float32) * kept[...], axis=0, keepdims=True)
    total[...] = jnp.zeros_like(total)
    for copy in copies:
        copy.wait()

    def places(index):
        relative = index ^ own
        core, rest = relative & 1, relative >> 1
        key_place = core * (count // 2) + turned_bits(rest, bits)
        return key_place * BLOCK, (core * (count // 2) + rest) * BLOCK

    def one_block(index, masked):
        key_first, value_first = places(index)
        for offset, extent, chunks in chunks_of(heads):
            first = pl.multiple_of(index * BLOCK + offset, SHORT_PART)
            keys = all_keys[pl.ds(first, extent), :]
            values = all_values[pl.ds(first, extent), :]
            keys_turned = keys.T
            key_sum = None
            value_sum = None
            for h, (column, width) in enumerate(chunks):
                at = slice(column, column + width)
                if offset == 0:
                    rows_query, rows_grad = short_query[...], short_grad[...]
                else:
                    cols = slice(h * head_dim, (h + 1) * head_dim)
                    rows_query, rows_grad = query[SHORT_PART:, cols], grad[SHORT_PART:, cols]
                scores = dotf(keys, turned[:, at]) * factor
                chance = jnp.exp2(scores - logs[:, at])
                if masked:
                    chance = jnp.where(visible_in(extent, width), chance, 0.0)
                chance_grad = dotf(values, grad_turned[:, at])
                score_low = (chance * (chance_grad - delta[:, at])).astype(jnp.bfloat16)
                key_part = dotf(score_low, rows_query)
                value_part = dotf(chance.astype(jnp.bfloat16), rows_grad)
                key_sum = key_part if key_sum is None else key_sum + key_part
                value_sum = value_part if value_sum is None else value_sum + value_part
                total[:, at] += dotf(keys_turned, score_low)
            key_rows = pl.ds(pl.multiple_of(key_first + offset, SHORT_PART), extent)
            value_rows = pl.ds(pl.multiple_of(value_first + offset, SHORT_PART), extent)
            key_grad[key_rows, :] = (key_sum * scale).astype(jnp.bfloat16)
            value_grad[value_rows, :] = value_sum.astype(jnp.bfloat16)

    def step(index, carry):
        one_block(index, False)
        return carry

    def clear(index, carry):
        nothing = jnp.zeros((BLOCK, head_dim), jnp.bfloat16)
        key_first, value_first = places(index)
        key_grad[pl.ds(pl.multiple_of(key_first, SHORT_PART), BLOCK), :] = nothing
        value_grad[pl.ds(pl.multiple_of(value_first, SHORT_PART), BLOCK), :] = nothing
        return carry

    lax.fori_loop(0, own, step, 0)
    one_block(own, True)
    lax.fori_loop(own + 1, count, clear, 0)
    for h in range(heads):
        cols = slice(h * head_dim, (h + 1) * head_dim)
        for rows, first, width in (
            (slice(0, SHORT_PART), h * SHORT_PART, SHORT_PART),
            (slice(SHORT_PART, BLOCK), heads * SHORT_PART + h * LONG_PART, LONG_PART),
        ):
            query_grad[rows, cols] = (total[:, first : first + width] * scale).T.astype(jnp.bfloat16)


def in_vmem(count):
    return [pl.BlockSpec(memory_space=pltpu.VMEM)] * count


def gathered_scratch(sources, head_dim):
    rows = sum(part.shape[0] for part in sources[:4])
    return [
        pltpu.VMEM((rows, head_dim), jnp.bfloat16),
        pltpu.VMEM((rows, head_dim), jnp.bfloat16),
        pltpu.SemaphoreType.DMA((2 * rows // BLOCK,)),
    ], rows


def attention_forward(group, query, sources, heads, head_dim):
    columns = heads * BLOCK
    scratch, rows = gathered_scratch(sources, head_dim)
    return pl.pallas_call(
        functools.partial(forward_kernel, heads, head_dim),
        out_shape=(
            jax.ShapeDtypeStruct(query.shape, jnp.bfloat16),
            jax.ShapeDtypeStruct((head_dim, columns), jnp.float32),
            jax.ShapeDtypeStruct((1, columns), jnp.float32),
        ),
        in_specs=[pl.BlockSpec(memory_space=pltpu.SMEM)]
        + in_vmem(1)
        + [pl.BlockSpec(memory_space=pl.ANY)] * 8,
        out_specs=tuple(in_vmem(3)),
        scratch_shapes=[
            pltpu.VMEM((head_dim, columns), jnp.bfloat16),
            pltpu.VMEM((1, columns), jnp.float32),
            pltpu.VMEM((1, columns), jnp.float32),
        ]
        + scratch,
        compiler_params=pltpu.CompilerParams(vmem_limit_bytes=50 << 20),
        cost_estimate=pl.CostEstimate(flops=2 * columns * rows * head_dim * 2, bytes_accessed=4 * rows * head_dim, transcendentals=0),
        name="attention_forward",
    )(group, query, *sources)


def attention_backward(group, query, grad, sources, kept, logs, heads, head_dim):
    columns = heads * BLOCK
    scratch, rows = gathered_scratch(sources, head_dim)
    return pl.pallas_call(
        functools.partial(backward_kernel, heads, head_dim),
        out_shape=(
            jax.ShapeDtypeStruct(query.shape, jnp.bfloat16),
            jax.ShapeDtypeStruct((rows, head_dim), jnp.bfloat16),
            jax.ShapeDtypeStruct((rows, head_dim), jnp.bfloat16),
        ),
        in_specs=[pl.BlockSpec(memory_space=pltpu.SMEM)]
        + in_vmem(4)
        + [pl.BlockSpec(memory_space=pl.ANY)] * 8,
        out_specs=tuple(in_vmem(3)),
        scratch_shapes=[
            pltpu.VMEM((head_dim, columns), jnp.bfloat16),
            pltpu.VMEM((head_dim, columns), jnp.bfloat16),
            pltpu.VMEM((head_dim, columns), jnp.float32),
            pltpu.VMEM((1, columns), jnp.float32),
            pltpu.VMEM((heads * SHORT_PART, head_dim), jnp.bfloat16),
            pltpu.VMEM((heads * SHORT_PART, head_dim), jnp.bfloat16),
        ]
        + scratch,
        compiler_params=pltpu.CompilerParams(vmem_limit_bytes=56 << 20),
        cost_estimate=pl.CostEstimate(flops=2 * columns * rows * head_dim * 2, bytes_accessed=4 * rows * head_dim, transcendentals=0),
        name="attention_backward",
    )(group, query, grad, kept, logs, *sources)


def normalize(rows, gain):
    return rows * lax.rsqrt(jnp.mean(rows * rows, axis=-1, keepdims=True) + EPS) * gain


def gated(gate_in, up_in):
    return jax.nn.silu(gate_in) * up_in


def after(value, *others):
    return lax.optimization_barrier((value,) + others)[0]


class Order:
    def __init__(self):
        self.last = ()

    def take(self, *values):
        out = lax.optimization_barrier(values + self.last)[: len(values)]
        return out if len(values) > 1 else out[0]

    def mark(self, *values):
        self.last = tuple(jax.tree.leaves(values))


def add_low(left, right):
    return (left.astype(jnp.float32) + right.astype(jnp.float32)).astype(jnp.bfloat16)


def plus_kernel(held, got, *outs):
    value = held[...].astype(jnp.float32) + got[...].astype(jnp.float32)
    if len(outs) == 1:
        outs[0][...] = value.astype(jnp.bfloat16)
        return
    half = pl.num_programs(0) // 2

    @pl.when(pl.program_id(0) < half)
    def _():
        outs[0][...] = value.astype(jnp.bfloat16)

    @pl.when(pl.program_id(0) >= half)
    def _():
        outs[1][...] = value.astype(jnp.bfloat16)


def plus(held, got, halves):
    rows, width = held.shape
    steps = 4 if rows % 64 == 0 else 2
    block = (rows // steps, width)
    if halves:
        half = steps // 2
        source = lambda i: (lax.rem(i + half, steps), 0)
        out_specs = [
            pl.BlockSpec(block, lambda i: (jnp.minimum(i, half - 1), 0)),
            pl.BlockSpec(block, lambda i: (jnp.maximum(i - half, 0), 0)),
        ]
        out_shape = [jax.ShapeDtypeStruct((rows // 2, width), jnp.bfloat16)] * 2
    else:
        source = lambda i: (i, 0)
        out_specs = [pl.BlockSpec(block, source)]
        out_shape = [jax.ShapeDtypeStruct((rows, width), jnp.bfloat16)]
    out = pl.pallas_call(
        plus_kernel,
        grid=(steps,),
        in_specs=[pl.BlockSpec(block, source)] * 2,
        out_specs=out_specs,
        out_shape=out_shape,
        compiler_params=pltpu.CompilerParams(vmem_limit_bytes=24 << 20),
        cost_estimate=FREE,
        name="plus",
    )(held, got)
    return out if halves else out[0]


def join_kernel(axis, *refs):
    *parts, out, inside, in_sems, out_sems = refs
    arriving, leaving, first = [], [], 0
    for i, part in enumerate(parts):
        extent = part.shape[axis]
        cut = (pl.ds(first, extent), slice(None)) if axis == 0 else (slice(None), pl.ds(first, extent))
        arriving.append(pltpu.make_async_copy(part, inside.at[cut], in_sems.at[i]))
        leaving.append(pltpu.make_async_copy(inside.at[cut], out.at[cut], out_sems.at[i]))
        first += extent
    for copy in arriving:
        copy.start()
    for arrived, left in zip(arriving, leaving):
        arrived.wait()
        left.start()
    for copy in leaving:
        copy.wait()


def join(parts, axis):
    shape = list(parts[0].shape)
    shape[axis] = sum(part.shape[axis] for part in parts)
    anywhere = pl.BlockSpec(memory_space=pl.ANY)
    return pl.pallas_call(
        functools.partial(join_kernel, axis),
        in_specs=[anywhere] * len(parts),
        out_specs=anywhere,
        out_shape=jax.ShapeDtypeStruct(tuple(shape), parts[0].dtype),
        scratch_shapes=[
            pltpu.VMEM(tuple(shape), parts[0].dtype),
            pltpu.SemaphoreType.DMA((len(parts),)),
            pltpu.SemaphoreType.DMA((len(parts),)),
        ],
        compiler_params=pltpu.CompilerParams(vmem_limit_bytes=24 << 20),
        cost_estimate=FREE,
        name="join",
    )(*parts)


def rows_kernel(contract, count, places, *refs):
    parts, (weight, out) = refs[:count], refs[count:]
    for i, part in enumerate(parts):
        rows = part.shape[contract[0] ^ 1]
        out[pl.ds(pl.multiple_of(places[i] * rows, 16), rows), :] = lax.dot_general(
            part[...],
            weight[...],
            (((contract[0],), (contract[1],)), ((), ())),
            preferred_element_type=jnp.float32,
        ).astype(jnp.bfloat16)


def rows_product(parts, weight, contract, name, places=None):
    count = len(parts)
    if places is None:
        places = jnp.arange(count, dtype=jnp.int32)
    rows, width = parts[0].shape[contract[0] ^ 1], weight.shape[contract[1] ^ 1]
    return pl.pallas_call(
        functools.partial(rows_kernel, contract, count),
        in_specs=[pl.BlockSpec(memory_space=pltpu.SMEM)] + in_vmem(count + 1),
        out_specs=pl.BlockSpec(memory_space=pltpu.VMEM),
        out_shape=jax.ShapeDtypeStruct((rows * count, width), jnp.bfloat16),
        compiler_params=pltpu.CompilerParams(vmem_limit_bytes=40 << 20),
        cost_estimate=FREE,
        name=name,
    )(places, *parts, weight)


def ring_of(count):
    return [0] + list(range(1, count, 2)) + list(range(2, count, 2))[::-1]


def ring_place(back):
    ring = ring_of(lax.axis_size("mp"))
    count = len(ring)
    table = [ring[(ring.index(i) - back) % count] for i in range(count)]
    return jnp.asarray(table, jnp.int32)[lax.axis_index("mp")]


def ring_pass(array):
    ring = ring_of(lax.axis_size("mp"))
    pairs = [(ring[i], ring[(i + 1) % len(ring)]) for i in range(len(ring))]
    return lax.ppermute(array, "mp", pairs)


def put_rows(whole_rows, rows, place):
    return lax.dynamic_update_slice_in_dim(whole_rows, rows, place * rows.shape[0], 0)


def take_rows(whole_rows, place):
    count = whole_rows.shape[0] // lax.axis_size("mp")
    return lax.dynamic_slice_in_dim(whole_rows, place * count, count, 0)


def ring_rows(parts):
    out = jnp.zeros((parts[0].shape[0] * len(parts),) + parts[0].shape[1:], parts[0].dtype)
    for step, rows in enumerate(parts):
        out = put_rows(out, rows, ring_place(step))
    return out


class RingGather:
    def __init__(self, rows):
        self.parts = [rows]
        self.start()

    def start(self):
        if len(self.parts) < lax.axis_size("mp"):
            self.flying = ring_pass(self.parts[-1])

    def step(self, order):
        if len(self.parts) < lax.axis_size("mp"):
            rows = order.take(self.flying)
            order.mark(rows)
            self.parts.append(rows)
            self.start()

    def steps_left(self):
        return lax.axis_size("mp") - len(self.parts)

    def rows(self):
        return ring_rows(self.parts)


class RingScatter:
    def __init__(self, part):
        self.part, self.steps = part, 1
        self.held = part(1)
        self.flying = ring_pass(self.held)

    def step(self, order):
        if self.steps_left():
            self.steps += 1
            got, own = order.take(self.flying, self.part(self.steps % lax.axis_size("mp")))
            self.held = add_low(own, got)
            order.mark(self.held)
            if self.steps_left():
                self.flying = ring_pass(self.held)

    def steps_left(self):
        return lax.axis_size("mp") - self.steps


def trade(array, bit):
    count = lax.axis_size("dp")
    return lax.ppermute(array, "dp", [(i, i ^ (1 << bit)) for i in range(count)])


def bit_here(bit):
    return (lax.axis_index("dp") >> bit) & 1


def orders():
    rest = list(range(1, bits_of(lax.axis_size("dp"))))
    return [0] + rest, [0] + rest[::-1]


class Lane:
    def __init__(self, partial, order, axis):
        self.bits, self.axis = order, axis
        self.steps = [("halve", bit) for bit in order]
        self.steps += [("double", bit) for bit in order[:0:-1]] + [("core", 0)]
        self.cut_and_start(lambda which, half: self.cut(partial, which, half), partial.shape[axis])

    def cut(self, array, which, half):
        return lax.dynamic_slice_in_dim(array, which * half, half, self.axis)

    def cut_and_start(self, part, extent):
        bit = self.steps[0][1]
        mine = bit_here(bit)
        self.sent, self.held = part(1 - mine, extent // 2), part(mine, extent // 2)
        self.flying = trade(self.sent, bit)

    def step(self, order):
        kind, _ = self.steps.pop(0)
        got, held = order.take(self.flying, self.held)
        if not self.steps:
            self.pieces = [held, got]
            order.mark(self.pieces)
            return
        following, bit = self.steps[0]
        if kind == "halve" and following == "halve":
            self.cut_and_start(
                lambda which, half: add_low(self.cut(held, which, half), self.cut(got, which, half)),
                held.shape[self.axis],
            )
        else:
            if kind == "halve":
                self.held = add_low(held, got)
            else:
                self.held = jnp.concatenate([held, got], axis=self.axis)
            self.sent = self.held
            self.flying = trade(self.sent, bit)
        order.mark(self.sent, self.held)

    def places(self):
        own = jnp.int32(0)
        for bit in self.bits[1:]:
            own = own * 2 + bit_here(bit)
        count = 1 << (len(self.bits) - 1)
        relative = jnp.arange(count, dtype=jnp.int32) ^ own
        core = bit_here(0)
        return jnp.concatenate([core * count + relative, (1 - core) * count + relative])


def kept_first(first_bit_first):
    count = lax.axis_size("dp")
    bits = bits_of(count) - 1
    order = [turned_bits(i, bits) if first_bit_first else i for i in range(count // 2)]
    own = lax.axis_index("dp").astype(jnp.int32)
    relative = jnp.asarray([2 * i for i in order] + [2 * i + 1 for i in order], jnp.int32)
    return relative ^ own


def product_kernel(groups, split, places, *refs):
    inputs, at = [], 0
    for parts, beside in groups:
        inputs.append((refs[at : at + parts], refs[at + parts : at + parts * (1 + beside)]))
        at += parts * (1 + beside)
    scratch = refs[len(refs) - 2 * len(groups) :]
    values = []
    for g, ((lefts, rights), (parts, _)) in enumerate(zip(inputs, groups)):
        left, right = scratch[2 * g : 2 * g + 2]
        count, width = rights[0].shape

        @pl.when(pl.program_id(0) == 0)
        def _(rights=rights, right=right, count=count, width=width, parts=parts):
            for i, part in enumerate(rights):
                row, column = i % parts * count, i // parts * width
                right[row : row + count, column : column + width] = part[...]

        for i, part in enumerate(lefts):
            left[i * count : (i + 1) * count, :] = part[...]
        values.append(
            lax.dot_general(
                left[...], right[...], (((0,), (0,)), ((), ())), preferred_element_type=jnp.float32
            ).astype(jnp.bfloat16)
        )
    first = 0
    for value in values:
        cut = (slice(None), slice(first, first + value.shape[1]))
        first += value.shape[1]
        if split is None:
            refs[at][cut] = value
            continue
        other, sent, held = refs[at : at + 3]
        total = (value.astype(jnp.float32) + other[cut].astype(jnp.float32)).astype(jnp.bfloat16)

        @pl.when(pl.program_id(0) < split)
        def _(total=total, cut=cut):
            sent[cut] = total

        @pl.when(pl.program_id(0) >= split)
        def _(total=total, cut=cut):
            held[cut] = total


def product_blocks(products, places, rows, name, other=None):
    blocks = places.shape[0]
    if other is None:
        split, order, inputs = None, lambda i: i, ()
    else:
        split, order, inputs = blocks // 2, lambda i: lax.rem(i + blocks // 2, blocks), (other,)
    arrays, in_specs, scratch, groups, total = [], [], [], [], 0
    for lefts, rights in products:
        tokens = lefts[0].shape[0]
        moving = pl.BlockSpec((tokens, rows), lambda i, places: (0, places[order(i)]))
        arrays += list(lefts)
        in_specs += [moving] * len(lefts)
        width = sum(right[0].shape[1] for right in rights)
        for right in rights:
            arrays += list(right)
            in_specs += [pl.BlockSpec(right[0].shape, lambda i, places: (0, 0))] * len(right)
        scratch += [
            pltpu.VMEM((tokens * len(lefts), rows), jnp.bfloat16),
            pltpu.VMEM((tokens * len(lefts), width), jnp.bfloat16),
        ]
        groups.append((len(lefts), len(rights)))
        total += width
    block = (rows, total)
    if other is None:
        out_specs = pl.BlockSpec(block, lambda i, places: (i, 0))
        out_shape = jax.ShapeDtypeStruct((blocks * rows, total), jnp.bfloat16)
    else:
        in_specs.append(pl.BlockSpec(block, lambda i, places: (order(i), 0)))
        out_specs = [
            pl.BlockSpec(block, lambda i, places: (jnp.minimum(i, split - 1), 0)),
            pl.BlockSpec(block, lambda i, places: (jnp.maximum(i - split, 0), 0)),
        ]
        out_shape = [jax.ShapeDtypeStruct((split * rows, total), jnp.bfloat16)] * 2
    return pl.pallas_call(
        functools.partial(product_kernel, tuple(groups), split),
        grid_spec=pltpu.PrefetchScalarGridSpec(
            num_scalar_prefetch=1,
            grid=(blocks,),
            in_specs=in_specs,
            out_specs=out_specs,
            scratch_shapes=scratch,
        ),
        out_shape=out_shape,
        compiler_params=pltpu.CompilerParams(vmem_limit_bytes=48 << 20),
        cost_estimate=FREE,
        name=name,
    )(places, *arrays, *inputs)


class BlockLane:
    def __init__(self, order, products, bits, name, first_row=0, rows=None):
        self.bits, self.name, self.products = list(bits), name, products
        self.rows = rows or products[0][0][0].shape[1] // lax.axis_size("dp")
        self.first_row = first_row
        self.places = kept_first(bits[1] == 1)
        self.table = self.places + first_row // self.rows
        half = self.places.shape[0] // 2
        self.sent = product_blocks(self.taken(order), self.table[half:], self.rows, name + "_sent")
        order.mark(self.sent)
        self.flying = trade(self.sent, 0)
        self.steps = ["product"] + ["halve"] * (len(bits) - 1) + ["double"] * (len(bits) - 1)
        self.steps += ["core"]

    def taken(self, order):
        leaves, shape = jax.tree.flatten(self.products)
        return jax.tree.unflatten(shape, order.take(*leaves))

    def step(self, order):
        kind = self.steps.pop(0)
        if kind == "product":
            self.bits.pop(0)
            got = order.take(self.flying)
            half = self.places.shape[0] // 2
            self.sent, self.held = product_blocks(
                self.taken(order), self.table[:half], self.rows, self.name + "_kept", got
            )
            self.done_bits = []
            self.flying = trade(self.sent, self.bits[0])
            order.mark(self.sent, self.held)
            return
        if kind == "both":
            near, far, own = order.take(*self.flying, self.held)
            self.held = self.sent = (own, near, far)
            self.flying = trade(near, self.done_bits[0])
            order.mark(self.held)
            return
        if kind == "rest":
            self.held = self.sent = join(order.take(*self.held, self.flying), 0)
            self.flying = trade(self.held, 0)
            order.mark(self.held)
            return
        got, held = order.take(self.flying, self.held)
        if kind == "core":
            self.pieces = [held, got]
            order.mark(self.pieces)
            return
        if kind == "halve":
            self.done_bits.append(self.bits.pop(0))
            if self.bits:
                self.sent, self.held = plus(held, got, True)
                self.flying = trade(self.sent, self.bits[0])
                order.mark(self.sent, self.held)
                return
            held = plus(held, got, False)
            if len(self.done_bits) == 2:
                self.steps = ["both", "rest", "core"]
                self.held = self.sent = held
                self.flying = (trade(held, self.done_bits[1]), trade(held, self.done_bits[0]))
                order.mark(held)
                return
        else:
            self.done_bits.pop()
            held = join([held, got], 0)
        self.held = self.sent = held
        self.flying = trade(held, self.done_bits[-1] if self.done_bits else 0)
        order.mark(self.held)


def block_lanes(order, products, name):
    first, second = orders()
    total = products[0][0][0].shape[1]
    rows = total // lax.axis_size("dp")
    if rows % 256:
        return [BlockLane(order, products, first, name)]
    return [
        BlockLane(order, products, first, name + "_low", 0, rows // 2),
        BlockLane(order, products, second, name + "_high", total // 2, rows // 2),
    ]


def unfold_kernel(firsts, pieces, targets, places, *refs):
    sets = 2 * len(firsts)
    sources, outs = refs[:sets], refs[sets : sets + len(targets)]
    landed = refs[sets + len(targets)]
    raised = refs[sets + len(targets) + 1 : -2]
    in_sems, out_sems = refs[-2:]
    rows = landed.shape[1]
    slots = raised[0].shape[0]
    total = sets * pieces

    def fetch(i):
        source = sources[i // pieces]
        return pltpu.make_async_copy(
            source.at[pl.ds(i % pieces * rows, rows), :], landed.at[i], in_sems.at[i]
        )

    def store(i):
        along = pl.multiple_of(firsts[i // (2 * pieces)] + places[i] * rows, rows)
        copies = []
        for k, ((_, turned), out) in enumerate(zip(targets, outs)):
            window = out.at[:, pl.ds(along, rows)] if turned else out.at[pl.ds(along, rows), :]
            copies.append(
                pltpu.make_async_copy(
                    raised[k].at[i % slots], window, out_sems.at[i * len(targets) + k]
                )
            )
        return copies

    for i in range(total):
        fetch(i).start()
    for i in range(total):
        fetch(i).wait()
        if i >= slots:
            for copy in store(i - slots):
                copy.wait()
        first = 0
        for k, (width, turned) in enumerate(targets):
            value = landed[i, :, first : first + width].astype(jnp.float32)
            raised[k][i % slots] = value.T if turned else value
            first += width
        for copy in store(i):
            copy.start()
    for i in range(max(total - slots, 0), total):
        for copy in store(i):
            copy.wait()


def unfold(lanes, targets, name):
    sets = [piece for lane in lanes for piece in lane.pieces]
    rows, width = lanes[0].rows, sets[0].shape[1]
    pieces = sets[0].shape[0] // rows
    total, slots = len(sets) * pieces, 4
    height = total * rows
    anywhere = pl.BlockSpec(memory_space=pl.ANY)
    return pl.pallas_call(
        functools.partial(
            unfold_kernel, tuple(lane.first_row for lane in lanes), pieces, tuple(targets)
        ),
        in_specs=[pl.BlockSpec(memory_space=pltpu.SMEM)] + [anywhere] * len(sets),
        out_specs=[anywhere] * len(targets),
        out_shape=[
            jax.ShapeDtypeStruct((w, height) if turned else (height, w), jnp.float32)
            for w, turned in targets
        ],
        scratch_shapes=[pltpu.VMEM((total, rows, width), jnp.bfloat16)]
        + [
            pltpu.VMEM((slots, w, rows) if turned else (slots, rows, w), jnp.float32)
            for w, turned in targets
        ]
        + [
            pltpu.SemaphoreType.DMA((total,)),
            pltpu.SemaphoreType.DMA((total * len(targets),)),
        ],
        compiler_params=pltpu.CompilerParams(vmem_limit_bytes=48 << 20),
        cost_estimate=FREE,
        name=name,
    )(jnp.concatenate([lane.places for lane in lanes]), *sets)


def lay_kernel(lanes, sets, pieces, axis, cuts, places, *refs):
    outs = refs[lanes * sets : -4]
    landed, raised, in_sems, out_sems = refs[-4:]
    rows, columns = landed.shape[1:]
    slots = raised.shape[0]
    total = lanes * sets * pieces

    def window(ref, along, across, extent):
        if axis == 0:
            return ref.at[pl.ds(along, rows), pl.ds(across, extent)]
        return ref.at[pl.ds(across, extent), pl.ds(along, columns)]

    def fetch(i):
        first = i % pieces * (rows, columns)[axis]
        source = refs[i // pieces]
        across = source.shape[1 - axis]
        return pltpu.make_async_copy(
            window(source, first, 0, across), window(landed.at[i], 0, 0, across), in_sems.at[i]
        )

    def store(i):
        along = pl.multiple_of(places[i] * (rows, columns)[axis], (rows, columns)[axis])
        return [
            pltpu.make_async_copy(
                window(raised.at[i % slots], 0, first, extent),
                window(outs[out], along, target, extent),
                out_sems.at[2 * i + k],
            )
            for k, (out, first, extent, target) in enumerate(cuts[i // (sets * pieces)])
        ]

    for i in range(total):
        fetch(i).start()
    for i in range(total):
        fetch(i).wait()
        if i >= slots:
            for copy in store(i - slots):
                copy.wait()
        extent = refs[i // pieces].shape[1 - axis]
        filled = (slice(None), slice(extent)) if axis == 0 else (slice(extent), slice(None))
        raised[(i % slots, *filled)] = landed[(i, *filled)].astype(jnp.float32)
        for copy in store(i):
            copy.start()
    for i in range(max(total - slots, 0), total):
        for copy in store(i):
            copy.wait()


def lay_out(lanes, cuts, shapes, name):
    sets = [piece for lane in lanes for piece in lane.pieces]
    axis = lanes[0].axis
    places = jnp.concatenate([lane.places() for lane in lanes])
    pieces = places.shape[0] // len(sets)
    block = [max(piece.shape[d] for piece in sets) for d in (0, 1)]
    block[axis] //= pieces
    total = len(sets) * pieces
    anywhere = pl.BlockSpec(memory_space=pl.ANY)
    return pl.pallas_call(
        functools.partial(lay_kernel, len(lanes), len(lanes[0].pieces), pieces, axis, cuts),
        in_specs=[pl.BlockSpec(memory_space=pltpu.SMEM)] + [anywhere] * len(sets),
        out_specs=[anywhere] * len(shapes),
        out_shape=[jax.ShapeDtypeStruct(shape, jnp.float32) for shape in shapes],
        scratch_shapes=[
            pltpu.VMEM((total, *block), jnp.bfloat16),
            pltpu.VMEM((min(total, 6), *block), jnp.float32),
            pltpu.SemaphoreType.DMA((total,)),
            pltpu.SemaphoreType.DMA((2 * total,)),
        ],
        compiler_params=pltpu.CompilerParams(vmem_limit_bytes=44 << 20),
        cost_estimate=FREE,
        name=name,
    )(places, *sets)


def own_share(array):
    share = array.shape[0] // lax.axis_size("mp")
    return lax.dynamic_slice_in_dim(array, lax.axis_index("mp") * share, share)


class BlockSum:
    def __init__(self, blocks, order):
        self.bits = list(order)
        half = blocks.shape[0] // 2
        self.held, self.sent = blocks[:half], blocks[half:]
        self.flying = trade(self.sent, self.bits[0])

    def step(self, order):
        self.bits.pop(0)
        got, held = order.take(self.flying, self.held)
        if self.bits:
            self.sent, self.held = plus(held, got, True)
            self.flying = trade(self.sent, self.bits[0])
        else:
            self.held = self.sent = plus(held, got, False)
        order.mark(self.sent, self.held)


class BlockGather:
    def __init__(self, rows, order):
        self.bits, self.held = list(order), rows
        self.flying = trade(rows, self.bits[0])

    def step(self, order):
        if not self.bits:
            got = order.take(*self.flying)
            order.mark(got)
            self.parts = self.held + list(got)
            return
        self.bits.pop(0)
        got, held = order.take(self.flying, self.held)
        if self.bits:
            self.held = jnp.concatenate([held, got], axis=0)
            self.flying = trade(self.held, self.bits[0])
        else:
            self.held = [held, got]
            self.flying = [trade(part, 0) for part in self.held]
        order.mark(self.held)


class SmallSum:
    def __init__(self, array, axis):
        self.axis, self.held = axis, array
        self.bits = list(range(bits_of(lax.axis_size(axis))))
        self.start()

    def start(self):
        if self.bits:
            count = lax.axis_size(self.axis)
            pairs = [(i, i ^ (1 << self.bits[0])) for i in range(count)]
            self.flying = lax.ppermute(self.held, self.axis, pairs)

    def step(self, order):
        if self.bits:
            self.bits.pop(0)
            got, held = order.take(self.flying, self.held)
            self.held = held + got
            order.mark(self.held)
            self.start()


def column_share(rows):
    ring = ring_of(lax.axis_size("mp"))
    count = len(ring)
    width = rows.shape[1] // count
    parts = []
    for step in range(count):
        part = lax.dynamic_slice_in_dim(rows, ring_place(-step) * width, width, 1)
        pairs = [(ring[i], ring[(i + step) % count]) for i in range(count)]
        parts.append(lax.ppermute(part, "mp", pairs) if step else part)
    return parts


def shards(
    tokens,
    attn_gain,
    query_down,
    query_up,
    key_value,
    attn_out,
    mlp_gain,
    gate_weight,
    up_weight,
    down_weight,
    out_grad,
):
    head_dim = HEAD_DIM
    local_heads = query_up.shape[1] // head_dim
    ranks = lax.axis_size("mp")
    group = lax.axis_index("dp").reshape(1).astype(jnp.int32)
    ring_places = jnp.stack([ring_place(i) for i in range(lax.axis_size("mp"))])
    first, second = orders()

    def rows_of(array):
        return lambda back: take_rows(array, ring_place(back))

    def parts_of(array):
        count = array.shape[0] // ranks
        return lambda back: array[back * count : (back + 1) * count]

    def weight_grad(left, right):
        return jnp.einsum("tk,td->kd", left, right, preferred_element_type=jnp.float32).astype(
            jnp.bfloat16
        )

    def steps(*moving):
        for one in moving:
            one.step(order)

    def finish(*lanes):
        while lanes[0].steps:
            steps(*lanes)

    order = Order()
    inputs = tokens.astype(jnp.float32)
    normal_one = normalize(inputs, attn_gain).astype(jnp.bfloat16)
    pair_local = dotf(normal_one, key_value).astype(jnp.bfloat16)
    order.mark(pair_local)
    pair_ring = RingGather(pair_local)
    latent = dotf(order.take(normal_one), query_down).astype(jnp.bfloat16)
    order.mark(latent)
    latent_ring = RingGather(latent)
    while pair_ring.steps_left() > 1:
        steps(pair_ring, latent_ring)
    steps(pair_ring)
    pair_own = pair_ring.rows()
    order.mark(pair_own)
    keys = BlockGather(pair_own[:, :head_dim], first[1:])
    values = BlockGather(pair_own[:, head_dim:], second[1:])
    while latent_ring.steps_left():
        steps(latent_ring)
    grad_ring = RingGather(order.take(out_grad))
    latent_full = order.take(latent_ring.rows())
    query_full = dotf(latent_full, query_up).astype(jnp.bfloat16)
    order.mark(query_full)
    steps(keys, values, grad_ring)
    while keys.bits:
        steps(keys, values)
    steps(grad_ring, keys, values)
    share_parts = column_share(order.take(normal_one))
    sources = order.take(*keys.parts, *values.parts)
    attended, kept, logs = attention_forward(group, query_full, sources, local_heads, head_dim)
    order.mark(attended)
    share_parts = order.take(*share_parts)
    order.mark(*share_parts)
    steps(grad_ring)
    attn_partial = dotf(order.take(attended), attn_out).astype(jnp.bfloat16)
    order.mark(attn_partial)
    attn_ring = RingScatter(rows_of(attn_partial))
    while grad_ring.steps_left():
        steps(grad_ring)
    grad_ringed = jnp.concatenate(order.take(*grad_ring.parts), axis=0)
    act_grad = jnp.einsum("td,fd->tf", grad_ringed, down_weight, preferred_element_type=jnp.float32)
    normal_share = ring_rows(share_parts)
    order.mark(act_grad, normal_share)
    while attn_ring.steps_left():
        steps(attn_ring)
    hidden_res = inputs + attn_ring.held.astype(jnp.float32)
    normal_two = normalize(hidden_res, mlp_gain).astype(jnp.bfloat16)
    order.mark(normal_two)
    two_ring = RingGather(normal_two)
    act_parts = parts_of(act_grad)
    activated, gate_low, up_low, two_terms = [], [], [], []
    two_sum = None
    for block in range(ranks):
        steps(*([two_ring] if block else []))
        rows = order.take(two_ring.parts[block])
        gate = dotf(rows, gate_weight)
        upward = dotf(rows, up_weight)
        _, gated_pull = jax.vjp(gated, gate, upward)
        gate_grad32, up_grad32 = gated_pull(act_parts(block))
        activated.append(gated(gate, upward).astype(jnp.bfloat16))
        gate_low.append(gate_grad32.astype(jnp.bfloat16))
        up_low.append(up_grad32.astype(jnp.bfloat16))
        two_terms.append(
            (
                jnp.einsum("tf,df->td", gate_low[-1], gate_weight, preferred_element_type=jnp.float32)
                + jnp.einsum("tf,df->td", up_low[-1], up_weight, preferred_element_type=jnp.float32)
            ).astype(jnp.bfloat16)
        )
        order.mark(two_terms[-1], activated[-1])
        if block == 1:
            two_sum = RingScatter(lambda back: two_terms[back])
        elif block > 1:
            steps(two_sum)
    while two_sum.steps_left():
        steps(two_sum)
    normal_two_grad = two_sum.held.astype(jnp.float32)
    _, norm_pull_two = jax.vjp(normalize, hidden_res, mlp_gain)
    resid_from_norm, mlp_gain_part = norm_pull_two(normal_two_grad)
    hidden_grad = out_grad.astype(jnp.float32) + resid_from_norm
    branch = hidden_grad.astype(jnp.bfloat16)
    order.mark(branch)
    branch_ring = RingGather(branch)
    def part_sent(*lanes):
        order.mark([lane.sent for lane in lanes])

    low_parts = []

    def low_part():
        rows = order.take(branch_ring.parts[len(low_parts)])
        low_parts.append(rows_product([rows], attn_out, (1, 1), "attended_low"))
        order.mark(low_parts[-1])

    mlp = block_lanes(
        order,
        [(grad_ring.parts, [activated]), (two_ring.parts, [gate_low, up_low])],
        "mlp_grads",
    )
    steps(branch_ring)
    low_part()
    low_part()
    steps(mlp[0])
    steps(branch_ring)
    low_part()
    steps(*mlp[1:])
    while branch_ring.steps_left():
        steps(branch_ring)
        low_part()
    while len(low_parts) < ranks:
        low_part()
    attended_low = ring_rows(low_parts)
    order.mark(attended_low)
    query_low, key_grads, value_grads = attention_backward(
        group, query_full, order.take(attended_low), sources, kept, logs, local_heads, head_dim
    )
    query_low, key_grads, value_grads = lax.optimization_barrier(
        (query_low, key_grads, value_grads, mlp[0].flying)
    )[:3]
    order.mark(query_low)
    key_sum = BlockSum(order.take(key_grads), first)
    value_sum = BlockSum(order.take(value_grads), second)
    part_sent(key_sum, value_sum)
    steps(*mlp)
    latent_partial = rows_product([order.take(query_low)], query_up, (1, 1), "latent_low")
    order.mark(latent_partial)
    latent_low = lax.psum_scatter(latent_partial, "mp", scatter_dimension=0, tiled=True)
    steps(key_sum, value_sum)
    up_query_part = rows_product([latent_full], order.take(query_low), (0, 0), "query_up_grad")
    out_part = weight_grad(attended, ring_rows(order.take(*branch_ring.parts)))
    order.mark(up_query_part, out_part)
    out_sum, up_query_sum = lax.psum((out_part, up_query_part), "dp")
    steps(key_sum, value_sum)
    steps(*mlp)
    while key_sum.bits:
        steps(key_sum, value_sum)
    pair_partial = join(order.take(key_sum.held, value_sum.held), 1)
    order.mark(pair_partial)
    pair_low_sum = RingScatter(rows_of(pair_partial))
    steps(pair_low_sum)
    latent_low = order.take(latent_low)
    order.mark(latent_low)
    low_full = lax.all_gather(latent_low, "mp", axis=0, tiled=True)
    while pair_low_sum.steps_left():
        steps(pair_low_sum)
    pair_low = pair_low_sum.held
    low_pair_ring = RingGather(pair_low)
    result_partial = rows_product(
        order.take(*activated), down_weight, (1, 0), "result", ring_places
    )
    order.mark(result_partial)
    steps(low_pair_ring)
    steps(*mlp)
    while low_pair_ring.steps_left():
        steps(low_pair_ring)
    pair_weight_part = rows_product(
        [normal_share], order.take(low_pair_ring.rows()), (0, 0), "key_value_grad"
    )
    order.mark(pair_weight_part)
    pair_weight = Lane(order.take(pair_weight_part), first, 0)
    part_sent(pair_weight)
    down_query_part = rows_product(
        [normal_share], order.take(low_full), (0, 0), "query_down_grad"
    )
    order.mark(down_query_part)
    down_query = Lane(order.take(down_query_part), second, 0)
    part_sent(down_query)
    result_sum = lax.psum_scatter(
        after(result_partial, low_full), "mp", scatter_dimension=0, tiled=True
    )
    steps(pair_weight, down_query)
    latent_term = jnp.einsum(
        "tr,dr->td", order.take(latent_low), query_down, preferred_element_type=jnp.float32
    )
    order.mark(latent_term)
    normal_one_grad = latent_term + jnp.einsum(
        "tp,dp->td", order.take(pair_low), key_value, preferred_element_type=jnp.float32
    )
    _, norm_pull_one = jax.vjp(normalize, inputs, attn_gain)
    input_from_norm, attn_gain_part = norm_pull_one(normal_one_grad)
    input_grad = hidden_grad + input_from_norm
    order.mark(input_grad, attn_gain_part)
    attn_gain_sum = SmallSum(order.take(attn_gain_part), "mp")
    mlp_gain_sum = SmallSum(order.take(mlp_gain_part), "mp")
    steps(pair_weight, down_query)
    while attn_gain_sum.bits or mlp_gain_sum.bits:
        steps(attn_gain_sum, mlp_gain_sum)
    gains = jnp.stack([own_share(attn_gain_sum.held), own_share(mlp_gain_sum.held)])
    order.mark(gains)
    steps(pair_weight, down_query)
    gains = SmallSum(order.take(gains), "dp")
    while len(down_query.steps) > 2:
        steps(pair_weight, down_query)
        steps(gains)
    out_sum, up_query_sum = order.take(out_sum, up_query_sum)
    order.mark(out_sum, up_query_sum)
    while len(mlp[0].steps) > 1:
        steps(*mlp)
    out_sum = order.take(out_sum).astype(jnp.float32)
    up_query_sum = up_query_sum.astype(jnp.float32)
    order.mark(out_sum, up_query_sum)
    while len(down_query.steps) > 1:
        steps(pair_weight, down_query)
    finish(*mlp)
    down_sum, gate_sum, up_sum = unfold(
        mlp, [(down_weight.shape[0], True)] + [(gate_weight.shape[1], False)] * 2, "mlp_grads_laid"
    )
    order.mark(down_sum)
    finish(pair_weight, down_query)
    while gains.bits:
        steps(gains)
    cuts = tuple(((i, 0, part.shape[1], 0),) for i, part in enumerate((query_down, key_value)))
    down_query_sum, pair_weight_sum = lay_out(
        [down_query, pair_weight],
        cuts,
        [(normal_share.shape[1], part.shape[1]) for part in (query_down, key_value)],
        "query_down_key_value_laid",
    )
    order.mark(down_query_sum)
    result = (hidden_res + order.take(result_sum).astype(jnp.float32)).astype(jnp.bfloat16)
    attn_gain_sum, mlp_gain_sum = gains.held[0], gains.held[1]
    return (
        result,
        input_grad,
        attn_gain_sum,
        down_query_sum,
        up_query_sum,
        pair_weight_sum,
        out_sum,
        mlp_gain_sum,
        gate_sum,
        up_sum,
        down_sum,
    )


def solution(mesh):
    return jax.shard_map(
        shards,
        mesh=mesh,
        in_specs=(
            P(("dp", "mp"), None),
            P(),
            P(),
            P(None, "mp"),
            P(),
            P("mp", None),
            P(),
            P(None, "mp"),
            P(None, "mp"),
            P("mp", None),
            P(("dp", "mp"), None),
        ),
        out_specs=(
            P(("dp", "mp"), None),
            P(("dp", "mp"), None),
            P("mp"),
            P("mp", None),
            P(None, "mp"),
            P("mp", None),
            P("mp", None),
            P("mp"),
            P(None, "mp"),
            P(None, "mp"),
            P("mp", None),
        ),
        check_vma=False,
    )
```

```python
import functools

import jax
import jax.numpy as jnp
from jax import lax
from jax.experimental import pallas as pl
from jax.experimental.pallas import tpu as pltpu
from jax.sharding import PartitionSpec as P

HEAD_DIM = 256
EPS = 1e-06
SHORT_PART = 128
LONG_PART = 512
BLOCK = SHORT_PART + LONG_PART
LOG2E = 1.4426950408889634
FREE = pl.CostEstimate(flops=0, bytes_accessed=0, transcendentals=0)


def dotf(left, right):
    return jnp.dot(left, right, preferred_element_type=jnp.float32)


def turned_bits(value, count):
    return sum(((value >> b) & 1) << (count - 1 - b) for b in range(count))


def bits_of(count):
    return max(count.bit_length() - 1, 0)


def chunks_of(heads):
    short = [(0, heads * SHORT_PART)]
    long = [(heads * SHORT_PART + h * LONG_PART, LONG_PART) for h in range(heads)]
    return ((0, SHORT_PART, short), (SHORT_PART, LONG_PART, long))


def spread(heads, head_dim, source, turned):
    for h in range(heads):
        cols = slice(h * head_dim, (h + 1) * head_dim)
        turned[:, h * SHORT_PART : (h + 1) * SHORT_PART] = source[:SHORT_PART, cols].T
        first = heads * SHORT_PART + h * LONG_PART
        turned[:, first : first + LONG_PART] = source[SHORT_PART:, cols].T


def visible_in(extent, width):
    key_pos = lax.broadcasted_iota(jnp.int32, (extent, width), 0)
    query_pos = lax.broadcasted_iota(jnp.int32, (extent, width), 1) & (extent - 1)
    return key_pos <= query_pos


def block_copies(own, sources, all_keys, all_values, sems):
    copies = []
    for kind, (parts, target) in enumerate(((sources[:4], all_keys), (sources[4:], all_values))):
        held = parts[0].shape[0] // BLOCK
        bits = bits_of(2 * held)
        for place, part in enumerate(parts):
            for i in range(held):
                relative = place % 2 * held + i
                if kind == 1:
                    relative = turned_bits(relative, bits)
                index = own ^ (2 * relative + place // 2)
                first = pl.multiple_of(index * BLOCK, BLOCK)
                copies.append(
                    pltpu.make_async_copy(
                        part.at[pl.ds(i * BLOCK, BLOCK), :],
                        target.at[pl.ds(first, BLOCK), :],
                        sems.at[len(copies)],
                    )
                )
    return copies


def forward_kernel(
    heads, head_dim, group, query, *refs
):
    sources, (out, kept, logs, turned, maxima, totals, all_keys, all_values, sems) = (
        refs[:8],
        refs[8:],
    )
    factor = head_dim ** (-0.5) * LOG2E
    own = group[0]
    copies = block_copies(own, sources, all_keys, all_values, sems)
    for copy in copies:
        copy.start()
    spread(heads, head_dim, query, turned)
    kept[...] = jnp.zeros_like(kept)
    maxima[...] = jnp.full_like(maxima, -jnp.inf)
    totals[...] = jnp.zeros_like(totals)
    for copy in copies:
        copy.wait()

    def one_block(index, masked):
        for offset, extent, chunks in chunks_of(heads):
            first = pl.multiple_of(index * BLOCK + offset, SHORT_PART)
            keys = all_keys[pl.ds(first, extent), :]
            values = all_values[pl.ds(first, extent), :].T
            for column, width in chunks:
                at = slice(column, column + width)
                scores = dotf(keys, turned[:, at]) * factor
                if masked:
                    scores = jnp.where(visible_in(extent, width), scores, -jnp.inf)
                old = maxima[:, at]
                new = jnp.maximum(old, jnp.max(scores, axis=0, keepdims=True))
                rescale = jnp.exp2(old - new)
                weights = jnp.exp2(scores - new)
                maxima[:, at] = new
                totals[:, at] = totals[:, at] * rescale + jnp.sum(weights, axis=0, keepdims=True)
                kept[:, at] = kept[:, at] * rescale + dotf(values, weights.astype(jnp.bfloat16))

    def step(index, carry):
        one_block(index, False)
        return carry

    lax.fori_loop(0, own, step, 0)
    one_block(own, True)
    logs[...] = maxima[...] + jnp.log2(totals[...])
    for h in range(heads):
        cols = slice(h * head_dim, (h + 1) * head_dim)
        for rows, first, width in (
            (slice(0, SHORT_PART), h * SHORT_PART, SHORT_PART),
            (slice(SHORT_PART, BLOCK), heads * SHORT_PART + h * LONG_PART, LONG_PART),
        ):
            at = slice(first, first + width)
            exact = kept[:, at] * (1.0 / totals[:, at])
            kept[:, at] = exact
            out[rows, cols] = exact.T.astype(jnp.bfloat16)


def backward_kernel(heads, head_dim, group, query, grad, kept, logs, *refs):
    sources = refs[:8]
    query_grad, key_grad, value_grad = refs[8:11]
    turned, grad_turned, total, delta, short_query, short_grad = refs[11:17]
    all_keys, all_values, sems = refs[17:]
    scale = head_dim ** (-0.5)
    factor = scale * LOG2E
    own = group[0]
    count = all_keys.shape[0] // BLOCK
    bits = bits_of(count) - 1
    copies = block_copies(own, sources, all_keys, all_values, sems)
    for copy in copies:
        copy.start()
    spread(heads, head_dim, query, turned)
    spread(heads, head_dim, grad, grad_turned)
    for h in range(heads):
        cols = slice(h * head_dim, (h + 1) * head_dim)
        rows = slice(h * SHORT_PART, (h + 1) * SHORT_PART)
        short_query[rows, :] = query[:SHORT_PART, cols]
        short_grad[rows, :] = grad[:SHORT_PART, cols]
    delta[...] = jnp.sum(grad_turned[...].astype(jnp.float32) * kept[...], axis=0, keepdims=True)
    total[...] = jnp.zeros_like(total)
    for copy in copies:
        copy.wait()

    def places(index):
        relative = index ^ own
        core, rest = relative & 1, relative >> 1
        key_place = core * (count // 2) + turned_bits(rest, bits)
        return key_place * BLOCK, (core * (count // 2) + rest) * BLOCK

    def one_block(index, masked):
        key_first, value_first = places(index)
        for offset, extent, chunks in chunks_of(heads):
            first = pl.multiple_of(index * BLOCK + offset, SHORT_PART)
            keys = all_keys[pl.ds(first, extent), :]
            values = all_values[pl.ds(first, extent), :]
            keys_turned = keys.T
            key_sum = None
            value_sum = None
            for h, (column, width) in enumerate(chunks):
                at = slice(column, column + width)
                if offset == 0:
                    rows_query, rows_grad = short_query[...], short_grad[...]
                else:
                    cols = slice(h * head_dim, (h + 1) * head_dim)
                    rows_query, rows_grad = query[SHORT_PART:, cols], grad[SHORT_PART:, cols]
                scores = dotf(keys, turned[:, at]) * factor
                chance = jnp.exp2(scores - logs[:, at])
                if masked:
                    chance = jnp.where(visible_in(extent, width), chance, 0.0)
                chance_grad = dotf(values, grad_turned[:, at])
                score_low = (chance * (chance_grad - delta[:, at])).astype(jnp.bfloat16)
                key_part = dotf(score_low, rows_query)
                value_part = dotf(chance.astype(jnp.bfloat16), rows_grad)
                key_sum = key_part if key_sum is None else key_sum + key_part
                value_sum = value_part if value_sum is None else value_sum + value_part
                total[:, at] += dotf(keys_turned, score_low)
            key_rows = pl.ds(pl.multiple_of(key_first + offset, SHORT_PART), extent)
            value_rows = pl.ds(pl.multiple_of(value_first + offset, SHORT_PART), extent)
            key_grad[key_rows, :] = (key_sum * scale).astype(jnp.bfloat16)
            value_grad[value_rows, :] = value_sum.astype(jnp.bfloat16)

    def step(index, carry):
        one_block(index, False)
        return carry

    def clear(index, carry):
        nothing = jnp.zeros((BLOCK, head_dim), jnp.bfloat16)
        key_first, value_first = places(index)
        key_grad[pl.ds(pl.multiple_of(key_first, SHORT_PART), BLOCK), :] = nothing
        value_grad[pl.ds(pl.multiple_of(value_first, SHORT_PART), BLOCK), :] = nothing
        return carry

    lax.fori_loop(0, own, step, 0)
    one_block(own, True)
    lax.fori_loop(own + 1, count, clear, 0)
    for h in range(heads):
        cols = slice(h * head_dim, (h + 1) * head_dim)
        for rows, first, width in (
            (slice(0, SHORT_PART), h * SHORT_PART, SHORT_PART),
            (slice(SHORT_PART, BLOCK), heads * SHORT_PART + h * LONG_PART, LONG_PART),
        ):
            query_grad[rows, cols] = (total[:, first : first + width] * scale).T.astype(jnp.bfloat16)


def in_vmem(count):
    return [pl.BlockSpec(memory_space=pltpu.VMEM)] * count


def gathered_scratch(sources, head_dim):
    rows = sum(part.shape[0] for part in sources[:4])
    return [
        pltpu.VMEM((rows, head_dim), jnp.bfloat16),
        pltpu.VMEM((rows, head_dim), jnp.bfloat16),
        pltpu.SemaphoreType.DMA((2 * rows // BLOCK,)),
    ], rows


def attention_forward(group, query, sources, heads, head_dim):
    columns = heads * BLOCK
    scratch, rows = gathered_scratch(sources, head_dim)
    return pl.pallas_call(
        functools.partial(forward_kernel, heads, head_dim),
        out_shape=(
            jax.ShapeDtypeStruct(query.shape, jnp.bfloat16),
            jax.ShapeDtypeStruct((head_dim, columns), jnp.float32),
            jax.ShapeDtypeStruct((1, columns), jnp.float32),
        ),
        in_specs=[pl.BlockSpec(memory_space=pltpu.SMEM)]
        + in_vmem(1)
        + [pl.BlockSpec(memory_space=pl.ANY)] * 8,
        out_specs=tuple(in_vmem(3)),
        scratch_shapes=[
            pltpu.VMEM((head_dim, columns), jnp.bfloat16),
            pltpu.VMEM((1, columns), jnp.float32),
            pltpu.VMEM((1, columns), jnp.float32),
        ]
        + scratch,
        compiler_params=pltpu.CompilerParams(vmem_limit_bytes=50 << 20),
        cost_estimate=pl.CostEstimate(flops=2 * columns * rows * head_dim * 2, bytes_accessed=4 * rows * head_dim, transcendentals=0),
        name="attention_forward",
    )(group, query, *sources)


def attention_backward(group, query, grad, sources, kept, logs, heads, head_dim):
    columns = heads * BLOCK
    scratch, rows = gathered_scratch(sources, head_dim)
    return pl.pallas_call(
        functools.partial(backward_kernel, heads, head_dim),
        out_shape=(
            jax.ShapeDtypeStruct(query.shape, jnp.bfloat16),
            jax.ShapeDtypeStruct((rows, head_dim), jnp.bfloat16),
            jax.ShapeDtypeStruct((rows, head_dim), jnp.bfloat16),
        ),
        in_specs=[pl.BlockSpec(memory_space=pltpu.SMEM)]
        + in_vmem(4)
        + [pl.BlockSpec(memory_space=pl.ANY)] * 8,
        out_specs=tuple(in_vmem(3)),
        scratch_shapes=[
            pltpu.VMEM((head_dim, columns), jnp.bfloat16),
            pltpu.VMEM((head_dim, columns), jnp.bfloat16),
            pltpu.VMEM((head_dim, columns), jnp.float32),
            pltpu.VMEM((1, columns), jnp.float32),
            pltpu.VMEM((heads * SHORT_PART, head_dim), jnp.bfloat16),
            pltpu.VMEM((heads * SHORT_PART, head_dim), jnp.bfloat16),
        ]
        + scratch,
        compiler_params=pltpu.CompilerParams(vmem_limit_bytes=56 << 20),
        cost_estimate=pl.CostEstimate(flops=2 * columns * rows * head_dim * 2, bytes_accessed=4 * rows * head_dim, transcendentals=0),
        name="attention_backward",
    )(group, query, grad, kept, logs, *sources)


def normalize(rows, gain):
    return rows * lax.rsqrt(jnp.mean(rows * rows, axis=-1, keepdims=True) + EPS) * gain


def gated(gate_in, up_in):
    return jax.nn.silu(gate_in) * up_in


def after(value, *others):
    return lax.optimization_barrier((value,) + others)[0]


class Order:
    def __init__(self):
        self.last = ()

    def take(self, *values):
        out = lax.optimization_barrier(values + self.last)[: len(values)]
        return out if len(values) > 1 else out[0]

    def mark(self, *values):
        self.last = tuple(jax.tree.leaves(values))


def add_low(left, right):
    return (left.astype(jnp.float32) + right.astype(jnp.float32)).astype(jnp.bfloat16)


def plus_kernel(held, got, *outs):
    value = held[...].astype(jnp.float32) + got[...].astype(jnp.float32)
    if len(outs) == 1:
        outs[0][...] = value.astype(jnp.bfloat16)
        return
    half = pl.num_programs(0) // 2

    @pl.when(pl.program_id(0) < half)
    def _():
        outs[0][...] = value.astype(jnp.bfloat16)

    @pl.when(pl.program_id(0) >= half)
    def _():
        outs[1][...] = value.astype(jnp.bfloat16)


def plus(held, got, halves):
    rows, width = held.shape
    steps = 4 if rows % 64 == 0 else 2
    block = (rows // steps, width)
    if halves:
        half = steps // 2
        source = lambda i: (lax.rem(i + half, steps), 0)
        out_specs = [
            pl.BlockSpec(block, lambda i: (jnp.minimum(i, half - 1), 0)),
            pl.BlockSpec(block, lambda i: (jnp.maximum(i - half, 0), 0)),
        ]
        out_shape = [jax.ShapeDtypeStruct((rows // 2, width), jnp.bfloat16)] * 2
    else:
        source = lambda i: (i, 0)
        out_specs = [pl.BlockSpec(block, source)]
        out_shape = [jax.ShapeDtypeStruct((rows, width), jnp.bfloat16)]
    out = pl.pallas_call(
        plus_kernel,
        grid=(steps,),
        in_specs=[pl.BlockSpec(block, source)] * 2,
        out_specs=out_specs,
        out_shape=out_shape,
        compiler_params=pltpu.CompilerParams(vmem_limit_bytes=24 << 20),
        cost_estimate=FREE,
        name="plus",
    )(held, got)
    return out if halves else out[0]


def join_kernel(axis, *refs):
    *parts, out, inside, in_sems, out_sems = refs
    arriving, leaving, first = [], [], 0
    for i, part in enumerate(parts):
        extent = part.shape[axis]
        cut = (pl.ds(first, extent), slice(None)) if axis == 0 else (slice(None), pl.ds(first, extent))
        arriving.append(pltpu.make_async_copy(part, inside.at[cut], in_sems.at[i]))
        leaving.append(pltpu.make_async_copy(inside.at[cut], out.at[cut], out_sems.at[i]))
        first += extent
    for copy in arriving:
        copy.start()
    for arrived, left in zip(arriving, leaving):
        arrived.wait()
        left.start()
    for copy in leaving:
        copy.wait()


def join(parts, axis):
    shape = list(parts[0].shape)
    shape[axis] = sum(part.shape[axis] for part in parts)
    anywhere = pl.BlockSpec(memory_space=pl.ANY)
    return pl.pallas_call(
        functools.partial(join_kernel, axis),
        in_specs=[anywhere] * len(parts),
        out_specs=anywhere,
        out_shape=jax.ShapeDtypeStruct(tuple(shape), parts[0].dtype),
        scratch_shapes=[
            pltpu.VMEM(tuple(shape), parts[0].dtype),
            pltpu.SemaphoreType.DMA((len(parts),)),
            pltpu.SemaphoreType.DMA((len(parts),)),
        ],
        compiler_params=pltpu.CompilerParams(vmem_limit_bytes=24 << 20),
        cost_estimate=FREE,
        name="join",
    )(*parts)


def rows_kernel(contract, count, places, *refs):
    parts, (weight, out) = refs[:count], refs[count:]
    for i, part in enumerate(parts):
        rows = part.shape[contract[0] ^ 1]
        out[pl.ds(pl.multiple_of(places[i] * rows, 16), rows), :] = lax.dot_general(
            part[...],
            weight[...],
            (((contract[0],), (contract[1],)), ((), ())),
            preferred_element_type=jnp.float32,
        ).astype(jnp.bfloat16)


def rows_product(parts, weight, contract, name, places=None):
    count = len(parts)
    if places is None:
        places = jnp.arange(count, dtype=jnp.int32)
    rows, width = parts[0].shape[contract[0] ^ 1], weight.shape[contract[1] ^ 1]
    return pl.pallas_call(
        functools.partial(rows_kernel, contract, count),
        in_specs=[pl.BlockSpec(memory_space=pltpu.SMEM)] + in_vmem(count + 1),
        out_specs=pl.BlockSpec(memory_space=pltpu.VMEM),
        out_shape=jax.ShapeDtypeStruct((rows * count, width), jnp.bfloat16),
        compiler_params=pltpu.CompilerParams(vmem_limit_bytes=40 << 20),
        cost_estimate=FREE,
        name=name,
    )(places, *parts, weight)


def ring_of(count):
    return [0] + list(range(1, count, 2)) + list(range(2, count, 2))[::-1]


def ring_place(back):
    ring = ring_of(lax.axis_size("mp"))
    count = len(ring)
    table = [ring[(ring.index(i) - back) % count] for i in range(count)]
    return jnp.asarray(table, jnp.int32)[lax.axis_index("mp")]


def ring_pass(array):
    ring = ring_of(lax.axis_size("mp"))
    pairs = [(ring[i], ring[(i + 1) % len(ring)]) for i in range(len(ring))]
    return lax.ppermute(array, "mp", pairs)


def put_rows(whole_rows, rows, place):
    return lax.dynamic_update_slice_in_dim(whole_rows, rows, place * rows.shape[0], 0)


def take_rows(whole_rows, place):
    count = whole_rows.shape[0] // lax.axis_size("mp")
    return lax.dynamic_slice_in_dim(whole_rows, place * count, count, 0)


def ring_rows(parts):
    out = jnp.zeros((parts[0].shape[0] * len(parts),) + parts[0].shape[1:], parts[0].dtype)
    for step, rows in enumerate(parts):
        out = put_rows(out, rows, ring_place(step))
    return out


class RingGather:
    def __init__(self, rows):
        self.parts = [rows]
        self.start()

    def start(self):
        if len(self.parts) < lax.axis_size("mp"):
            self.flying = ring_pass(self.parts[-1])

    def step(self, order):
        if len(self.parts) < lax.axis_size("mp"):
            rows = order.take(self.flying)
            order.mark(rows)
            self.parts.append(rows)
            self.start()

    def steps_left(self):
        return lax.axis_size("mp") - len(self.parts)

    def rows(self):
        return ring_rows(self.parts)


class RingScatter:
    def __init__(self, part):
        self.part, self.steps = part, 1
        self.held = part(1)
        self.flying = ring_pass(self.held)

    def step(self, order):
        if self.steps_left():
            self.steps += 1
            got, own = order.take(self.flying, self.part(self.steps % lax.axis_size("mp")))
            self.held = add_low(own, got)
            order.mark(self.held)
            if self.steps_left():
                self.flying = ring_pass(self.held)

    def steps_left(self):
        return lax.axis_size("mp") - self.steps


def trade(array, bit):
    count = lax.axis_size("dp")
    return lax.ppermute(array, "dp", [(i, i ^ (1 << bit)) for i in range(count)])


def bit_here(bit):
    return (lax.axis_index("dp") >> bit) & 1


def orders():
    rest = list(range(1, bits_of(lax.axis_size("dp"))))
    return [0] + rest, [0] + rest[::-1]


class Lane:
    def __init__(self, partial, order, axis):
        self.bits, self.axis = order, axis
        self.steps = [("halve", bit) for bit in order]
        self.steps += [("double", bit) for bit in order[:0:-1]] + [("core", 0)]
        self.cut_and_start(lambda which, half: self.cut(partial, which, half), partial.shape[axis])

    def cut(self, array, which, half):
        return lax.dynamic_slice_in_dim(array, which * half, half, self.axis)

    def cut_and_start(self, part, extent):
        bit = self.steps[0][1]
        mine = bit_here(bit)
        self.sent, self.held = part(1 - mine, extent // 2), part(mine, extent // 2)
        self.flying = trade(self.sent, bit)

    def step(self, order):
        kind, _ = self.steps.pop(0)
        got, held = order.take(self.flying, self.held)
        if not self.steps:
            self.pieces = [held, got]
            order.mark(self.pieces)
            return
        following, bit = self.steps[0]
        if kind == "halve" and following == "halve":
            self.cut_and_start(
                lambda which, half: add_low(self.cut(held, which, half), self.cut(got, which, half)),
                held.shape[self.axis],
            )
        else:
            if kind == "halve":
                self.held = add_low(held, got)
            else:
                self.held = jnp.concatenate([held, got], axis=self.axis)
            self.sent = self.held
            self.flying = trade(self.sent, bit)
        order.mark(self.sent, self.held)

    def places(self):
        own = jnp.int32(0)
        for bit in self.bits[1:]:
            own = own * 2 + bit_here(bit)
        count = 1 << (len(self.bits) - 1)
        relative = jnp.arange(count, dtype=jnp.int32) ^ own
        core = bit_here(0)
        return jnp.concatenate([core * count + relative, (1 - core) * count + relative])


def kept_first(first_bit_first):
    count = lax.axis_size("dp")
    bits = bits_of(count) - 1
    order = [turned_bits(i, bits) if first_bit_first else i for i in range(count // 2)]
    own = lax.axis_index("dp").astype(jnp.int32)
    relative = jnp.asarray([2 * i for i in order] + [2 * i + 1 for i in order], jnp.int32)
    return relative ^ own


def product_kernel(groups, split, places, *refs):
    inputs, at = [], 0
    for parts, beside in groups:
        inputs.append((refs[at : at + parts], refs[at + parts : at + parts * (1 + beside)]))
        at += parts * (1 + beside)
    scratch = refs[len(refs) - 2 * len(groups) :]
    values = []
    for g, ((lefts, rights), (parts, _)) in enumerate(zip(inputs, groups)):
        left, right = scratch[2 * g : 2 * g + 2]
        count, width = rights[0].shape

        @pl.when(pl.program_id(0) == 0)
        def _(rights=rights, right=right, count=count, width=width, parts=parts):
            for i, part in enumerate(rights):
                row, column = i % parts * count, i // parts * width
                right[row : row + count, column : column + width] = part[...]

        for i, part in enumerate(lefts):
            left[i * count : (i + 1) * count, :] = part[...]
        values.append(
            lax.dot_general(
                left[...], right[...], (((0,), (0,)), ((), ())), preferred_element_type=jnp.float32
            ).astype(jnp.bfloat16)
        )
    first = 0
    for value in values:
        cut = (slice(None), slice(first, first + value.shape[1]))
        first += value.shape[1]
        if split is None:
            refs[at][cut] = value
            continue
        other, sent, held = refs[at : at + 3]
        total = (value.astype(jnp.float32) + other[cut].astype(jnp.float32)).astype(jnp.bfloat16)

        @pl.when(pl.program_id(0) < split)
        def _(total=total, cut=cut):
            sent[cut] = total

        @pl.when(pl.program_id(0) >= split)
        def _(total=total, cut=cut):
            held[cut] = total


def product_blocks(products, places, rows, name, other=None):
    blocks = places.shape[0]
    if other is None:
        split, order, inputs = None, lambda i: i, ()
    else:
        split, order, inputs = blocks // 2, lambda i: lax.rem(i + blocks // 2, blocks), (other,)
    arrays, in_specs, scratch, groups, total = [], [], [], [], 0
    for lefts, rights in products:
        tokens = lefts[0].shape[0]
        moving = pl.BlockSpec((tokens, rows), lambda i, places: (0, places[order(i)]))
        arrays += list(lefts)
        in_specs += [moving] * len(lefts)
        width = sum(right[0].shape[1] for right in rights)
        for right in rights:
            arrays += list(right)
            in_specs += [pl.BlockSpec(right[0].shape, lambda i, places: (0, 0))] * len(right)
        scratch += [
            pltpu.VMEM((tokens * len(lefts), rows), jnp.bfloat16),
            pltpu.VMEM((tokens * len(lefts), width), jnp.bfloat16),
        ]
        groups.append((len(lefts), len(rights)))
        total += width
    block = (rows, total)
    if other is None:
        out_specs = pl.BlockSpec(block, lambda i, places: (i, 0))
        out_shape = jax.ShapeDtypeStruct((blocks * rows, total), jnp.bfloat16)
    else:
        in_specs.append(pl.BlockSpec(block, lambda i, places: (order(i), 0)))
        out_specs = [
            pl.BlockSpec(block, lambda i, places: (jnp.minimum(i, split - 1), 0)),
            pl.BlockSpec(block, lambda i, places: (jnp.maximum(i - split, 0), 0)),
        ]
        out_shape = [jax.ShapeDtypeStruct((split * rows, total), jnp.bfloat16)] * 2
    return pl.pallas_call(
        functools.partial(product_kernel, tuple(groups), split),
        grid_spec=pltpu.PrefetchScalarGridSpec(
            num_scalar_prefetch=1,
            grid=(blocks,),
            in_specs=in_specs,
            out_specs=out_specs,
            scratch_shapes=scratch,
        ),
        out_shape=out_shape,
        compiler_params=pltpu.CompilerParams(vmem_limit_bytes=48 << 20),
        cost_estimate=FREE,
        name=name,
    )(places, *arrays, *inputs)


class BlockLane:
    def __init__(self, order, products, bits, name, first_row=0, rows=None):
        self.bits, self.name, self.products = list(bits), name, products
        self.rows = rows or products[0][0][0].shape[1] // lax.axis_size("dp")
        self.first_row = first_row
        self.places = kept_first(bits[1] == 1)
        self.table = self.places + first_row // self.rows
        half = self.places.shape[0] // 2
        self.sent = product_blocks(self.taken(order), self.table[half:], self.rows, name + "_sent")
        order.mark(self.sent)
        self.flying = trade(self.sent, 0)
        self.steps = ["product"] + ["halve"] * (len(bits) - 1) + ["double"] * (len(bits) - 1)
        self.steps += ["core"]

    def taken(self, order):
        leaves, shape = jax.tree.flatten(self.products)
        return jax.tree.unflatten(shape, order.take(*leaves))

    def step(self, order):
        kind = self.steps.pop(0)
        if kind == "product":
            self.bits.pop(0)
            got = order.take(self.flying)
            half = self.places.shape[0] // 2
            self.sent, self.held = product_blocks(
                self.taken(order), self.table[:half], self.rows, self.name + "_kept", got
            )
            self.done_bits = []
            self.flying = trade(self.sent, self.bits[0])
            order.mark(self.sent, self.held)
            return
        if kind == "both":
            near, far, own = order.take(*self.flying, self.held)
            self.held = self.sent = (own, near, far)
            self.flying = trade(near, self.done_bits[0])
            order.mark(self.held)
            return
        if kind == "rest":
            self.held = self.sent = join(order.take(*self.held, self.flying), 0)
            self.flying = trade(self.held, 0)
            order.mark(self.held)
            return
        got, held = order.take(self.flying, self.held)
        if kind == "core":
            self.pieces = [held, got]
            order.mark(self.pieces)
            return
        if kind == "halve":
            self.done_bits.append(self.bits.pop(0))
            if self.bits:
                self.sent, self.held = plus(held, got, True)
                self.flying = trade(self.sent, self.bits[0])
                order.mark(self.sent, self.held)
                return
            held = plus(held, got, False)
            if len(self.done_bits) == 2:
                self.steps = ["both", "rest", "core"]
                self.held = self.sent = held
                self.flying = (trade(held, self.done_bits[1]), trade(held, self.done_bits[0]))
                order.mark(held)
                return
        else:
            self.done_bits.pop()
            held = join([held, got], 0)
        self.held = self.sent = held
        self.flying = trade(held, self.done_bits[-1] if self.done_bits else 0)
        order.mark(self.held)


def block_lanes(order, products, name, between):
    first, second = orders()
    total = products[0][0][0].shape[1]
    rows = total // lax.axis_size("dp")
    if rows % 256:
        between()
        return [BlockLane(order, products, first, name)]
    low = BlockLane(order, products, first, name + "_low", 0, rows // 2)
    between()
    return [low, BlockLane(order, products, second, name + "_high", total // 2, rows // 2)]


def unfold_kernel(firsts, pieces, targets, places, *refs):
    sets = 2 * len(firsts)
    sources, outs = refs[:sets], refs[sets : sets + len(targets)]
    landed = refs[sets + len(targets)]
    raised = refs[sets + len(targets) + 1 : -2]
    in_sems, out_sems = refs[-2:]
    rows = landed.shape[1]
    slots = raised[0].shape[0]
    total = sets * pieces

    def fetch(i):
        source = sources[i // pieces]
        return pltpu.make_async_copy(
            source.at[pl.ds(i % pieces * rows, rows), :], landed.at[i], in_sems.at[i]
        )

    def store(i):
        along = pl.multiple_of(firsts[i // (2 * pieces)] + places[i] * rows, rows)
        copies = []
        for k, ((_, turned), out) in enumerate(zip(targets, outs)):
            window = out.at[:, pl.ds(along, rows)] if turned else out.at[pl.ds(along, rows), :]
            copies.append(
                pltpu.make_async_copy(
                    raised[k].at[i % slots], window, out_sems.at[i * len(targets) + k]
                )
            )
        return copies

    for i in range(total):
        fetch(i).start()
    for i in range(total):
        fetch(i).wait()
        if i >= slots:
            for copy in store(i - slots):
                copy.wait()
        first = 0
        for k, (width, turned) in enumerate(targets):
            value = landed[i, :, first : first + width].astype(jnp.float32)
            raised[k][i % slots] = value.T if turned else value
            first += width
        for copy in store(i):
            copy.start()
    for i in range(max(total - slots, 0), total):
        for copy in store(i):
            copy.wait()


def unfold(lanes, targets, name):
    sets = [piece for lane in lanes for piece in lane.pieces]
    rows, width = lanes[0].rows, sets[0].shape[1]
    pieces = sets[0].shape[0] // rows
    total, slots = len(sets) * pieces, 4
    height = total * rows
    anywhere = pl.BlockSpec(memory_space=pl.ANY)
    return pl.pallas_call(
        functools.partial(
            unfold_kernel, tuple(lane.first_row for lane in lanes), pieces, tuple(targets)
        ),
        in_specs=[pl.BlockSpec(memory_space=pltpu.SMEM)] + [anywhere] * len(sets),
        out_specs=[anywhere] * len(targets),
        out_shape=[
            jax.ShapeDtypeStruct((w, height) if turned else (height, w), jnp.float32)
            for w, turned in targets
        ],
        scratch_shapes=[pltpu.VMEM((total, rows, width), jnp.bfloat16)]
        + [
            pltpu.VMEM((slots, w, rows) if turned else (slots, rows, w), jnp.float32)
            for w, turned in targets
        ]
        + [
            pltpu.SemaphoreType.DMA((total,)),
            pltpu.SemaphoreType.DMA((total * len(targets),)),
        ],
        compiler_params=pltpu.CompilerParams(vmem_limit_bytes=48 << 20),
        cost_estimate=FREE,
        name=name,
    )(jnp.concatenate([lane.places for lane in lanes]), *sets)


def lay_kernel(lanes, sets, pieces, axis, cuts, places, *refs):
    outs = refs[lanes * sets : -4]
    landed, raised, in_sems, out_sems = refs[-4:]
    rows, columns = landed.shape[1:]
    slots = raised.shape[0]
    total = lanes * sets * pieces

    def window(ref, along, across, extent):
        if axis == 0:
            return ref.at[pl.ds(along, rows), pl.ds(across, extent)]
        return ref.at[pl.ds(across, extent), pl.ds(along, columns)]

    def fetch(i):
        first = i % pieces * (rows, columns)[axis]
        source = refs[i // pieces]
        across = source.shape[1 - axis]
        return pltpu.make_async_copy(
            window(source, first, 0, across), window(landed.at[i], 0, 0, across), in_sems.at[i]
        )

    def store(i):
        along = pl.multiple_of(places[i] * (rows, columns)[axis], (rows, columns)[axis])
        return [
            pltpu.make_async_copy(
                window(raised.at[i % slots], 0, first, extent),
                window(outs[out], along, target, extent),
                out_sems.at[2 * i + k],
            )
            for k, (out, first, extent, target) in enumerate(cuts[i // (sets * pieces)])
        ]

    for i in range(total):
        fetch(i).start()
    for i in range(total):
        fetch(i).wait()
        if i >= slots:
            for copy in store(i - slots):
                copy.wait()
        extent = refs[i // pieces].shape[1 - axis]
        filled = (slice(None), slice(extent)) if axis == 0 else (slice(extent), slice(None))
        raised[(i % slots, *filled)] = landed[(i, *filled)].astype(jnp.float32)
        for copy in store(i):
            copy.start()
    for i in range(max(total - slots, 0), total):
        for copy in store(i):
            copy.wait()


def lay_out(lanes, cuts, shapes, name):
    sets = [piece for lane in lanes for piece in lane.pieces]
    axis = lanes[0].axis
    places = jnp.concatenate([lane.places() for lane in lanes])
    pieces = places.shape[0] // len(sets)
    block = [max(piece.shape[d] for piece in sets) for d in (0, 1)]
    block[axis] //= pieces
    total = len(sets) * pieces
    anywhere = pl.BlockSpec(memory_space=pl.ANY)
    return pl.pallas_call(
        functools.partial(lay_kernel, len(lanes), len(lanes[0].pieces), pieces, axis, cuts),
        in_specs=[pl.BlockSpec(memory_space=pltpu.SMEM)] + [anywhere] * len(sets),
        out_specs=[anywhere] * len(shapes),
        out_shape=[jax.ShapeDtypeStruct(shape, jnp.float32) for shape in shapes],
        scratch_shapes=[
            pltpu.VMEM((total, *block), jnp.bfloat16),
            pltpu.VMEM((min(total, 6), *block), jnp.float32),
            pltpu.SemaphoreType.DMA((total,)),
            pltpu.SemaphoreType.DMA((2 * total,)),
        ],
        compiler_params=pltpu.CompilerParams(vmem_limit_bytes=44 << 20),
        cost_estimate=FREE,
        name=name,
    )(places, *sets)


def own_share(array):
    share = array.shape[0] // lax.axis_size("mp")
    return lax.dynamic_slice_in_dim(array, lax.axis_index("mp") * share, share)


class BlockSum:
    def __init__(self, blocks, order):
        self.bits = list(order)
        half = blocks.shape[0] // 2
        self.held, self.sent = blocks[:half], blocks[half:]
        self.flying = trade(self.sent, self.bits[0])

    def step(self, order):
        self.bits.pop(0)
        got, held = order.take(self.flying, self.held)
        if self.bits:
            self.sent, self.held = plus(held, got, True)
            self.flying = trade(self.sent, self.bits[0])
        else:
            self.held = self.sent = plus(held, got, False)
        order.mark(self.sent, self.held)


class BlockGather:
    def __init__(self, rows, order):
        self.bits, self.held = list(order), rows
        self.flying = trade(rows, self.bits[0])

    def step(self, order):
        if not self.bits:
            got = order.take(*self.flying)
            order.mark(got)
            self.parts = self.held + list(got)
            return
        self.bits.pop(0)
        got, held = order.take(self.flying, self.held)
        if self.bits:
            self.held = jnp.concatenate([held, got], axis=0)
            self.flying = trade(self.held, self.bits[0])
        else:
            self.held = [held, got]
            self.flying = [trade(part, 0) for part in self.held]
        order.mark(self.held)


class SmallSum:
    def __init__(self, array, axis):
        self.axis, self.held = axis, array
        self.bits = list(range(bits_of(lax.axis_size(axis))))
        self.start()

    def start(self):
        if self.bits:
            count = lax.axis_size(self.axis)
            pairs = [(i, i ^ (1 << self.bits[0])) for i in range(count)]
            self.flying = lax.ppermute(self.held, self.axis, pairs)

    def step(self, order):
        if self.bits:
            self.bits.pop(0)
            got, held = order.take(self.flying, self.held)
            self.held = held + got
            order.mark(self.held)
            self.start()


def column_share(rows):
    ring = ring_of(lax.axis_size("mp"))
    count = len(ring)
    width = rows.shape[1] // count
    parts = []
    for step in range(count):
        part = lax.dynamic_slice_in_dim(rows, ring_place(-step) * width, width, 1)
        pairs = [(ring[i], ring[(i + step) % count]) for i in range(count)]
        parts.append(lax.ppermute(part, "mp", pairs) if step else part)
    return parts


def shards(
    tokens,
    attn_gain,
    query_down,
    query_up,
    key_value,
    attn_out,
    mlp_gain,
    gate_weight,
    up_weight,
    down_weight,
    out_grad,
):
    head_dim = HEAD_DIM
    local_heads = query_up.shape[1] // head_dim
    ranks = lax.axis_size("mp")
    group = lax.axis_index("dp").reshape(1).astype(jnp.int32)
    ring_places = jnp.stack([ring_place(i) for i in range(lax.axis_size("mp"))])
    first, second = orders()

    def rows_of(array):
        return lambda back: take_rows(array, ring_place(back))

    def parts_of(array):
        count = array.shape[0] // ranks
        return lambda back: array[back * count : (back + 1) * count]

    def weight_grad(left, right):
        return jnp.einsum("tk,td->kd", left, right, preferred_element_type=jnp.float32).astype(
            jnp.bfloat16
        )

    def steps(*moving):
        for one in moving:
            one.step(order)

    def finish(*lanes):
        while lanes[0].steps:
            steps(*lanes)

    order = Order()
    inputs = tokens.astype(jnp.float32)
    normal_one = normalize(inputs, attn_gain).astype(jnp.bfloat16)
    pair_local = dotf(normal_one, key_value).astype(jnp.bfloat16)
    order.mark(pair_local)
    pair_ring = RingGather(pair_local)
    latent = dotf(order.take(normal_one), query_down).astype(jnp.bfloat16)
    order.mark(latent)
    latent_ring = RingGather(latent)
    while pair_ring.steps_left() > 1:
        steps(pair_ring, latent_ring)
    steps(pair_ring)
    pair_own = pair_ring.rows()
    order.mark(pair_own)
    keys = BlockGather(pair_own[:, :head_dim], first[1:])
    values = BlockGather(pair_own[:, head_dim:], second[1:])
    while latent_ring.steps_left():
        steps(latent_ring)
    grad_ring = RingGather(order.take(out_grad))
    latent_full = order.take(latent_ring.rows())
    query_full = dotf(latent_full, query_up).astype(jnp.bfloat16)
    order.mark(query_full)
    steps(keys, values, grad_ring)
    while keys.bits:
        steps(keys, values)
    steps(grad_ring, keys, values)
    share_parts = column_share(order.take(normal_one))
    sources = order.take(*keys.parts, *values.parts)
    attended, kept, logs = attention_forward(group, query_full, sources, local_heads, head_dim)
    order.mark(attended)
    share_parts = order.take(*share_parts)
    order.mark(*share_parts)
    steps(grad_ring)
    attn_partial = dotf(order.take(attended), attn_out).astype(jnp.bfloat16)
    order.mark(attn_partial)
    attn_ring = RingScatter(rows_of(attn_partial))
    while grad_ring.steps_left():
        steps(grad_ring)
    grad_ringed = jnp.concatenate(order.take(*grad_ring.parts), axis=0)
    act_grad = jnp.einsum("td,fd->tf", grad_ringed, down_weight, preferred_element_type=jnp.float32)
    normal_share = ring_rows(share_parts)
    order.mark(act_grad, normal_share)
    while attn_ring.steps_left():
        steps(attn_ring)
    hidden_res = inputs + attn_ring.held.astype(jnp.float32)
    normal_two = normalize(hidden_res, mlp_gain).astype(jnp.bfloat16)
    order.mark(normal_two)
    two_ring = RingGather(normal_two)
    act_parts = parts_of(act_grad)
    activated, gate_low, up_low, two_terms = [], [], [], []
    two_sum = None
    for block in range(ranks):
        steps(*([two_ring] if block else []))
        rows = order.take(two_ring.parts[block])
        gate = dotf(rows, gate_weight)
        upward = dotf(rows, up_weight)
        _, gated_pull = jax.vjp(gated, gate, upward)
        gate_grad32, up_grad32 = gated_pull(act_parts(block))
        activated.append(gated(gate, upward).astype(jnp.bfloat16))
        gate_low.append(gate_grad32.astype(jnp.bfloat16))
        up_low.append(up_grad32.astype(jnp.bfloat16))
        two_terms.append(
            (
                jnp.einsum("tf,df->td", gate_low[-1], gate_weight, preferred_element_type=jnp.float32)
                + jnp.einsum("tf,df->td", up_low[-1], up_weight, preferred_element_type=jnp.float32)
            ).astype(jnp.bfloat16)
        )
        order.mark(two_terms[-1], activated[-1])
        if block == 1:
            two_sum = RingScatter(lambda back: two_terms[back])
        elif block > 1:
            steps(two_sum)
    while two_sum.steps_left():
        steps(two_sum)
    normal_two_grad = two_sum.held.astype(jnp.float32)
    _, norm_pull_two = jax.vjp(normalize, hidden_res, mlp_gain)
    resid_from_norm, mlp_gain_part = norm_pull_two(normal_two_grad)
    hidden_grad = out_grad.astype(jnp.float32) + resid_from_norm
    branch = hidden_grad.astype(jnp.bfloat16)
    order.mark(branch)
    branch_ring = RingGather(branch)
    def part_sent(*lanes):
        order.mark([lane.sent for lane in lanes])

    low_parts = []

    def low_part():
        rows = order.take(branch_ring.parts[len(low_parts)])
        low_parts.append(rows_product([rows], attn_out, (1, 1), "attended_low"))
        order.mark(low_parts[-1])

    mlp = block_lanes(
        order,
        [(grad_ring.parts, [activated]), (two_ring.parts, [gate_low, up_low])],
        "mlp_grads",
        lambda: steps(branch_ring),
    )
    low_part()
    low_part()
    steps(mlp[0])
    steps(branch_ring)
    low_part()
    steps(*mlp[1:])
    while branch_ring.steps_left():
        steps(branch_ring)
        low_part()
    while len(low_parts) < ranks:
        low_part()
    attended_low = ring_rows(low_parts)
    order.mark(attended_low)
    query_low, key_grads, value_grads = attention_backward(
        group, query_full, order.take(attended_low), sources, kept, logs, local_heads, head_dim
    )
    query_low, key_grads, value_grads = lax.optimization_barrier(
        (query_low, key_grads, value_grads, mlp[0].flying)
    )[:3]
    order.mark(query_low)
    key_sum = BlockSum(order.take(key_grads), first)
    value_sum = BlockSum(order.take(value_grads), second)
    part_sent(key_sum, value_sum)
    steps(*mlp)
    latent_partial = rows_product([order.take(query_low)], query_up, (1, 1), "latent_low")
    order.mark(latent_partial)
    latent_low = lax.psum_scatter(latent_partial, "mp", scatter_dimension=0, tiled=True)
    steps(key_sum, value_sum)
    up_query_part = rows_product([latent_full], order.take(query_low), (0, 0), "query_up_grad")
    out_part = weight_grad(attended, ring_rows(order.take(*branch_ring.parts)))
    order.mark(up_query_part, out_part)
    out_sum, up_query_sum = lax.psum((out_part, up_query_part), "dp")
    steps(key_sum, value_sum)
    steps(*mlp)
    while key_sum.bits:
        steps(key_sum, value_sum)
    pair_partial = join(order.take(key_sum.held, value_sum.held), 1)
    order.mark(pair_partial)
    pair_low_sum = RingScatter(rows_of(pair_partial))
    steps(pair_low_sum)
    latent_low = order.take(latent_low)
    order.mark(latent_low)
    low_full = lax.all_gather(latent_low, "mp", axis=0, tiled=True)
    while pair_low_sum.steps_left():
        steps(pair_low_sum)
    pair_low = pair_low_sum.held
    low_pair_ring = RingGather(pair_low)
    result_partial = rows_product(
        order.take(*activated), down_weight, (1, 0), "result", ring_places
    )
    order.mark(result_partial)
    steps(low_pair_ring)
    steps(*mlp)
    while low_pair_ring.steps_left():
        steps(low_pair_ring)
    pair_weight_part = rows_product(
        [normal_share], order.take(low_pair_ring.rows()), (0, 0), "key_value_grad"
    )
    order.mark(pair_weight_part)
    pair_weight = Lane(order.take(pair_weight_part), first, 0)
    part_sent(pair_weight)
    down_query_part = rows_product(
        [normal_share], order.take(low_full), (0, 0), "query_down_grad"
    )
    order.mark(down_query_part)
    down_query = Lane(order.take(down_query_part), second, 0)
    part_sent(down_query)
    result_sum = lax.psum_scatter(
        after(result_partial, low_full), "mp", scatter_dimension=0, tiled=True
    )
    steps(pair_weight, down_query)
    latent_term = jnp.einsum(
        "tr,dr->td", order.take(latent_low), query_down, preferred_element_type=jnp.float32
    )
    order.mark(latent_term)
    normal_one_grad = latent_term + jnp.einsum(
        "tp,dp->td", order.take(pair_low), key_value, preferred_element_type=jnp.float32
    )
    _, norm_pull_one = jax.vjp(normalize, inputs, attn_gain)
    input_from_norm, attn_gain_part = norm_pull_one(normal_one_grad)
    input_grad = hidden_grad + input_from_norm
    order.mark(input_grad, attn_gain_part)
    attn_gain_sum = SmallSum(order.take(attn_gain_part), "mp")
    mlp_gain_sum = SmallSum(order.take(mlp_gain_part), "mp")
    steps(pair_weight, down_query)
    while attn_gain_sum.bits or mlp_gain_sum.bits:
        steps(attn_gain_sum, mlp_gain_sum)
    gains = jnp.stack([own_share(attn_gain_sum.held), own_share(mlp_gain_sum.held)])
    order.mark(gains)
    steps(pair_weight, down_query)
    gains = SmallSum(order.take(gains), "dp")
    while len(down_query.steps) > 2:
        steps(pair_weight, down_query)
        steps(gains)
    out_sum, up_query_sum = order.take(out_sum, up_query_sum)
    order.mark(out_sum, up_query_sum)
    while len(mlp[0].steps) > 1:
        steps(*mlp)
    out_sum = order.take(out_sum).astype(jnp.float32)
    up_query_sum = up_query_sum.astype(jnp.float32)
    order.mark(out_sum, up_query_sum)
    while len(down_query.steps) > 1:
        steps(pair_weight, down_query)
    finish(*mlp)
    down_sum, gate_sum, up_sum = unfold(
        mlp, [(down_weight.shape[0], True)] + [(gate_weight.shape[1], False)] * 2, "mlp_grads_laid"
    )
    order.mark(down_sum)
    finish(pair_weight, down_query)
    while gains.bits:
        steps(gains)
    cuts = tuple(((i, 0, part.shape[1], 0),) for i, part in enumerate((query_down, key_value)))
    down_query_sum, pair_weight_sum = lay_out(
        [down_query, pair_weight],
        cuts,
        [(normal_share.shape[1], part.shape[1]) for part in (query_down, key_value)],
        "query_down_key_value_laid",
    )
    order.mark(down_query_sum)
    result = (hidden_res + order.take(result_sum).astype(jnp.float32)).astype(jnp.bfloat16)
    attn_gain_sum, mlp_gain_sum = gains.held[0], gains.held[1]
    return (
        result,
        input_grad,
        attn_gain_sum,
        down_query_sum,
        up_query_sum,
        pair_weight_sum,
        out_sum,
        mlp_gain_sum,
        gate_sum,
        up_sum,
        down_sum,
    )


def solution(mesh):
    return jax.shard_map(
        shards,
        mesh=mesh,
        in_specs=(
            P(("dp", "mp"), None),
            P(),
            P(),
            P(None, "mp"),
            P(),
            P("mp", None),
            P(),
            P(None, "mp"),
            P(None, "mp"),
            P("mp", None),
            P(("dp", "mp"), None),
        ),
        out_specs=(
            P(("dp", "mp"), None),
            P(("dp", "mp"), None),
            P("mp"),
            P("mp", None),
            P(None, "mp"),
            P("mp", None),
            P("mp", None),
            P("mp"),
            P(None, "mp"),
            P(None, "mp"),
            P("mp", None),
        ),
        check_vma=False,
    )
```
